32 devices in a mesh: pts: 16 (over z, y, x), sub: 2 (over core).
Axes of the slice: x: 2, y: 2, z: 4, core: 2. Of those that a mesh axis runs over, the one named last changes fastest.
Arguments:
- points: bfloat16 [65536, 6], P(('pts', 'sub')), may hold values from -18 to 18
- route: int32 [65536], P(('pts', 'sub')), may hold values from 0 to 4095, as said below
- labels: int32 [65536], P(('pts', 'sub')), may hold values from 0 to 12, as said below
- interp_src: int32 [65536, 3], P(('pts', 'sub')), may hold values from 0 to 1023
- pool_nbr: int32 [16384, 16], P('pts'), may hold values from 0 to 8191, as said below
- sample: int32 [16384], P('pts'), may hold values from 0 to 8191, as said below
- coarse_nbr: int32 [16384, 16], P('pts'), may hold values from 0 to 1023
- owner: int32 [5], replicated, may hold values from 0 to 15, as said below
- step: int32 [1], replicated, may hold values from 2 to 20
- flat: float32 [6909], replicated
- flat_mom: float32 [6909], replicated, may hold values from -9.1552734e-05 to 9.1552734e-05
- flat_sec: float32 [6909], replicated, may hold values from 1.0953302e-10 to 7.667312e-10
- flat_ema: float32 [6909], replicated
- mats: float32 [16, 64, 64], P('pts'), may hold values from -0.75 to 0.75
- mats_mom: float32 [16, 64, 64], P('pts'), may hold values from -9.1552734e-05 to 9.1552734e-05
- mats_sec: float32 [16, 64, 64], P('pts'), may hold values from 1.0953302e-10 to 7.667312e-10
- mats_left: float32 [16, 64, 64], P('pts')
- mats_right: float32 [16, 64, 64], P('pts')
- mats_basis_l: float32 [16, 64, 64], P('pts')
- mats_basis_r: float32 [16, 64, 64], P('pts')
- mats_ema: float32 [16, 64, 64], P('pts'), may hold values from -0.75 to 0.75
Outputs:
- loss: float32 [], replicated
- grad_norm: float32 [], replicated
- flat_new: float32 [6909], replicated
- flat_mom_new: float32 [6909], replicated
- flat_sec_new: float32 [6909], replicated
- flat_ema_new: float32 [6909], replicated
- mats_new: float32 [16, 64, 64], P('pts')
- mats_mom_new: float32 [16, 64, 64], P('pts')
- mats_sec_new: float32 [16, 64, 64], P('pts')
- mats_left_new: float32 [16, 64, 64], P('pts')
- mats_right_new: float32 [16, 64, 64], P('pts')
- mats_basis_l_new: float32 [16, 64, 64], P('pts')
- mats_basis_r_new: float32 [16, 64, 64], P('pts')
- mats_ema_new: float32 [16, 64, 64], P('pts')
The draws below stay inside these ranges and needn't reach their ends.
Inputs may be any that keep to these rules, and one draw needn't show every extreme that they name: `route`: within one device's rows the values are distinct; value // 256 is the coarse owner along pts and value % 256 the slot. In every draw some device sends 256 rows to one owner, and one owner receives 256 rows from every device. `labels`: every class occurs. `pool_nbr`: each names a received row of the coarse point's owner that some fine point fills. `sample`: each names a received row of the coarse point's owner that some fine point fills. `owner`: distinct slots.
All inputs are finite; a program needn't handle non-finite values.
Results may differ from the reference program's by a relative error of at most 0.0004.
The reference program's roundings to bfloat16 on the way count: a program that leaves them out, or rounds other values in their place, can miss the bound.
Values may be sent and summed in bfloat16 or wider, within the bound.
A program may use at most 128 MiB of HBM per device.

```python
import math
import jax
import jax.numpy as jnp
import numpy as np
from jax import lax

C0 = 32
C1 = 64
NEIGH = 16
NCLS = 13
GROUPS = 8
NMATS = 5
FINE_DEV = 2048
CAP = 256
COARSE_DEV = 1024
FINE = 65536
COARSE = 16384
OWNERS = 16
RECV = 8192
FLAT = 6909
NPARAM = 27389
N_PTS = 16
N_SUB = 2
DEVICES = 32


def layout_drawn():
    return [('w_stem', (6, C0)), ('b_stem', (C0,)), ('w_down', (3 + C0, C1)), ('b_down', (C1,)), ('w_pos', (3, C1)), ('b_pos', (C1,)), ('w_att1', (C1, GROUPS)), ('b_att1', (GROUPS,)), ('w_att2', (GROUPS, GROUPS)), ('b_att2', (GROUPS,)), ('w_up', (C1, C0)), ('b_up', (C0,)), ('w_skip', (C0, C0)), ('w_head', (C0, NCLS)), ('b_head', (NCLS,))]


def flat_scales():
    pieces = []
    for entry_name, entry_shape in layout_drawn():
        if len(entry_shape) == 2:
            pieces.append(np.full(entry_shape[0] * entry_shape[1], entry_shape[0] ** (-0.5), np.float32))
        else:
            pieces.append(np.full(entry_shape[0], 0.3, np.float32))
    return np.concatenate(pieces)


def draw_flat(key, part):
    return jax.random.normal(jax.random.fold_in(key, 31), (FLAT,), jnp.float32) * jnp.asarray(flat_scales())


def draw_flat_ema(key, part):
    return jax.random.normal(jax.random.fold_in(key, 37), (FLAT,), jnp.float32) * jnp.asarray(flat_scales())


def draw_points(key, part):
    key_val = jax.random.fold_in(key, 61)
    device_of = (jnp.arange(FINE, dtype=jnp.int32) // FINE_DEV).astype(jnp.float32)
    ramp = device_of / (DEVICES - 1)
    values = jnp.clip(jax.random.normal(key_val, (FINE, 6), jnp.float32), -6.0, 6.0)
    rise = 1.0 + 2.0 * ramp
    return (values * rise[:, None]).astype(jnp.bfloat16)


def statistics(key):
    key_diag, key_off = jax.random.split(key)
    base = 0.000337 / NPARAM
    diagonal = jnp.exp(jax.random.uniform(key_diag, (OWNERS, 1, 1), jnp.float32, 0.0, math.log(4.0)))
    raw_magnitudes = jax.random.uniform(key_off, (OWNERS, C1, C1), jnp.float32, -0.8, 0.8) / C1
    symmetric = 0.5 * (raw_magnitudes + jnp.swapaxes(raw_magnitudes, 1, 2))
    identity = (jnp.arange(C1)[:, None] == jnp.arange(C1)[None, :]).astype(jnp.float32)
    return base * diagonal * (identity + symmetric)


def draw_mats_left(key, part):
    return statistics(jax.random.fold_in(key, 41))


def draw_mats_right(key, part):
    return statistics(jax.random.fold_in(key, 43))


def rotation_basis(key):
    key_one, key_perm, key_two = jax.random.split(key, 3)
    row_ids = jnp.arange(C1)[:, None]
    col_ids = jnp.arange(C1)[None, :]
    angle_one = jax.random.uniform(key_one, (OWNERS, C1 // 2), jnp.float32, -math.pi, math.pi)
    cosine = jnp.repeat(jnp.cos(angle_one), 2, axis=1)[:, :, None]
    sine = jnp.repeat(jnp.sin(angle_one), 2, axis=1)[:, :, None]
    signed = jnp.where(row_ids % 2 == 0, -1.0, 1.0)
    block = jnp.where(row_ids == col_ids, cosine, jnp.where(row_ids // 2 == col_ids // 2, signed * sine, 0.0))
    orders = jax.vmap(lambda sub_key: jax.random.permutation(sub_key, C1))(jax.random.split(key_perm, OWNERS))
    permuted = jnp.take_along_axis(block, orders[:, :, None], axis=1)
    angle_two = jax.random.uniform(key_two, (OWNERS, C1 // 2, 1), jnp.float32, -math.pi, math.pi)
    pairs = permuted.reshape(OWNERS, C1 // 2, 2, C1)
    upper = pairs[:, :, 0]
    lower = pairs[:, :, 1]
    turned = jnp.stack([jnp.cos(angle_two) * upper - jnp.sin(angle_two) * lower, jnp.sin(angle_two) * upper + jnp.cos(angle_two) * lower], axis=2)
    return turned.reshape(OWNERS, C1, C1)


def draw_mats_basis_l(key, part):
    return rotation_basis(jax.random.fold_in(key, 47))


def draw_mats_basis_r(key, part):
    return rotation_basis(jax.random.fold_in(key, 49))


def route_table(key):
    base_key = jax.random.fold_in(key, 17)
    frequent_random_seed, key_fixed, key_second, key_raw, key_order = jax.random.split(base_key, 5)
    overall_summation = N_PTS * CAP
    bucket_position_array = jnp.arange(overall_summation, dtype=jnp.int32)
    holder_position_array = bucket_position_array // CAP
    frequent_reward = jax.random.randint(frequent_random_seed, (N_PTS,), 0, 3) * 300
    fixed = jax.random.randint(key_fixed, (), 0, N_PTS)
    second = jax.random.randint(key_second, (DEVICES, 1), 0, N_PTS)
    imposed_selection = jnp.logical_or(holder_position_array[None, :] == fixed, holder_position_array[None, :] == second).astype(jnp.int32)
    raw_magnitudes = jax.random.randint(key_raw, (DEVICES, overall_summation), 0, 1024)
    dispatch_rating = (raw_magnitudes + frequent_reward[holder_position_array][None, :] + 4096 * imposed_selection) * overall_summation + bucket_position_array[None, :]
    chosen = lax.top_k(dispatch_rating, FINE_DEV)[1]
    shuffle = jax.vmap(lambda sub_key: jax.random.permutation(sub_key, FINE_DEV))(jax.random.split(key_order, DEVICES))
    return (jnp.take_along_axis(chosen, shuffle, axis=1).astype(jnp.int32), fixed)


def draw_route(key, part):
    return route_table(key)[0].reshape(FINE)


def receive_lists(key):
    route, fixed = route_table(key)
    filled = jnp.zeros((DEVICES, N_PTS * CAP), jnp.int32)
    filled = filled.at[jnp.arange(DEVICES, dtype=jnp.int32)[:, None], route].set(1)
    filled = filled.reshape(N_PTS, N_SUB, N_PTS, CAP).transpose(2, 1, 0, 3).reshape(N_PTS, RECV)
    totals = jnp.maximum(jnp.sum(filled, axis=1), 1)
    order = jnp.argsort(1 - filled, axis=1, stable=True).astype(jnp.int32)
    return (order, totals, fixed)


def pick_filled(key, tail, salt):
    order, totals, fixed = receive_lists(key)
    picks = jax.random.randint(jax.random.fold_in(key, salt), (N_PTS,) + tail, 0, totals.reshape((N_PTS,) + (1,) * len(tail)))
    chosen = jnp.take_along_axis(order, picks.reshape(N_PTS, -1), axis=1).reshape((N_PTS,) + tail)
    return (chosen, fixed)


def draw_pool_nbr(key, part):
    chosen, fixed = pick_filled(key, (COARSE_DEV, NEIGH), 5)
    chosen = chosen.at[fixed, 0, 0].set(0).at[fixed, 1, 0].set(RECV - 1)
    return chosen.reshape(COARSE, NEIGH).astype(jnp.int32)


def draw_sample(key, part):
    chosen, fixed = pick_filled(key, (COARSE_DEV,), 6)
    chosen = chosen.at[fixed, 0].set(0).at[fixed, 1].set(RECV - 1)
    return chosen.reshape(COARSE).astype(jnp.int32)


def draw_labels(key, part):
    key_any, key_inner, key_pick = jax.random.split(jax.random.fold_in(key, 23), 3)
    anywhere = jax.random.randint(key_any, (FINE,), 0, NCLS)
    inner = jax.random.randint(key_inner, (FINE,), 0, 420)
    pick = jax.random.randint(key_pick, (FINE,), 0, 4)
    device_of = jnp.arange(FINE, dtype=jnp.int32) // FINE_DEV
    upper = device_of % N_SUB >= 1
    split = (NCLS + 1) // 2
    lower_end = jnp.where(upper, split, 0)
    width_of = jnp.where(upper, NCLS - split, split)
    shift_pts = device_of // N_SUB * 7 // N_PTS
    in_half = lower_end + (inner + shift_pts) % width_of
    chosen = jnp.where(pick < 3, in_half, anywhere)
    return chosen.at[jnp.arange(NCLS)].set(jnp.arange(NCLS, dtype=jnp.int32)).astype(jnp.int32)


def draw_owner(key, part):
    key_mid, key_order = jax.random.split(jax.random.fold_in(key, 53))
    middle = jax.random.permutation(key_mid, N_PTS - 2)[:NMATS - 2] + 1
    ends = jnp.array([0, N_PTS - 1], jnp.int32)
    slots = jnp.concatenate([ends, middle.astype(jnp.int32)])
    return jax.random.permutation(key_order, slots).astype(jnp.int32)


def place_ends(values, own_key, least, largest):
    spot = [jax.random.randint(jax.random.fold_in(own_key, axis), (), 0, length) for axis, length in enumerate(values.shape)]
    longest = values.shape.index(max(values.shape))
    next_to = spot[:longest] + [(spot[longest] + 1) % values.shape[longest]] + spot[longest + 1:]
    return values.at[tuple(spot)].set(least).at[tuple(next_to)].set(largest)


def block_levels(stream_key, dims, cuts, low, largest):
    factor_of = 1.0
    for position, blocks in cuts:
        steps = jax.random.uniform(jax.random.fold_in(jax.random.fold_in(stream_key, 6), position), (blocks,), jnp.float32, low / len(cuts), largest / len(cuts))
        factor_of = factor_of * jnp.repeat(jnp.exp(steps), dims[position] // blocks).reshape((-1,) + (1,) * (len(dims) - 1 - position))
    return factor_of


def normal_values(stream_key, shape, spread, reach, cuts=(), held_as=jnp.bfloat16):
    values = jax.random.normal(stream_key, shape, jnp.float32) * spread
    if len(cuts) > 0:
        values = block_levels(stream_key, shape, cuts, -0.22, 0.18) * values
    return jnp.clip(values, min=-reach, max=reach).astype(held_as)


def setup_inputs(seed: int = 0) -> dict:
    key_of = jax.random.split(jax.random.key(seed), 22)
    points = draw_points(jax.random.fold_in(key_of[21], 71), 0)
    route = draw_route(jax.random.fold_in(key_of[21], 71), 0)
    labels = draw_labels(jax.random.fold_in(key_of[21], 71), 0)
    interp_src = place_ends(jax.random.randint(key_of[3], (FINE, 3), 0, COARSE_DEV), jax.random.fold_in(key_of[3], 1), 0, COARSE_DEV - 1).astype(jnp.int32)
    pool_nbr = draw_pool_nbr(jax.random.fold_in(key_of[21], 71), 0)
    sample = draw_sample(jax.random.fold_in(key_of[21], 71), 0)
    coarse_nbr = place_ends(jax.random.randint(key_of[6], (COARSE, NEIGH), 0, COARSE_DEV), jax.random.fold_in(key_of[6], 1), 0, COARSE_DEV - 1).astype(jnp.int32)
    owner = draw_owner(jax.random.fold_in(key_of[21], 71), 0)
    step = jax.random.randint(key_of[8], (1,), 2, 21).astype(jnp.int32)
    flat = draw_flat(jax.random.fold_in(key_of[21], 71), 0)
    flat_mom = normal_values(key_of[10], (FLAT,), (0.0011 / NPARAM ** 0.5), 9.1552734375e-05, (), jnp.float32)
    flat_sec = jnp.clip(jnp.exp(jax.random.uniform(key_of[11], (FLAT,), jnp.float32, math.log(1.0953302154170785e-10), math.log(7.667311785475306e-10))), 1.0953302154170785e-10, 7.667311785475306e-10)
    flat_ema = draw_flat_ema(jax.random.fold_in(key_of[21], 71), 0)
    mats = normal_values(key_of[13], (OWNERS, C1, C1), C1 ** -0.5, 0.75, ((0, 16),), jnp.float32)
    mats_mom = normal_values(key_of[14], (OWNERS, C1, C1), (0.0011 / NPARAM ** 0.5), 9.1552734375e-05, ((0, 16),), jnp.float32)
    mats_sec = jnp.clip(jnp.exp(math.log(7.667311785475306e-10) - 1.9459102 * jax.random.uniform(key_of[15], (OWNERS, C1, C1), jnp.float32) ** block_levels(key_of[15], (OWNERS, C1, C1), ((0, 16),), -0.2, 0.2)), 1.0953302154170785e-10, 7.667311785475306e-10)
    mats_left = draw_mats_left(jax.random.fold_in(key_of[21], 71), 0)
    mats_right = draw_mats_right(jax.random.fold_in(key_of[21], 71), 0)
    mats_basis_l = draw_mats_basis_l(jax.random.fold_in(key_of[21], 71), 0)
    mats_basis_r = draw_mats_basis_r(jax.random.fold_in(key_of[21], 71), 0)
    mats_ema = normal_values(key_of[20], (OWNERS, C1, C1), C1 ** -0.5, 0.75, ((0, 16),), jnp.float32)
    return dict(points=points, route=route, labels=labels, interp_src=interp_src, pool_nbr=pool_nbr, sample=sample, coarse_nbr=coarse_nbr, owner=owner, step=step, flat=flat, flat_mom=flat_mom, flat_sec=flat_sec, flat_ema=flat_ema, mats=mats, mats_mom=mats_mom, mats_sec=mats_sec, mats_left=mats_left, mats_right=mats_right, mats_basis_l=mats_basis_l, mats_basis_r=mats_basis_r, mats_ema=mats_ema)


@jax.custom_vjp
def low(v):
    return lax.optimization_barrier(v.astype(jnp.bfloat16)).astype(jnp.float32)

@jax.custom_vjp
def low_back(v):
    return v

def low_keep(v):
    return (low(v), None)

def low_pass(kept, grad):
    return (grad,)

def back_keep(v):
    return (v, None)

def back_low(kept, grad):
    return (low(grad),)
low.defvjp(low_keep, low_pass)
low_back.defvjp(back_keep, back_low)
HIGHEST = lax.Precision.HIGHEST
CLIP_NORM = 0.01
BETA_ONE = 0.9
BETA_TWO = 0.95
ADAM_EPS = 1e-08
LEARN_RATE = 0.1
WEIGHT_DECAY = 0.01
EMA_KEEP = 0.9
INTERP_EPS = 0.01

def layout():
    return [('w_stem', (6, C0)), ('b_stem', (C0,)), ('w_down', (3 + C0, C1)), ('b_down', (C1,)), ('w_pos', (3, C1)), ('b_pos', (C1,)), ('w_att1', (C1, GROUPS)), ('b_att1', (GROUPS,)), ('w_att2', (GROUPS, GROUPS)), ('b_att2', (GROUPS,)), ('w_up', (C1, C0)), ('b_up', (C0,)), ('w_skip', (C0, C0)), ('w_head', (C0, NCLS)), ('b_head', (NCLS,))]

def unpack(flat):
    parts = {}
    offset = 0
    for entry_name, entry_shape in layout():
        number = math.prod(entry_shape)
        parts[entry_name] = flat[offset:offset + number].reshape(entry_shape)
        offset = offset + number
    return parts

def product(left, right):
    return low_back(jnp.einsum('...i,ij->...j', low(left), low(right), precision=HIGHEST))

def exact_dot(left, right):
    return jnp.dot(left, right, precision=HIGHEST)

def relu(values):
    return jnp.maximum(values, 0.0)

def fine_index(route, received, owner_of):
    blocks = route.reshape(DEVICES, FINE_DEV)
    inverse = jnp.zeros((DEVICES, N_PTS * CAP), jnp.int32)
    inverse = inverse.at[jnp.arange(DEVICES, dtype=jnp.int32)[:, None], blocks].set(jnp.arange(FINE_DEV, dtype=jnp.int32)[None, :])
    sub_part = received // (N_PTS * CAP)
    remain = received % (N_PTS * CAP)
    sender = remain // CAP * N_SUB + sub_part
    slot_at = owner_of * CAP + remain % CAP
    return (sender * FINE_DEV + inverse[sender, slot_at]).astype(jnp.int32)

def forward(flat, layer_mats, points, route, labels, interp_src, pool_nbr, sample, coarse_nbr):
    params = unpack(flat)
    feats = points.astype(jnp.float32)
    xyz = feats[:, :3]
    stem = relu(product(feats, params['w_stem']) + params['b_stem'])
    projected = low(product(jnp.concatenate([xyz, stem], 1), params['w_down']))
    coarse_owner = jnp.arange(COARSE, dtype=jnp.int32) // COARSE_DEV
    pool_fine = fine_index(route, pool_nbr, coarse_owner[:, None])
    centre = xyz[fine_index(route, sample, coarse_owner)]
    centre_term = product(centre, params['w_down'][:3])
    pool_in = projected[pool_fine] - centre_term[:, None, :] + params['b_down']
    pooled = jax.nn.logsumexp(pool_in, axis=1)
    w_qkv = jnp.concatenate([layer_mats[0], layer_mats[1], layer_mats[2]], 1)
    qkv_rows = product(pooled, w_qkv)
    queries = qkv_rows[:, :C1]
    key_rows = qkv_rows[:, C1:2 * C1]
    value_rows = qkv_rows[:, 2 * C1:]
    neighbour = coarse_owner[:, None] * COARSE_DEV + coarse_nbr
    offsets = centre[:, None, :] - centre[neighbour]
    pos_hid = relu(product(offsets, params['w_pos']) + params['b_pos'])
    pos_enc = product(pos_hid, layer_mats[3])
    edge = queries[:, None, :] - key_rows[neighbour] + pos_enc
    score_one = relu(product(edge, params['w_att1']) + params['b_att1'])
    score_two = product(score_one, params['w_att2']) + params['b_att2']
    attn = jax.nn.softmax(score_two, axis=1)
    carried = (value_rows[neighbour] + pos_enc).reshape(COARSE, NEIGH, GROUPS, C1 // GROUPS)
    mixed = lax.optimization_barrier(jnp.sum(attn[..., None] * carried, axis=1)).reshape(COARSE, C1)
    block_out = pooled + product(mixed, layer_mats[4])
    coarse_up = product(block_out, params['w_up']) + params['b_up']
    source = (route // CAP)[:, None] * COARSE_DEV + interp_src
    src_xyz = centre[source]
    diffs = xyz[:, None, :] - src_xyz
    dist = lax.optimization_barrier(jnp.sum(diffs * diffs, axis=2))
    inverse_d = 1.0 / (dist + INTERP_EPS)
    interp_wts = inverse_d / lax.optimization_barrier(jnp.sum(inverse_d, axis=1, keepdims=True))
    interp_rows = low(low_back(lax.optimization_barrier(jnp.sum(interp_wts[..., None] * coarse_up[source], axis=1))))
    joined = interp_rows + product(stem, params['w_skip'])
    logits = product(relu(joined), params['w_head']) + params['b_head']
    onehot = (labels[:, None] == jnp.arange(NCLS, dtype=jnp.int32)[None, :]).astype(jnp.float32)
    counts = lax.optimization_barrier(jnp.sum(onehot, axis=0))
    class_wts = FINE / (NCLS * counts)
    cross = jax.nn.logsumexp(logits, axis=1) - lax.optimization_barrier(jnp.sum(onehot * logits, axis=1))
    return jnp.sum(lax.optimization_barrier(jnp.sum(onehot * class_wts, axis=1)) * cross) / FINE

def orthonormal(matrix):
    size = matrix.shape[0]

    def column(column_at, basis):
        vector = lax.dynamic_slice_in_dim(matrix, column_at, 1, 1)
        keep = (jnp.arange(size) < column_at).astype(matrix.dtype)[None, :]
        masked = basis * keep
        for repeat in range(2):
            vector = vector - exact_dot(masked, exact_dot(masked.T, vector))
        vector = vector * lax.rsqrt(jnp.sum(vector * vector))
        return lax.dynamic_update_slice_in_dim(basis, vector, column_at, 1)
    return lax.fori_loop(0, size, column, jnp.zeros_like(matrix))

def soap_update(weight, grad, first, second, left, right, basis_l, basis_r, average, count):
    left_new = BETA_TWO * left + (1.0 - BETA_TWO) * exact_dot(grad, grad.T)
    right_new = BETA_TWO * right + (1.0 - BETA_TWO) * exact_dot(grad.T, grad)
    rotated = exact_dot(exact_dot(basis_l.T, grad), basis_r)
    first_new = BETA_ONE * first + (1.0 - BETA_ONE) * rotated
    second_new = BETA_TWO * second + (1.0 - BETA_TWO) * rotated * rotated
    scaled = first_new / (1.0 - BETA_ONE ** count) / (jnp.sqrt(second_new / (1.0 - BETA_TWO ** count)) + ADAM_EPS)
    weight_new = weight - LEARN_RATE * (exact_dot(exact_dot(basis_l, scaled), basis_r.T) + WEIGHT_DECAY * weight)
    basis_l_new = orthonormal(exact_dot(left_new, basis_l))
    basis_r_new = orthonormal(exact_dot(right_new, basis_r))
    plain = exact_dot(exact_dot(basis_l, first_new), basis_r.T)
    first_out = exact_dot(exact_dot(basis_l_new.T, plain), basis_r_new)
    average_new = EMA_KEEP * average + (1.0 - EMA_KEEP) * weight_new
    return (weight_new, first_out, second_new, left_new, right_new, basis_l_new, basis_r_new, average_new)

def adam_update(weight, grad, first, second, average, count):
    first_new = BETA_ONE * first + (1.0 - BETA_ONE) * grad
    second_new = BETA_TWO * second + (1.0 - BETA_TWO) * grad * grad
    scaled = first_new / (1.0 - BETA_ONE ** count) / (jnp.sqrt(second_new / (1.0 - BETA_TWO ** count)) + ADAM_EPS)
    weight_new = weight - LEARN_RATE * (scaled + WEIGHT_DECAY * weight)
    return (weight_new, first_new, second_new, EMA_KEEP * average + (1.0 - EMA_KEEP) * weight_new)

def reference(points, route, labels, interp_src, pool_nbr, sample, coarse_nbr, owner, step, flat, flat_mom, flat_sec, flat_ema, mats, mats_mom, mats_sec, mats_left, mats_right, mats_basis_l, mats_basis_r, mats_ema):
    layer_mats = mats[owner]

    def loss_of(flat_in, mats_in):
        return forward(flat_in, mats_in, points, route, labels, interp_src, pool_nbr, sample, coarse_nbr)
    loss, pullback = jax.vjp(loss_of, flat, layer_mats)
    flat_grad, mats_grad = pullback(jnp.ones((), jnp.float32))
    grad_norm = jnp.sqrt(jnp.sum(flat_grad * flat_grad) + jnp.sum(mats_grad * mats_grad))
    factor = jnp.minimum(1.0, CLIP_NORM / grad_norm)
    count = step[0].astype(jnp.float32)
    flat_out = adam_update(flat, flat_grad * factor, flat_mom, flat_sec, flat_ema, count)
    states = [mats, mats_mom, mats_sec, mats_left, mats_right, mats_basis_l, mats_basis_r, mats_ema]
    results = jax.vmap(soap_update, in_axes=(0, 0, 0, 0, 0, 0, 0, 0, 0, None))(layer_mats, mats_grad * factor, mats_mom[owner], mats_sec[owner], mats_left[owner], mats_right[owner], mats_basis_l[owner], mats_basis_r[owner], mats_ema[owner], count)
    placed = [jnp.zeros_like(held).at[owner].set(result) for held, result in zip(states, results)]
    return (loss, grad_norm, flat_out[0], flat_out[1], flat_out[2], flat_out[3], placed[0], placed[1], placed[2], placed[3], placed[4], placed[5], placed[6], placed[7])
```

```python
import functools
import math

import jax
import jax.numpy as jnp
from jax import lax
from jax.experimental import pallas as pl
from jax.experimental.pallas import tpu as pltpu
from jax.sharding import PartitionSpec as P

C0 = 32
C1 = 64
NEIGH = 16
NCLS = 13
GROUPS = 8
NMATS = 5

HIGHEST = lax.Precision.HIGHEST
CLIP_NORM = 0.01
BETA_ONE = 0.9
BETA_TWO = 0.95
ADAM_EPS = 1e-08
LEARN_RATE = 0.1
WEIGHT_DECAY = 0.01
EMA_KEEP = 0.9
INTERP_EPS = 0.01

F32 = jnp.float32
BF16 = jnp.bfloat16
I32 = jnp.int32
MESH = pl.DeviceIdType.MESH
VMEM = pltpu.VMEM

LANES = 128
FLAT_ROWS = 64
LOW_B = 256
CH = 80
NEG = -1e30


def offsets():
    shapes = [
        ("w_stem", (6, C0)),
        ("b_stem", (C0,)),
        ("w_down", (3 + C0, C1)),
        ("b_down", (C1,)),
        ("w_pos", (3, C1)),
        ("b_pos", (C1,)),
        ("w_att1", (C1, GROUPS)),
        ("b_att1", (GROUPS,)),
        ("w_att2", (GROUPS, GROUPS)),
        ("b_att2", (GROUPS,)),
        ("w_up", (C1, C0)),
        ("b_up", (C0,)),
        ("w_skip", (C0, C0)),
        ("w_head", (C0, NCLS)),
        ("b_head", (NCLS,)),
    ]
    found = {}
    total = 0
    for name, shape in shapes:
        found[name] = total
        total += math.prod(shape)
    return found, total


OFF, FLAT = offsets()


def dot(left, right):
    return lax.dot_general(left, right, (((1,), (0,)), ((), ())), preferred_element_type=F32)


def dot_nt(left, right):
    return lax.dot_general(left, right, (((1,), (1,)), ((), ())), preferred_element_type=F32)


def exact(left, right, dims=((1,), (0,))):
    return lax.dot_general(
        left, right, (dims, ((), ())), precision=HIGHEST, preferred_element_type=F32
    )


def relu(values):
    return jnp.maximum(values, 0.0)


def rows_of(count, length):
    return lax.broadcasted_iota(I32, (count, length), 0)


def lanes_of(count, length):
    return lax.broadcasted_iota(I32, (count, length), 1)


def onehot(low, count):
    hit = rows_of(count, low.shape[1]) == low
    return jnp.where(hit, 1.0, 0.0).astype(BF16)


def pick(spread, high, parts):
    each = spread.shape[0] // parts
    found = spread[0:each]
    for part in range(1, parts):
        found = jnp.where(high == part, spread[part * each : (part + 1) * each], found)
    return found


def place(values, high, parts):
    return jnp.concatenate(
        [jnp.where(high == part, values, 0.0) for part in range(parts)], 0
    ).astype(BF16)


def unpack(flat_ref, out_ref, offset, rows, width, at):
    stride = LANES // width if LANES % width == 0 else rows
    for first in range(min(stride, rows)):
        count = (rows - first + stride - 1) // stride
        padded = -(-count // 8) * 8
        line, lane = divmod(offset + first * width, LANES)
        values = flat_ref[line : line + padded, :]
        if lane:
            values = pltpu.roll(values, LANES - lane, 1)
        if lane + width > LANES:
            following = pltpu.roll(flat_ref[line + 1 : line + 1 + padded, :], LANES - lane, 1)
            values = jnp.where(lanes_of(padded, LANES) < LANES - lane, values, following)
        values = jnp.where(lanes_of(padded, LANES) < width, values, 0.0)
        if count == 1:
            out_ref[at + first : at + first + 1, :] = values[0:1]
        else:
            out_ref[pl.ds(at + first, count, stride=stride), :] = values[0:count]


def pack(out_ref, base, source_ref, row, lane_from, offset, rows, width):
    stride = LANES // width if LANES % width == 0 else rows
    for first in range(min(stride, rows)):
        count = (rows - first + stride - 1) // stride
        line, lane = divmod(offset + first * width, LANES)
        if count == 1:
            values = source_ref[row + first : row + first + 1, :]
        else:
            values = source_ref[pl.ds(row + first, count, stride=stride), :]
        shift = (lane - lane_from) % LANES
        padded = -(-count // 8) * 8
        if padded != count:
            values = jnp.concatenate([values, jnp.zeros((padded - count, LANES), F32)], 0)
        if shift:
            values = pltpu.roll(values, shift, 1)
        values = values[0:count]
        at = lanes_of(count, LANES)
        here = jnp.where((at >= lane) & (at < lane + width), values, 0.0)
        out_ref[base + line : base + line + count, :] += here
        if lane + width > LANES:
            there = jnp.where(at < lane + width - LANES, values, 0.0)
            out_ref[base + line + 1 : base + line + 1 + count, :] += there


def main_kernel(
    n_pts,
    n_sub,
    pts_ref,
    route_ref,
    labels_ref,
    src_ref,
    pool_ref,
    sample_ref,
    cnbr_ref,
    owner_ref,
    flat_ref,
    mats_ref,
    out_ref,
    data,
    sacc,
    sendb,
    recv,
    matmine,
    matall,
    tabb,
    cen,
    pin,
    cat,
    pooled_ref,
    rsum_ref,
    ctab,
    btab,
    est,
    ohs,
    car,
    sc,
    mixed_ref,
    blk_ref,
    slot,
    dcp,
    dcr,
    dkp,
    dkr,
    wst,
    wd,
    wp,
    w1,
    w2,
    wu,
    wsk,
    wh,
    bias,
    ga,
    gb,
    gc,
    gd,
    ge,
    gbuf,
    gsib,
    ghalf,
    gsh,
    gfull,
    a2a_send,
    a2a_recv,
    mat_send,
    mat_recv,
    red_send,
    red_recv,
    gat_send,
    gat_recv,
    sib_send,
    sib_recv,
):
    fine = route_ref.shape[1]
    coarse = sample_ref.shape[1]
    cap = sendb.shape[2]
    slots = n_pts * cap
    half = coarse // n_sub
    sources = n_sub * n_pts
    parts = coarse // LOW_B
    my_parts = parts // n_sub
    shift = cap.bit_length() - 1
    low_shift = LOW_B.bit_length() - 1
    span = 512
    me = lax.axis_index("pts")
    sub = lax.axis_index("sub")
    half_at = pl.multiple_of(sub * half, half)

    barrier = pltpu.get_barrier_semaphore()

    def greet(step, carry):
        peer = lax.rem(me + step, n_pts)
        pl.semaphore_signal(barrier, inc=1, device_id={"pts": peer}, device_id_type=MESH)
        return carry

    lax.fori_loop(1, n_pts, greet, 0)
    pl.semaphore_signal(barrier, inc=1, device_id={"sub": 1 - sub}, device_id_type=MESH)

    def sibling(number, source, target):
        return pltpu.make_async_remote_copy(
            src_ref=source,
            dst_ref=target,
            send_sem=sib_send.at[number],
            recv_sem=sib_recv.at[number],
            device_id={"sub": 1 - sub},
            device_id_type=MESH,
        )

    data[0:6, :] = pts_ref[...].astype(F32)
    data[6:8, :] = jnp.zeros((2, fine), F32)
    source_rows = src_ref[...]
    data[8:11, :] = lax.shift_right_logical(source_rows, 5).astype(F32)
    data[11:14, :] = (source_rows & 31).astype(F32)
    data[14:15, :] = (labels_ref[...] + 1).astype(F32)
    data[15:16, :] = jnp.zeros((1, fine), F32)
    sacc[...] = jnp.zeros_like(sacc)
    counts = jnp.zeros((16, 32), F32)
    for chunk in range(fine // span):
        lanes = slice(chunk * span, (chunk + 1) * span)
        route = route_ref[:, lanes]
        high = lax.shift_right_logical(route, shift)
        spread = place(data[:, lanes], high, n_pts)
        sacc[...] += dot_nt(spread, onehot(route & (cap - 1), cap))
        classes = onehot(labels_ref[:, lanes], 16)
        counts = counts + dot_nt(jnp.ones((16, span), BF16), jnp.concatenate([classes, classes], 0))
    count_high = jnp.floor(counts * (1.0 / 128.0))
    count_low = counts - 128.0 * count_high
    digits = jnp.where(lanes_of(16, 32) < 16, count_low, count_high)
    digits = jnp.where(rows_of(16, 32) == 15, digits, 0.0)
    data[:, 0:cap] = jnp.zeros((16, cap), F32)
    data[:, 0:32] = digits
    sendb[...] = (sacc[...].reshape(n_pts, 16, cap) + data[:, 0:cap][None]).astype(BF16)
    matrix = mats_ref[...]
    matmine[...] = jnp.concatenate([matrix[0:32], matrix[32:64]], 1).astype(BF16)

    pl.semaphore_wait(barrier, n_pts)

    def block_copy(peer, index):
        return pltpu.make_async_remote_copy(
            src_ref=sendb.at[peer],
            dst_ref=recv.at[sub * n_pts + index],
            send_sem=a2a_send.at[peer],
            recv_sem=a2a_recv.at[index],
            device_id={"pts": peer},
            device_id_type=MESH,
        )

    def mat_copy(peer, index):
        return pltpu.make_async_remote_copy(
            src_ref=matmine,
            dst_ref=matall.at[index],
            send_sem=mat_send.at[peer],
            recv_sem=mat_recv.at[index],
            device_id={"pts": peer},
            device_id_type=MESH,
        )

    def send_blocks(step, carry):
        block_copy(lax.rem(me + step, n_pts), me).start()
        return carry

    def send_mats(step, carry):
        mat_copy(lax.rem(me + step, n_pts), me).start()
        return carry

    lax.fori_loop(1, n_pts, send_blocks, 0)
    lax.fori_loop(1, n_pts, send_mats, 0)
    recv[sub * n_pts + me] = sendb[me]
    matall[me] = matmine[...]

    for ref in (wst, wd, wp, w1, w2, wu, wsk, wh, bias):
        ref[...] = jnp.zeros_like(ref)
    unpack(flat_ref, wst, OFF["w_stem"], 6, C0, 0)
    unpack(flat_ref, wd, OFF["w_down"], 3, C1, 0)
    unpack(flat_ref, wd, OFF["w_down"] + 3 * C1, C0, C1, 16)
    unpack(flat_ref, wp, OFF["w_pos"], 3, C1, 8)
    unpack(flat_ref, w1, OFF["w_att1"], C1, GROUPS, 0)
    unpack(flat_ref, w2, OFF["w_att2"], GROUPS, GROUPS, 0)
    unpack(flat_ref, wu, OFF["w_up"], C1, C0, 0)
    unpack(flat_ref, wsk, OFF["w_skip"], C0, C0, 0)
    unpack(flat_ref, wh, OFF["w_head"], C0, NCLS, 0)
    names = ("b_stem", "b_down", "b_pos", "b_att1", "b_att2", "b_up", "b_head")
    widths = (C0, C1, C1, GROUPS, GROUPS, C0, NCLS)
    for position, (name, width) in enumerate(zip(names, widths)):
        unpack(flat_ref, bias, OFF[name], 1, width, position)
    columns = bias[...].T
    b_stem = columns[0:C0, 0:1]
    b_down = columns[0:C1, 1:2]
    b_pos = columns[0:C1, 2:3]
    b_att1 = columns[0:GROUPS, 3:4]
    b_att2 = columns[0:GROUPS, 4:5]
    b_up = columns[0:C0, 5:6]
    b_head = jnp.where(rows_of(16, 1) < NCLS, columns[0:16, 6:7], NEG)
    w_stem_t = wst[...].T[0:C0, 0:16].astype(BF16)
    w_down_t = wd[...].T[0:C1, 0:48].astype(BF16)
    w_pos_t = wp[...].T[0:C1, 0:16].astype(BF16)
    w_att1_t = w1[...].T[0:GROUPS, 0:C1].astype(BF16)
    w_att2_t = w2[...].T[0:GROUPS, 0:16].astype(BF16)
    w_up_t = wu[...].T[0:C0, 0:C1].astype(BF16)
    w_skip_t = wsk[...].T[0:C0, 0:C0].astype(BF16)
    w_head_t = wh[...].T[0:16, 0:C0].astype(BF16)
    w_down_stem = wd[16:48, 0:C1].astype(BF16)
    w_att1 = w1[0:C1, 0:16].astype(BF16)
    w_att2 = w2[0:GROUPS, 0:16].astype(BF16)
    w_up = wu[0:C1, 0:C0].astype(BF16)
    w_skip = wsk[0:C0, 0:C0].astype(BF16)
    w_head = wh[0:C0, 0:16].astype(BF16)

    def wait_blocks(step, carry):
        peer = lax.rem(me + step, n_pts)
        block_copy(peer, peer).wait_recv()
        return carry

    lax.fori_loop(1, n_pts, wait_blocks, 0)
    mine = recv.at[pl.ds(sub * n_pts, n_pts)]
    forward = sibling(0, mine, mine)
    forward.start()
    for source in range(n_pts):
        slot[:, source * cap : (source + 1) * cap] = recv[sub * n_pts + source].astype(F32)
    forward.wait_recv()

    table = recv[...].astype(F32)[:, 0:8, :].reshape(sources * 8, cap)
    ones_row = (rows_of(sources * 8, cap) & 7) == 7
    tabb[...] = jnp.where(ones_row, 1.0, table).astype(BF16)
    count_row = jnp.sum(recv[...].astype(F32)[:, 8:16, :], axis=0)[7:8, 0:32]
    count_at = jnp.broadcast_to(count_row, (16, 32))
    low_hit = lanes_of(16, 32) == rows_of(16, 32)
    high_hit = lanes_of(16, 32) == rows_of(16, 32) + 16
    class_counts = jnp.sum(
        jnp.where(low_hit, count_at, 0.0) + jnp.where(high_hit, 128.0 * count_at, 0.0),
        axis=1,
        keepdims=True,
    )
    total_fine = float(fine * n_pts * n_sub)
    class_w = jnp.where(rows_of(16, 1) < NCLS, total_fine / (NCLS * class_counts), 0.0)

    def gather_points(index):
        hot = onehot(index & (cap - 1), cap)
        return pick(dot(tabb[...], hot), lax.shift_right_logical(index, shift), sources)

    zeros8 = jnp.zeros((8, span), F32)
    for chunk in range(coarse // span):
        lanes = slice(chunk * span, (chunk + 1) * span)
        found = gather_points(sample_ref[:, lanes])
        cen[:, lanes] = jnp.where(rows_of(8, span) < 6, found, 0.0)
    centre = cen[:, pl.ds(half_at, half)]
    centre_low = jnp.concatenate([centre, zeros8], 0).astype(BF16)
    w_xyz_t = jnp.where(lanes_of(C1, 16) < 3, wd[...].T[0:C1, 0:16], 0.0).astype(BF16)
    centre_term = dot(w_xyz_t, centre_low)

    def pool_step(k, most):
        found = gather_points(pool_ref[pl.ds(k, 1), pl.ds(half_at, half)])
        low = jnp.concatenate([found, zeros8], 0).astype(BF16)
        stem = relu(dot(w_stem_t, low) + b_stem)
        joined = jnp.concatenate([found, zeros8, stem], 0).astype(BF16)
        cat[k] = joined
        projected = dot(w_down_t, joined).astype(BF16).astype(F32)
        value = projected - centre_term + b_down
        pin[k] = value
        return jnp.maximum(most, value)

    most = lax.fori_loop(0, NEIGH, pool_step, jnp.full((C1, half), -jnp.inf, F32))

    def exp_step(k, total):
        value = jnp.exp(pin[k] - most)
        pin[k] = value
        return total + value

    total = lax.fori_loop(0, NEIGH, exp_step, jnp.zeros((C1, half), F32))
    pooled = most + jnp.log(total)
    pooled_ref[...] = pooled
    rsum_ref[...] = 1.0 / total

    def table_rows(values, target):
        for part in range(my_parts):
            lanes = slice(part * LOW_B, (part + 1) * LOW_B)
            stacked = jnp.concatenate(
                [values[:, lanes], centre[:, lanes], jnp.zeros((8, LOW_B), F32)], 0
            )
            target[sub * my_parts + part] = stacked.astype(BF16)

    table_rows(pooled, ctab)
    my_ctab = ctab.at[pl.ds(sub * my_parts, my_parts)]
    give_pooled = sibling(1, my_ctab, my_ctab)
    give_pooled.start()

    def wait_mats(step, carry):
        peer = lax.rem(me + step, n_pts)
        mat_copy(peer, peer).wait_recv()
        return carry

    lax.fori_loop(1, n_pts, wait_mats, 0)

    def layer(position):
        folded = matall[owner_ref[position]].astype(F32)
        return jnp.concatenate([folded[:, 0:C1], folded[:, C1 : 2 * C1]], 0)

    w_qkv32 = jnp.concatenate([layer(0), layer(1), layer(2)], 1)
    w_qkv = w_qkv32.astype(BF16)
    w_query_t = w_qkv32[:, 0:C1].T.astype(BF16)
    w_kv_t = jnp.concatenate([w_qkv32[:, C1 : 2 * C1].T, w_qkv32[:, 2 * C1 :].T], 0).astype(BF16)
    w_pos2_32 = layer(3)
    w_pos2 = w_pos2_32.astype(BF16)
    w_pos2_t = w_pos2_32.T.astype(BF16)
    w_out_32 = layer(4)
    w_out = w_out_32.astype(BF16)
    w_out_t = w_out_32.T.astype(BF16)
    pooled_low = pooled.astype(BF16)
    queries = dot(w_query_t, pooled_low)
    give_pooled.wait_recv()

    def expand(values):
        return jnp.concatenate(
            [jnp.broadcast_to(values[g : g + 1], (8, values.shape[1])) for g in range(GROUPS)], 0
        )

    def attend(k, most):
        index = cnbr_ref[pl.ds(k, 1), pl.ds(half_at, half)]
        high = lax.shift_right_logical(index, low_shift)
        hot = onehot(index & (LOW_B - 1), LOW_B)
        ohs[k] = hot
        found = pick(dot(ctab[...].reshape(parts * CH, LOW_B), hot), high, parts)
        near = found[0:C1].astype(BF16)
        rows = dot(w_kv_t, near)
        offset = jnp.where(rows_of(8, half) == 7, 1.0, centre - found[C1 : C1 + 8])
        off_low = jnp.concatenate([zeros8, offset], 0).astype(BF16)
        pos_low = relu(dot(w_pos_t, off_low) + b_pos).astype(BF16)
        pos_enc = dot(w_pos2_t, pos_low)
        edge_low = (queries - rows[0:C1] + pos_enc).astype(BF16)
        act = relu(dot(w_att1_t, edge_low) + b_att1)
        act_off = jnp.concatenate([act, offset], 0).astype(BF16)
        score = dot(w_att2_t, act_off) + b_att2
        est[k, 0:64, :] = edge_low
        est[k, 64:128, :] = pos_low
        est[k, 128:144, :] = act_off
        car[k] = rows[C1 : 2 * C1] + pos_enc
        sc[k] = score
        return jnp.maximum(most, score)

    top = lax.fori_loop(0, NEIGH, attend, jnp.full((GROUPS, half), -jnp.inf, F32))

    def weigh(k, total):
        value = jnp.exp(sc[k] - top)
        sc[k] = value
        return total + value

    scale = 1.0 / lax.fori_loop(0, NEIGH, weigh, jnp.zeros((GROUPS, half), F32))

    def mix(k, total):
        weight = sc[k] * scale
        sc[k] = weight
        return total + expand(weight) * car[k]

    mixed = lax.fori_loop(0, NEIGH, mix, jnp.zeros((C1, half), F32))
    mixed_ref[...] = mixed
    block = pooled_ref[...] + dot(w_out_t, mixed.astype(BF16))
    blk_ref[...] = block
    table_rows(block, btab)
    my_btab = btab.at[pl.ds(sub * my_parts, my_parts)]
    give_block = sibling(2, my_btab, my_btab)
    give_block.start()
    give_block.wait_recv()

    ga[...] = jnp.zeros_like(ga)
    dcp[...] = jnp.zeros_like(dcp)

    def fine_step(step, loss):
        at = pl.multiple_of(step * span, span)
        rows = slot[:, pl.ds(at, span)]
        points = rows[0:8]
        source = (32.0 * rows[8:11] + rows[11:14]).astype(I32)
        label = rows[14:15].astype(I32)
        hots = []
        highs = []
        ups = []
        inverses = []
        for i in range(3):
            index = source[i : i + 1]
            high = lax.shift_right_logical(index, low_shift)
            hot = onehot(index & (LOW_B - 1), LOW_B)
            found = pick(dot(btab[...].reshape(parts * CH, LOW_B), hot), high, parts)
            ups.append(dot(w_up_t, found[0:C1].astype(BF16)) + b_up)
            diff = jnp.where(rows_of(8, span) < 3, points - found[C1 : C1 + 8], 0.0)
            inverses.append(1.0 / (jnp.sum(diff * diff, axis=0, keepdims=True) + INTERP_EPS))
            hots.append(hot)
            highs.append(high)
        norm = inverses[0] + inverses[1] + inverses[2]
        weights = [inverse / norm for inverse in inverses]
        interp = weights[0] * ups[0] + weights[1] * ups[1] + weights[2] * ups[2]
        interp = interp.astype(BF16).astype(F32)
        ones = jnp.where(rows_of(8, span) == 7, 1.0, points)
        points_low = jnp.concatenate([ones, zeros8], 0).astype(BF16)
        stem_pre = dot(w_stem_t, points_low) + b_stem
        stem_low = relu(stem_pre).astype(BF16)
        joined = interp + dot(w_skip_t, stem_low)
        joined_low = relu(joined).astype(BF16)
        logits = dot(w_head_t, joined_low) + b_head
        hit = jnp.where(rows_of(16, span) + 1 == label, 1.0, 0.0)
        row_w = jnp.sum(hit * class_w, axis=0, keepdims=True) * (1.0 / total_fine)
        peak = jnp.max(logits, axis=0, keepdims=True)
        lse = peak + jnp.log(jnp.sum(jnp.exp(logits - peak), axis=0, keepdims=True))
        loss = loss + row_w * (lse - jnp.sum(hit * logits, axis=0, keepdims=True))
        dlog_low = (row_w * (jnp.exp(logits - lse) - hit)).astype(BF16)
        dfused_low = jnp.where(joined > 0, dot(w_head, dlog_low), 0.0).astype(BF16)
        dfused = dfused_low.astype(F32)
        dstem = jnp.where(stem_pre > 0, dot(w_skip, dfused_low), 0.0).astype(BF16)
        inputs = jnp.concatenate([points_low, stem_low, joined_low], 0)
        grads = jnp.concatenate([dfused_low, dstem, dlog_low], 0)
        ga[:, 0:80] += dot_nt(inputs, grads)
        spread = jnp.concatenate(
            [place(weights[i] * dfused, highs[i], parts) for i in range(3)], 1
        )
        dcp[...] += dot_nt(spread, jnp.concatenate(hots, 1)).reshape(parts, C0, LOW_B)
        return loss

    loss = lax.fori_loop(0, slots // span, fine_step, jnp.zeros((1, span), F32))

    other = (1 - sub) * my_parts
    own = sub * my_parts
    give_dup = sibling(3, dcp.at[pl.ds(other, my_parts)], dcr)
    give_dup.start()
    give_dup.wait_recv()

    def own_half(partial, received):
        return jnp.concatenate(
            [partial[own + part] + received[part] for part in range(my_parts)], 1
        )

    dup_low = own_half(dcp, dcr).astype(BF16)
    dblock = dot(w_up, dup_low)
    dbranch_low = dblock.astype(BF16)
    dmixed = dot(w_out, dbranch_low)
    inputs = jnp.concatenate(
        [blk_ref[...].astype(BF16), mixed_ref[...].astype(BF16), jnp.ones((16, half), BF16)], 0
    )
    grads = jnp.concatenate([dup_low, jnp.zeros((C0, half), BF16), dbranch_low], 0)
    gd[...] = dot_nt(inputs, grads)

    def group_sum(values):
        return jnp.concatenate(
            [
                jnp.sum(values[8 * g : 8 * g + 8], axis=0, keepdims=True)
                for g in range(GROUPS)
            ],
            0,
        )

    centred = group_sum(dmixed * mixed_ref[...])
    gc[...] = jnp.zeros_like(gc)
    ge[...] = jnp.zeros_like(ge)
    dkp[...] = jnp.zeros_like(dkp)

    def attend_back(k, total):
        weight = sc[k]
        act_off = est[k, 128:144, :].astype(F32)
        pos_low = est[k, 64:128, :]
        ds2 = weight * (group_sum(dmixed * car[k]) - centred)
        ds2_low = jnp.concatenate([ds2, zeros8], 0).astype(BF16)
        ds1 = jnp.where(act_off[0:8] > 0, dot(w_att2, ds2_low), 0.0)
        ds1_low = jnp.concatenate([ds1, zeros8], 0).astype(BF16)
        ds1_kept = ds1_low.astype(F32)[0:8]
        dedge = dot(w_att1, ds1_low)
        dcarried = expand(weight) * dmixed
        dpos_low = (dedge + dcarried).astype(BF16)
        dpos_pre = jnp.where(pos_low.astype(F32) > 0, dot(w_pos2, dpos_low), 0.0).astype(BF16)
        small = jnp.concatenate([ds1, ds2], 0).astype(BF16)
        result = dot_nt(est[k], jnp.concatenate([dpos_pre, dpos_low, small], 0))
        gc[...] += result[:, 0:128]
        ge[:, 0:16] += result[:, 128:144]
        index = cnbr_ref[pl.ds(k, 1), pl.ds(half_at, half)]
        high = lax.shift_right_logical(index, low_shift)
        spread = place(jnp.concatenate([dcarried, ds1_kept], 0), high, parts)
        dkp[...] += dot_nt(spread, ohs[k]).reshape(parts, C1 + 8, LOW_B)
        return total + ds1_kept

    ds1_total = lax.fori_loop(0, NEIGH, attend_back, jnp.zeros((GROUPS, half), F32))
    give_dkv = sibling(4, dkp.at[pl.ds(other, my_parts)], dkr)
    give_dkv.start()
    give_dkv.wait_recv()
    dkv = own_half(dkp, dkr)
    w_att1_exact = w1[0:C1, 0:16].astype(BF16).astype(F32)[:, 0:8]
    dqueries = exact(w_att1_exact, ds1_total)
    dkeys = -exact(w_att1_exact, dkv[C1 : C1 + 8])
    dqkv_low = jnp.concatenate([dqueries, dkeys, dkv[0:C1]], 0).astype(BF16)
    gbuf[...] = jnp.zeros_like(gbuf)
    gbuf[0:64, :] = dot_nt(pooled_ref[...].astype(BF16), dqkv_low[0:128])
    gbuf[64:128, 0:64] = dot_nt(pooled_ref[...].astype(BF16), dqkv_low[128:192])
    dpooled = dblock + dot(w_qkv, dqkv_low)

    gb[...] = jnp.zeros_like(gb)
    gb[0:16, 0:C1] = dot_nt(centre_low, (-dpooled).astype(BF16))
    dscaled = dpooled * rsum_ref[...]

    def pool_back(k, carry):
        dpin = (pin[k] * dscaled).astype(BF16)
        joined = cat[k]
        dstem = jnp.where(joined[16:48].astype(F32) > 0, dot(w_down_stem, dpin), 0.0).astype(BF16)
        gb[:, 0:96] += dot_nt(joined, jnp.concatenate([dpin, dstem], 0))
        return carry

    lax.fori_loop(0, NEIGH, pool_back, 0)

    left = lanes_of(64, LANES) < 64
    gd_out = gd[64:128, :]
    gbuf[64:128, :] = jnp.where(left, gbuf[64:128, :], gc[64:128, :])
    gbuf[128:160, :] = jnp.where(left[0:32], pltpu.roll(gd_out[0:32], 64, 1), gd_out[32:64])
    base = 160
    pack(gbuf, base, ga, 0, 32, OFF["w_stem"], 6, C0)
    pack(gbuf, base, gb, 0, 64, OFF["w_stem"], 6, C0)
    pack(gbuf, base, ga, 7, 32, OFF["b_stem"], 1, C0)
    pack(gbuf, base, gb, 7, 64, OFF["b_stem"], 1, C0)
    pack(gbuf, base, gb, 0, 0, OFF["w_down"], 3, C1)
    pack(gbuf, base, gb, 16, 0, OFF["w_down"] + 3 * C1, C0, C1)
    pack(gbuf, base, gb, 7, 0, OFF["b_down"], 1, C1)
    pack(gbuf, base, gc, 136, 0, OFF["w_pos"], 3, C1)
    pack(gbuf, base, gc, 143, 0, OFF["b_pos"], 1, C1)
    pack(gbuf, base, ge, 0, 0, OFF["w_att1"], C1, GROUPS)
    pack(gbuf, base, ge, 143, 0, OFF["b_att1"], 1, GROUPS)
    pack(gbuf, base, ge, 128, 8, OFF["w_att2"], GROUPS, GROUPS)
    pack(gbuf, base, ge, 143, 8, OFF["b_att2"], 1, GROUPS)
    pack(gbuf, base, gd, 0, 0, OFF["w_up"], C1, C0)
    pack(gbuf, base, gd, 128, 0, OFF["b_up"], 1, C0)
    pack(gbuf, base, ga, 16, 0, OFF["w_skip"], C0, C0)
    pack(gbuf, base, ga, 48, 64, OFF["w_head"], C0, NCLS)
    pack(gbuf, base, ga, 7, 64, OFF["b_head"], 1, NCLS)
    loss_sum = jnp.sum(loss, axis=1, keepdims=True)
    line, lane = divmod(FLAT, LANES)
    at_loss = lanes_of(1, LANES) == lane
    gbuf[base + line : base + line + 1, :] += jnp.where(at_loss, loss_sum, 0.0)

    rows = gbuf.shape[0] // n_sub
    shards = rows // 8
    give_grad = sibling(5, gbuf.at[pl.ds(pl.multiple_of((1 - sub) * rows, rows), rows)], gsib)
    give_grad.start()
    give_grad.wait_recv()
    ghalf[...] = gbuf[pl.ds(pl.multiple_of(sub * rows, rows), rows), :] + gsib[...]
    mine_at = pl.multiple_of(sub * rows + me * 8, 8)

    def shard_copy(peer, index):
        return pltpu.make_async_remote_copy(
            src_ref=ghalf.at[pl.ds(pl.multiple_of(peer * 8, 8), 8)],
            dst_ref=gsh.at[index],
            send_sem=red_send.at[peer],
            recv_sem=red_recv.at[index],
            device_id={"pts": peer},
            device_id_type=MESH,
        )

    def sum_copy(peer, index):
        at = pl.multiple_of(sub * rows + index * 8, 8)
        return pltpu.make_async_remote_copy(
            src_ref=gfull.at[pl.ds(at, 8)],
            dst_ref=gfull.at[pl.ds(at, 8)],
            send_sem=gat_send.at[peer],
            recv_sem=gat_recv.at[index],
            device_id={"pts": peer},
            device_id_type=MESH,
        )

    holds = None if n_pts <= shards else me < shards

    def when(condition, run):
        if condition is None:
            run()
        else:
            pl.when(condition)(run)

    def each_peer(run, limited):
        def body(step, carry):
            peer = lax.rem(me + step, n_pts)
            when(None if holds is None or not limited else peer < shards, lambda: run(peer))
            return carry

        lax.fori_loop(1, n_pts, body, 0)

    each_peer(lambda peer: shard_copy(peer, me).start(), True)

    def reduce():
        gsh[me] = ghalf[pl.ds(pl.multiple_of(me * 8, 8), 8), :]
        each_peer(lambda peer: shard_copy(peer, peer).wait_recv(), False)
        gfull[pl.ds(mine_at, 8), :] = jnp.sum(gsh[...], axis=0)
        each_peer(lambda peer: sum_copy(peer, me).start(), False)

    when(holds, reduce)
    each_peer(lambda peer: sum_copy(peer, peer).wait_recv(), True)
    half_rows = gfull.at[pl.ds(pl.multiple_of(sub * rows, rows), rows)]
    give_full = sibling(6, half_rows, half_rows)
    give_full.start()

    each_peer(lambda peer: block_copy(peer, me).wait_send(), False)
    each_peer(lambda peer: mat_copy(peer, me).wait_send(), False)
    each_peer(lambda peer: shard_copy(peer, me).wait_send(), True)
    when(holds, lambda: each_peer(lambda peer: sum_copy(peer, me).wait_send(), False))
    for copy in (forward, give_pooled, give_block, give_dup, give_dkv, give_grad, give_full):
        copy.wait_send()
    give_full.wait_recv()
    out_ref[...] = gfull[...]


def orthonormal_pair(matrix):
    size = matrix.shape[0]
    lane = lanes_of(size, 2 * size)
    left = lane < size
    column = lanes_of(1, 2 * size)
    left_row = column < size
    place_row = jnp.where(left_row, column, column - size)
    for repeat in range(2):
        for j in range(size):
            pivot = jnp.where(left, matrix[:, j : j + 1], matrix[:, size + j : size + j + 1])
            products = jnp.sum(pivot * matrix, axis=0, keepdims=True)
            norms = jnp.where(
                left_row, products[:, j : j + 1], products[:, size + j : size + j + 1]
            )
            factor = jnp.where(place_row > j, products / norms, 0.0)
            matrix = matrix - pivot * factor
        matrix = matrix * lax.rsqrt(jnp.sum(matrix * matrix, axis=0, keepdims=True))
    return matrix


def soap_kernel(
    grads_ref,
    owner_ref,
    step_ref,
    weight_ref,
    first_ref,
    second_ref,
    left_ref,
    right_ref,
    basis_l_ref,
    basis_r_ref,
    average_ref,
    weight_out,
    first_out,
    second_out,
    left_out,
    right_out,
    basis_l_out,
    basis_r_out,
    average_out,
    flat_out,
    scalars_out,
):
    me = lax.axis_index("pts")
    grads = grads_ref[...]
    line, lane = divmod(FLAT, LANES)
    place_row = rows_of(256, LANES)
    at_loss = (place_row == 160 + line) & (lanes_of(256, LANES) == lane)
    loss = jnp.sum(jnp.where(at_loss, grads, 0.0))
    cleaned = jnp.where(at_loss, 0.0, grads)
    squares = jnp.sum(jnp.sum(cleaned * cleaned, axis=0, keepdims=True), axis=1, keepdims=True)
    norm = jnp.sqrt(squares)
    factor = jnp.minimum(1.0, CLIP_NORM / norm)
    flat_out[...] = cleaned[160:216] * factor
    at = lanes_of(8, LANES)
    scalars_out[...] = jnp.where(at == 0, loss, jnp.where(at == 1, norm, 0.0))
    folded = cleaned[128:160]
    stacked = [
        cleaned[0:64, 0:64],
        cleaned[0:64, 64:128],
        cleaned[64:128, 0:64],
        cleaned[64:128, 64:128],
        jnp.concatenate([folded[:, 0:64], folded[:, 64:128]], 0),
    ]
    grad = jnp.zeros((C1, C1), F32)
    owned = 0.0
    for position in range(NMATS):
        flag = jnp.where(owner_ref[position] == me, 1.0, 0.0)
        grad = grad + flag * stacked[position]
        owned = owned + flag
    grad = grad * factor
    count = jnp.full((1, 1), step_ref[0].astype(F32), F32)
    one_scale = 1.0 - jnp.exp(count * math.log(BETA_ONE))
    two_scale = 1.0 - jnp.exp(count * math.log(BETA_TWO))
    basis_l = basis_l_ref[...]
    basis_r = basis_r_ref[...]
    left_new = BETA_TWO * left_ref[...] + (1.0 - BETA_TWO) * exact(grad, grad, ((1,), (1,)))
    right_new = BETA_TWO * right_ref[...] + (1.0 - BETA_TWO) * exact(grad, grad, ((0,), (0,)))
    both = orthonormal_pair(
        jnp.concatenate([exact(left_new, basis_l), exact(right_new, basis_r)], 1)
    )
    basis_l_new = both[:, 0:C1]
    basis_r_new = both[:, C1 : 2 * C1]
    rotated = exact(exact(basis_l, grad, ((0,), (0,))), basis_r)
    first_new = BETA_ONE * first_ref[...] + (1.0 - BETA_ONE) * rotated
    second_new = BETA_TWO * second_ref[...] + (1.0 - BETA_TWO) * rotated * rotated
    scaled = first_new / one_scale / (jnp.sqrt(second_new / two_scale) + ADAM_EPS)
    weight = weight_ref[...]
    weight_new = weight - LEARN_RATE * (
        exact(exact(basis_l, scaled), basis_r, ((1,), (1,))) + WEIGHT_DECAY * weight
    )
    plain = exact(exact(basis_l, first_new), basis_r, ((1,), (1,)))
    first_rotated = exact(exact(basis_l_new, plain, ((0,), (0,))), basis_r_new)
    average_new = EMA_KEEP * average_ref[...] + (1.0 - EMA_KEEP) * weight_new
    held = owned > 0.5
    weight_out[...] = jnp.where(held, weight_new, 0.0)
    first_out[...] = jnp.where(held, first_rotated, 0.0)
    second_out[...] = jnp.where(held, second_new, 0.0)
    left_out[...] = jnp.where(held, left_new, 0.0)
    right_out[...] = jnp.where(held, right_new, 0.0)
    basis_l_out[...] = jnp.where(held, basis_l_new, 0.0)
    basis_r_out[...] = jnp.where(held, basis_r_new, 0.0)
    average_out[...] = jnp.where(held, average_new, 0.0)


def adam_update(weight, grad, first, second, average, count):
    first_new = BETA_ONE * first + (1.0 - BETA_ONE) * grad
    second_new = BETA_TWO * second + (1.0 - BETA_TWO) * grad * grad
    scaled = (
        first_new
        / (1.0 - BETA_ONE**count)
        / (jnp.sqrt(second_new / (1.0 - BETA_TWO**count)) + ADAM_EPS)
    )
    weight_new = weight - LEARN_RATE * (scaled + WEIGHT_DECAY * weight)
    return (weight_new, first_new, second_new, EMA_KEEP * average + (1.0 - EMA_KEEP) * weight_new)


def local(
    points,
    route,
    labels,
    interp_src,
    pool_nbr,
    sample,
    coarse_nbr,
    owner,
    step,
    flat,
    flat_mom,
    flat_sec,
    flat_ema,
    mats,
    mats_mom,
    mats_sec,
    mats_left,
    mats_right,
    mats_basis_l,
    mats_basis_r,
    mats_ema,
):
    n_pts = lax.axis_size("pts")
    n_sub = lax.axis_size("sub")
    fine = points.shape[0]
    coarse = sample.shape[0]
    cap = n_sub * fine // n_pts
    slots = n_pts * cap
    sources = n_sub * n_pts
    half = coarse // n_sub
    parts = coarse // LOW_B
    my_parts = parts // n_sub
    flat2 = jnp.pad(flat, (0, FLAT_ROWS * LANES - FLAT)).reshape(FLAT_ROWS, LANES)
    vmem = pl.BlockSpec(memory_space=pltpu.VMEM)
    smem = pl.BlockSpec(memory_space=pltpu.SMEM)
    dma = pltpu.SemaphoreType.DMA
    scratch = [
        VMEM((16, fine), F32),
        VMEM((n_pts * 16, cap), F32),
        VMEM((n_pts, 16, cap), BF16),
        VMEM((sources, 16, cap), BF16),
        VMEM((32, LANES), BF16),
        VMEM((n_pts, 32, LANES), BF16),
        VMEM((sources * 8, cap), BF16),
        VMEM((8, coarse), F32),
        VMEM((NEIGH, C1, half), F32),
        VMEM((NEIGH, 48, half), BF16),
        VMEM((C1, half), F32),
        VMEM((C1, half), F32),
        VMEM((parts, CH, LOW_B), BF16),
        VMEM((parts, CH, LOW_B), BF16),
        VMEM((NEIGH, 144, half), BF16),
        VMEM((NEIGH, LOW_B, half), BF16),
        VMEM((NEIGH, C1, half), F32),
        VMEM((NEIGH, GROUPS, half), F32),
        VMEM((C1, half), F32),
        VMEM((C1, half), F32),
        VMEM((16, slots), F32),
        VMEM((parts, C0, LOW_B), F32),
        VMEM((my_parts, C0, LOW_B), F32),
        VMEM((parts, C1 + 8, LOW_B), F32),
        VMEM((my_parts, C1 + 8, LOW_B), F32),
        VMEM((LANES, LANES), F32),
        VMEM((LANES, LANES), F32),
        VMEM((LANES, LANES), F32),
        VMEM((LANES, LANES), F32),
        VMEM((LANES, LANES), F32),
        VMEM((LANES, LANES), F32),
        VMEM((LANES, LANES), F32),
        VMEM((LANES, LANES), F32),
        VMEM((LANES, LANES), F32),
        VMEM((80, LANES), F32),
        VMEM((48, LANES), F32),
        VMEM((144, LANES), F32),
        VMEM((144, LANES), F32),
        VMEM((144, LANES), F32),
        VMEM((256, LANES), F32),
        VMEM((128, LANES), F32),
        VMEM((128, LANES), F32),
        VMEM((n_pts, 8, LANES), F32),
        VMEM((256, LANES), F32),
        dma((n_pts,)),
        dma((n_pts,)),
        dma((n_pts,)),
        dma((n_pts,)),
        dma((n_pts,)),
        dma((n_pts,)),
        dma((n_pts,)),
        dma((n_pts,)),
        dma((8,)),
        dma((8,)),
    ]
    reduced = pl.pallas_call(
        functools.partial(main_kernel, n_pts, n_sub),
        out_shape=jax.ShapeDtypeStruct((256, LANES), F32),
        in_specs=[vmem] * 7 + [smem] + [vmem] * 2,
        out_specs=vmem,
        scratch_shapes=scratch,
        compiler_params=pltpu.CompilerParams(
            collective_id=0, has_side_effects=True, vmem_limit_bytes=48 * 1024 * 1024
        ),
    )(
        points.T,
        route.reshape(1, fine),
        labels.reshape(1, fine),
        interp_src.T,
        pool_nbr.T,
        sample.reshape(1, coarse),
        coarse_nbr.T,
        owner,
        flat2,
        mats[0],
    )
    square = jax.ShapeDtypeStruct((C1, C1), F32)
    results = pl.pallas_call(
        soap_kernel,
        out_shape=[square] * 8
        + [
            jax.ShapeDtypeStruct((56, LANES), F32),
            jax.ShapeDtypeStruct((8, LANES), F32),
        ],
        in_specs=[vmem] + [smem] * 2 + [vmem] * 8,
        out_specs=[vmem] * 10,
    )(
        reduced,
        owner,
        step,
        mats[0],
        mats_mom[0],
        mats_sec[0],
        mats_left[0],
        mats_right[0],
        mats_basis_l[0],
        mats_basis_r[0],
        mats_ema[0],
    )
    flat_grad = results[8].reshape(-1)[:FLAT]
    count = step[0].astype(F32)
    flat_out = adam_update(flat, flat_grad, flat_mom, flat_sec, flat_ema, count)
    return (results[9][0, 0], results[9][0, 1]) + flat_out + tuple(
        result[None] for result in results[:8]
    )


def solution(mesh):
    placed = (
        P(("pts", "sub"), None),
        P(("pts", "sub")),
        P(("pts", "sub")),
        P(("pts", "sub"), None),
        P("pts", None),
        P("pts"),
        P("pts", None),
        P(),
        P(),
        P(),
        P(),
        P(),
        P(),
    ) + (P("pts", None, None),) * 8
    return jax.shard_map(
        local,
        mesh=mesh,
        in_specs=placed,
        out_specs=(P(),) * 6 + (P("pts", None, None),) * 8,
        check_vma=False,
    )
```

```python
import functools
import math

import jax
import jax.numpy as jnp
from jax import lax
from jax.experimental import pallas as pl
from jax.experimental.pallas import tpu as pltpu
from jax.sharding import PartitionSpec as P

C0 = 32
C1 = 64
NEIGH = 16
NCLS = 13
GROUPS = 8
NMATS = 5

HIGHEST = lax.Precision.HIGHEST
CLIP_NORM = 0.01
BETA_ONE = 0.9
BETA_TWO = 0.95
ADAM_EPS = 1e-08
LEARN_RATE = 0.1
WEIGHT_DECAY = 0.01
EMA_KEEP = 0.9
INTERP_EPS = 0.01

F32 = jnp.float32
BF16 = jnp.bfloat16
I32 = jnp.int32
MESH = pl.DeviceIdType.MESH
VMEM = pltpu.VMEM

LANES = 128
FLAT_ROWS = 64
LOW_B = 256
CH = 80
NEG = -1e30


def offsets():
    shapes = [
        ("w_stem", (6, C0)),
        ("b_stem", (C0,)),
        ("w_down", (3 + C0, C1)),
        ("b_down", (C1,)),
        ("w_pos", (3, C1)),
        ("b_pos", (C1,)),
        ("w_att1", (C1, GROUPS)),
        ("b_att1", (GROUPS,)),
        ("w_att2", (GROUPS, GROUPS)),
        ("b_att2", (GROUPS,)),
        ("w_up", (C1, C0)),
        ("b_up", (C0,)),
        ("w_skip", (C0, C0)),
        ("w_head", (C0, NCLS)),
        ("b_head", (NCLS,)),
    ]
    found = {}
    total = 0
    for name, shape in shapes:
        found[name] = total
        total += math.prod(shape)
    return found, total


OFF, FLAT = offsets()


def dot(left, right):
    return lax.dot_general(left, right, (((1,), (0,)), ((), ())), preferred_element_type=F32)


def dot_nt(left, right):
    return lax.dot_general(left, right, (((1,), (1,)), ((), ())), preferred_element_type=F32)


def exact(left, right, dims=((1,), (0,))):
    return lax.dot_general(
        left, right, (dims, ((), ())), precision=HIGHEST, preferred_element_type=F32
    )


def relu(values):
    return jnp.maximum(values, 0.0)


def rows_of(count, length):
    return lax.broadcasted_iota(I32, (count, length), 0)


def lanes_of(count, length):
    return lax.broadcasted_iota(I32, (count, length), 1)


def onehot(low, count):
    hit = rows_of(count, low.shape[1]) == low
    return jnp.where(hit, 1.0, 0.0).astype(BF16)


def pick(spread, high, parts):
    each = spread.shape[0] // parts
    found = spread[0:each]
    for part in range(1, parts):
        found = jnp.where(high == part, spread[part * each : (part + 1) * each], found)
    return found


def place(values, high, parts):
    return jnp.concatenate(
        [jnp.where(high == part, values, 0.0) for part in range(parts)], 0
    ).astype(BF16)


def unpack(flat_ref, out_ref, offset, rows, width, at):
    stride = LANES // width if LANES % width == 0 else rows
    for first in range(min(stride, rows)):
        count = (rows - first + stride - 1) // stride
        padded = -(-count // 8) * 8
        line, lane = divmod(offset + first * width, LANES)
        values = flat_ref[line : line + padded, :]
        if lane:
            values = pltpu.roll(values, LANES - lane, 1)
        if lane + width > LANES:
            following = pltpu.roll(flat_ref[line + 1 : line + 1 + padded, :], LANES - lane, 1)
            values = jnp.where(lanes_of(padded, LANES) < LANES - lane, values, following)
        values = jnp.where(lanes_of(padded, LANES) < width, values, 0.0)
        if count == 1:
            out_ref[at + first : at + first + 1, :] = values[0:1]
        else:
            out_ref[pl.ds(at + first, count, stride=stride), :] = values[0:count]


def pack(out_ref, base, source_ref, row, lane_from, offset, rows, width):
    stride = LANES // width if LANES % width == 0 else rows
    for first in range(min(stride, rows)):
        count = (rows - first + stride - 1) // stride
        line, lane = divmod(offset + first * width, LANES)
        if count == 1:
            values = source_ref[row + first : row + first + 1, :]
        else:
            values = source_ref[pl.ds(row + first, count, stride=stride), :]
        shift = (lane - lane_from) % LANES
        padded = -(-count // 8) * 8
        if padded != count:
            values = jnp.concatenate([values, jnp.zeros((padded - count, LANES), F32)], 0)
        if shift:
            values = pltpu.roll(values, shift, 1)
        values = values[0:count]
        at = lanes_of(count, LANES)
        here = jnp.where((at >= lane) & (at < lane + width), values, 0.0)
        out_ref[base + line : base + line + count, :] += here
        if lane + width > LANES:
            there = jnp.where(at < lane + width - LANES, values, 0.0)
            out_ref[base + line + 1 : base + line + 1 + count, :] += there


def main_kernel(
    n_pts,
    n_sub,
    pts_hbm,
    route_hbm,
    labels_hbm,
    src_hbm,
    pool_hbm,
    sample_hbm,
    cnbr_hbm,
    owner_hbm,
    mats_hbm,
    flat_ref,
    out_ref,
    pts_ref,
    route_ref,
    labels_ref,
    src_ref,
    pool_ref,
    sample_ref,
    cnbr_ref,
    owner_ref,
    mats_ref,
    data,
    sacc,
    sendb,
    recv,
    matmine,
    matall,
    tabb,
    cen,
    pin,
    cat,
    pooled_ref,
    rsum_ref,
    ctab,
    btab,
    est,
    ohs,
    car,
    sc,
    mixed_ref,
    blk_ref,
    slot,
    dcp,
    dcr,
    dkp,
    dkr,
    wst,
    wd,
    wp,
    w1,
    w2,
    wu,
    wsk,
    wh,
    bias,
    ga,
    gb,
    gc,
    gd,
    ge,
    gbuf,
    gsib,
    ghalf,
    gsh,
    gfull,
    a2a_send,
    a2a_recv,
    mat_send,
    mat_recv,
    red_send,
    red_recv,
    gat_send,
    gat_recv,
    sib_send,
    sib_recv,
    load_sem,
):
    fine = route_ref.shape[1]
    coarse = sample_ref.shape[1]
    cap = sendb.shape[2]
    slots = n_pts * cap
    half = coarse // n_sub
    sources = n_sub * n_pts
    parts = coarse // LOW_B
    my_parts = parts // n_sub
    shift = cap.bit_length() - 1
    low_shift = LOW_B.bit_length() - 1
    span = 512
    me = lax.axis_index("pts")
    sub = lax.axis_index("sub")
    half_at = pl.multiple_of(sub * half, half)

    held = (pts_hbm, route_hbm, labels_hbm, src_hbm, mats_hbm, sample_hbm, pool_hbm, cnbr_hbm, owner_hbm)
    near = (pts_ref, route_ref, labels_ref, src_ref, mats_ref, sample_ref, pool_ref, cnbr_ref, owner_ref)
    loads = [
        pltpu.make_async_copy(source, target, load_sem.at[number])
        for number, (source, target) in enumerate(zip(held, near))
    ]
    for load in loads:
        load.start()

    barrier = pltpu.get_barrier_semaphore()

    def greet(step, carry):
        peer = lax.rem(me + step, n_pts)
        pl.semaphore_signal(barrier, inc=1, device_id={"pts": peer}, device_id_type=MESH)
        return carry

    lax.fori_loop(1, n_pts, greet, 0)
    pl.semaphore_signal(barrier, inc=1, device_id={"sub": 1 - sub}, device_id_type=MESH)

    def sibling(number, source, target):
        return pltpu.make_async_remote_copy(
            src_ref=source,
            dst_ref=target,
            send_sem=sib_send.at[number],
            recv_sem=sib_recv.at[number],
            device_id={"sub": 1 - sub},
            device_id_type=MESH,
        )

    for load in loads[0:5]:
        load.wait()
    data[0:6, :] = pts_ref[...].astype(F32)
    data[6:8, :] = jnp.zeros((2, fine), F32)
    source_rows = src_ref[...]
    data[8:11, :] = lax.shift_right_logical(source_rows, 5).astype(F32)
    data[11:14, :] = (source_rows & 31).astype(F32)
    data[14:15, :] = (labels_ref[...] + 1).astype(F32)
    data[15:16, :] = jnp.zeros((1, fine), F32)
    sacc[...] = jnp.zeros_like(sacc)
    counts = jnp.zeros((16, 32), F32)
    for chunk in range(fine // span):
        lanes = slice(chunk * span, (chunk + 1) * span)
        route = route_ref[:, lanes]
        high = lax.shift_right_logical(route, shift)
        spread = place(data[:, lanes], high, n_pts)
        sacc[...] += dot_nt(spread, onehot(route & (cap - 1), cap))
        classes = onehot(labels_ref[:, lanes], 16)
        counts = counts + dot_nt(jnp.ones((16, span), BF16), jnp.concatenate([classes, classes], 0))
    count_high = jnp.floor(counts * (1.0 / 128.0))
    count_low = counts - 128.0 * count_high
    digits = jnp.where(lanes_of(16, 32) < 16, count_low, count_high)
    digits = jnp.where(rows_of(16, 32) == 15, digits, 0.0)
    data[:, 0:cap] = jnp.zeros((16, cap), F32)
    data[:, 0:32] = digits
    sendb[...] = (sacc[...].reshape(n_pts, 16, cap) + data[:, 0:cap][None]).astype(BF16)
    matrix = mats_ref[...]
    matmine[...] = jnp.concatenate([matrix[0:32], matrix[32:64]], 1).astype(BF16)

    pl.semaphore_wait(barrier, n_pts)

    def block_copy(peer, index):
        return pltpu.make_async_remote_copy(
            src_ref=sendb.at[peer],
            dst_ref=recv.at[sub * n_pts + index],
            send_sem=a2a_send.at[peer],
            recv_sem=a2a_recv.at[index],
            device_id={"pts": peer},
            device_id_type=MESH,
        )

    def mat_copy(peer, index):
        return pltpu.make_async_remote_copy(
            src_ref=matmine,
            dst_ref=matall.at[index],
            send_sem=mat_send.at[peer],
            recv_sem=mat_recv.at[index],
            device_id={"pts": peer},
            device_id_type=MESH,
        )

    def send_blocks(step, carry):
        block_copy(lax.rem(me + step, n_pts), me).start()
        return carry

    def send_mats(step, carry):
        mat_copy(lax.rem(me + step, n_pts), me).start()
        return carry

    lax.fori_loop(1, n_pts, send_blocks, 0)
    recv[sub * n_pts + me] = sendb[me]
    matall[me] = matmine[...]

    for ref in (wst, wd, wp, w1, w2, wu, wsk, wh, bias):
        ref[...] = jnp.zeros_like(ref)
    unpack(flat_ref, wst, OFF["w_stem"], 6, C0, 0)
    unpack(flat_ref, wd, OFF["w_down"], 3, C1, 0)
    unpack(flat_ref, wd, OFF["w_down"] + 3 * C1, C0, C1, 16)
    unpack(flat_ref, wp, OFF["w_pos"], 3, C1, 8)
    unpack(flat_ref, w1, OFF["w_att1"], C1, GROUPS, 0)
    unpack(flat_ref, w2, OFF["w_att2"], GROUPS, GROUPS, 0)
    unpack(flat_ref, wu, OFF["w_up"], C1, C0, 0)
    unpack(flat_ref, wsk, OFF["w_skip"], C0, C0, 0)
    unpack(flat_ref, wh, OFF["w_head"], C0, NCLS, 0)
    names = ("b_stem", "b_down", "b_pos", "b_att1", "b_att2", "b_up", "b_head")
    widths = (C0, C1, C1, GROUPS, GROUPS, C0, NCLS)
    for position, (name, width) in enumerate(zip(names, widths)):
        unpack(flat_ref, bias, OFF[name], 1, width, position)
    columns = bias[...].T
    b_stem = columns[0:C0, 0:1]
    b_down = columns[0:C1, 1:2]
    b_pos = columns[0:C1, 2:3]
    b_att1 = columns[0:GROUPS, 3:4]
    b_att2 = columns[0:GROUPS, 4:5]
    b_up = columns[0:C0, 5:6]
    b_head = jnp.where(rows_of(16, 1) < NCLS, columns[0:16, 6:7], NEG)
    w_stem_t = wst[...].T[0:C0, 0:16].astype(BF16)
    w_down_t = wd[...].T[0:C1, 0:48].astype(BF16)
    w_pos_t = wp[...].T[0:C1, 0:16].astype(BF16)
    w_att1_t = w1[...].T[0:GROUPS, 0:C1].astype(BF16)
    w_att2_t = w2[...].T[0:GROUPS, 0:16].astype(BF16)
    w_up_t = wu[...].T[0:C0, 0:C1].astype(BF16)
    w_skip_t = wsk[...].T[0:C0, 0:C0].astype(BF16)
    w_head_t = wh[...].T[0:16, 0:C0].astype(BF16)
    w_down_stem = wd[16:48, 0:C1].astype(BF16)
    w_att1 = w1[0:C1, 0:16].astype(BF16)
    w_att2 = w2[0:GROUPS, 0:16].astype(BF16)
    w_up = wu[0:C1, 0:C0].astype(BF16)
    w_skip = wsk[0:C0, 0:C0].astype(BF16)
    w_head = wh[0:C0, 0:16].astype(BF16)

    def wait_blocks(step, carry):
        peer = lax.rem(me + step, n_pts)
        block_copy(peer, peer).wait_recv()
        return carry

    lax.fori_loop(1, n_pts, wait_blocks, 0)
    lax.fori_loop(1, n_pts, send_mats, 0)
    for load in loads[5:]:
        load.wait()
    mine = recv.at[pl.ds(sub * n_pts, n_pts)]
    forward = sibling(0, mine, mine)
    forward.start()
    for source in range(n_pts):
        slot[:, source * cap : (source + 1) * cap] = recv[sub * n_pts + source].astype(F32)
    forward.wait_recv()

    table = recv[...].astype(F32)[:, 0:8, :].reshape(sources * 8, cap)
    ones_row = (rows_of(sources * 8, cap) & 7) == 7
    tabb[...] = jnp.where(ones_row, 1.0, table).astype(BF16)
    count_row = jnp.sum(recv[...].astype(F32)[:, 8:16, :], axis=0)[7:8, 0:32]
    count_at = jnp.broadcast_to(count_row, (16, 32))
    low_hit = lanes_of(16, 32) == rows_of(16, 32)
    high_hit = lanes_of(16, 32) == rows_of(16, 32) + 16
    class_counts = jnp.sum(
        jnp.where(low_hit, count_at, 0.0) + jnp.where(high_hit, 128.0 * count_at, 0.0),
        axis=1,
        keepdims=True,
    )
    total_fine = float(fine * n_pts * n_sub)
    class_w = jnp.where(rows_of(16, 1) < NCLS, total_fine / (NCLS * class_counts), 0.0)

    def gather_points(index):
        hot = onehot(index & (cap - 1), cap)
        return pick(dot(tabb[...], hot), lax.shift_right_logical(index, shift), sources)

    zeros8 = jnp.zeros((8, span), F32)
    for chunk in range(coarse // span):
        lanes = slice(chunk * span, (chunk + 1) * span)
        found = gather_points(sample_ref[:, lanes])
        cen[:, lanes] = jnp.where(rows_of(8, span) < 6, found, 0.0)
    centre = cen[:, pl.ds(half_at, half)]
    centre_low = jnp.concatenate([centre, zeros8], 0).astype(BF16)
    w_xyz_t = jnp.where(lanes_of(C1, 16) < 3, wd[...].T[0:C1, 0:16], 0.0).astype(BF16)
    centre_term = dot(w_xyz_t, centre_low)

    def pool_step(k, most):
        found = gather_points(pool_ref[pl.ds(k, 1), pl.ds(half_at, half)])
        low = jnp.concatenate([found, zeros8], 0).astype(BF16)
        stem = relu(dot(w_stem_t, low) + b_stem)
        joined = jnp.concatenate([found, zeros8, stem], 0).astype(BF16)
        cat[k] = joined
        projected = dot(w_down_t, joined).astype(BF16).astype(F32)
        value = projected - centre_term + b_down
        pin[k] = value
        return jnp.maximum(most, value)

    most = lax.fori_loop(0, NEIGH, pool_step, jnp.full((C1, half), -jnp.inf, F32), unroll=4)

    def exp_step(k, total):
        value = jnp.exp(pin[k] - most)
        pin[k] = value
        return total + value

    total = lax.fori_loop(0, NEIGH, exp_step, jnp.zeros((C1, half), F32), unroll=4)
    pooled = most + jnp.log(total)
    pooled_ref[...] = pooled
    rsum_ref[...] = 1.0 / total

    def table_rows(values, target):
        for part in range(my_parts):
            lanes = slice(part * LOW_B, (part + 1) * LOW_B)
            stacked = jnp.concatenate(
                [values[:, lanes], centre[:, lanes], jnp.zeros((8, LOW_B), F32)], 0
            )
            target[sub * my_parts + part] = stacked.astype(BF16)

    table_rows(pooled, ctab)
    my_ctab = ctab.at[pl.ds(sub * my_parts, my_parts)]
    give_pooled = sibling(1, my_ctab, my_ctab)
    give_pooled.start()

    def wait_mats(step, carry):
        peer = lax.rem(me + step, n_pts)
        mat_copy(peer, peer).wait_recv()
        return carry

    lax.fori_loop(1, n_pts, wait_mats, 0)

    def layer(position):
        folded = matall[owner_ref[position]].astype(F32)
        return jnp.concatenate([folded[:, 0:C1], folded[:, C1 : 2 * C1]], 0)

    w_qkv32 = jnp.concatenate([layer(0), layer(1), layer(2)], 1)
    w_qkv = w_qkv32.astype(BF16)
    w_query_t = w_qkv32[:, 0:C1].T.astype(BF16)
    w_kv_t = jnp.concatenate([w_qkv32[:, C1 : 2 * C1].T, w_qkv32[:, 2 * C1 :].T], 0).astype(BF16)
    w_pos2_32 = layer(3)
    w_pos2 = w_pos2_32.astype(BF16)
    w_pos2_t = w_pos2_32.T.astype(BF16)
    w_out_32 = layer(4)
    w_out = w_out_32.astype(BF16)
    w_out_t = w_out_32.T.astype(BF16)
    pooled_low = pooled.astype(BF16)
    queries = dot(w_query_t, pooled_low)
    give_pooled.wait_recv()

    def expand(values):
        return jnp.concatenate(
            [jnp.broadcast_to(values[g : g + 1], (8, values.shape[1])) for g in range(GROUPS)], 0
        )

    def attend(k, most):
        index = cnbr_ref[pl.ds(k, 1), pl.ds(half_at, half)]
        high = lax.shift_right_logical(index, low_shift)
        hot = onehot(index & (LOW_B - 1), LOW_B)
        ohs[k] = hot
        found = pick(dot(ctab[...].reshape(parts * CH, LOW_B), hot), high, parts)
        near = found[0:C1].astype(BF16)
        rows = dot(w_kv_t, near)
        offset = jnp.where(rows_of(8, half) == 7, 1.0, centre - found[C1 : C1 + 8])
        off_low = jnp.concatenate([zeros8, offset], 0).astype(BF16)
        pos_low = relu(dot(w_pos_t, off_low) + b_pos).astype(BF16)
        pos_enc = dot(w_pos2_t, pos_low)
        edge_low = (queries - rows[0:C1] + pos_enc).astype(BF16)
        act = relu(dot(w_att1_t, edge_low) + b_att1)
        act_off = jnp.concatenate([act, offset], 0).astype(BF16)
        score = dot(w_att2_t, act_off) + b_att2
        est[k, 0:64, :] = edge_low
        est[k, 64:128, :] = pos_low
        est[k, 128:144, :] = act_off
        car[k] = rows[C1 : 2 * C1] + pos_enc
        sc[k] = score
        return jnp.maximum(most, score)

    top = lax.fori_loop(0, NEIGH, attend, jnp.full((GROUPS, half), -jnp.inf, F32), unroll=4)

    def weigh(k, total):
        value = jnp.exp(sc[k] - top)
        sc[k] = value
        return total + value

    scale = 1.0 / lax.fori_loop(0, NEIGH, weigh, jnp.zeros((GROUPS, half), F32), unroll=8)

    def mix(k, total):
        weight = sc[k] * scale
        sc[k] = weight
        return total + expand(weight) * car[k]

    mixed = lax.fori_loop(0, NEIGH, mix, jnp.zeros((C1, half), F32), unroll=4)
    mixed_ref[...] = mixed
    block = pooled_ref[...] + dot(w_out_t, mixed.astype(BF16))
    blk_ref[...] = block
    table_rows(block, btab)
    my_btab = btab.at[pl.ds(sub * my_parts, my_parts)]
    give_block = sibling(2, my_btab, my_btab)
    give_block.start()
    give_block.wait_recv()

    ga[...] = jnp.zeros_like(ga)
    dcp[...] = jnp.zeros_like(dcp)

    def fine_step(step, loss):
        at = pl.multiple_of(step * span, span)
        rows = slot[:, pl.ds(at, span)]
        points = rows[0:8]
        source = (32.0 * rows[8:11] + rows[11:14]).astype(I32)
        label = rows[14:15].astype(I32)
        hots = []
        highs = []
        ups = []
        inverses = []
        for i in range(3):
            index = source[i : i + 1]
            high = lax.shift_right_logical(index, low_shift)
            hot = onehot(index & (LOW_B - 1), LOW_B)
            found = pick(dot(btab[...].reshape(parts * CH, LOW_B), hot), high, parts)
            ups.append(dot(w_up_t, found[0:C1].astype(BF16)) + b_up)
            diff = jnp.where(rows_of(8, span) < 3, points - found[C1 : C1 + 8], 0.0)
            inverses.append(1.0 / (jnp.sum(diff * diff, axis=0, keepdims=True) + INTERP_EPS))
            hots.append(hot)
            highs.append(high)
        norm = inverses[0] + inverses[1] + inverses[2]
        weights = [inverse / norm for inverse in inverses]
        interp = weights[0] * ups[0] + weights[1] * ups[1] + weights[2] * ups[2]
        interp = interp.astype(BF16).astype(F32)
        ones = jnp.where(rows_of(8, span) == 7, 1.0, points)
        points_low = jnp.concatenate([ones, zeros8], 0).astype(BF16)
        stem_pre = dot(w_stem_t, points_low) + b_stem
        stem_low = relu(stem_pre).astype(BF16)
        joined = interp + dot(w_skip_t, stem_low)
        joined_low = relu(joined).astype(BF16)
        logits = dot(w_head_t, joined_low) + b_head
        hit = jnp.where(rows_of(16, span) + 1 == label, 1.0, 0.0)
        row_w = jnp.sum(hit * class_w, axis=0, keepdims=True) * (1.0 / total_fine)
        peak = jnp.max(logits, axis=0, keepdims=True)
        lse = peak + jnp.log(jnp.sum(jnp.exp(logits - peak), axis=0, keepdims=True))
        loss = loss + row_w * (lse - jnp.sum(hit * logits, axis=0, keepdims=True))
        dlog_low = (row_w * (jnp.exp(logits - lse) - hit)).astype(BF16)
        dfused_low = jnp.where(joined > 0, dot(w_head, dlog_low), 0.0).astype(BF16)
        dfused = dfused_low.astype(F32)
        dstem = jnp.where(stem_pre > 0, dot(w_skip, dfused_low), 0.0).astype(BF16)
        inputs = jnp.concatenate([points_low, stem_low, joined_low], 0)
        grads = jnp.concatenate([dfused_low, dstem, dlog_low], 0)
        ga[:, 0:80] += dot_nt(inputs, grads)
        spread = jnp.concatenate(
            [place(weights[i] * dfused, highs[i], parts) for i in range(3)], 1
        )
        dcp[...] += dot_nt(spread, jnp.concatenate(hots, 1)).reshape(parts, C0, LOW_B)
        return loss

    loss = lax.fori_loop(0, slots // span, fine_step, jnp.zeros((1, span), F32), unroll=2)

    other = (1 - sub) * my_parts
    own = sub * my_parts
    give_dup = sibling(3, dcp.at[pl.ds(other, my_parts)], dcr)
    give_dup.start()
    give_dup.wait_recv()

    def own_half(partial, received):
        return jnp.concatenate(
            [partial[own + part] + received[part] for part in range(my_parts)], 1
        )

    dup_low = own_half(dcp, dcr).astype(BF16)
    dblock = dot(w_up, dup_low)
    dbranch_low = dblock.astype(BF16)
    dmixed = dot(w_out, dbranch_low)
    inputs = jnp.concatenate(
        [blk_ref[...].astype(BF16), mixed_ref[...].astype(BF16), jnp.ones((16, half), BF16)], 0
    )
    grads = jnp.concatenate([dup_low, jnp.zeros((C0, half), BF16), dbranch_low], 0)
    gd[...] = dot_nt(inputs, grads)

    def group_sum(values):
        return jnp.concatenate(
            [
                jnp.sum(values[8 * g : 8 * g + 8], axis=0, keepdims=True)
                for g in range(GROUPS)
            ],
            0,
        )

    centred = group_sum(dmixed * mixed_ref[...])
    gc[...] = jnp.zeros_like(gc)
    ge[...] = jnp.zeros_like(ge)
    dkp[...] = jnp.zeros_like(dkp)

    def attend_back(k, total):
        weight = sc[k]
        act_off = est[k, 128:144, :].astype(F32)
        pos_low = est[k, 64:128, :]
        ds2 = weight * (group_sum(dmixed * car[k]) - centred)
        ds2_low = jnp.concatenate([ds2, zeros8], 0).astype(BF16)
        ds1 = jnp.where(act_off[0:8] > 0, dot(w_att2, ds2_low), 0.0)
        ds1_low = jnp.concatenate([ds1, zeros8], 0).astype(BF16)
        ds1_kept = ds1_low.astype(F32)[0:8]
        dedge = dot(w_att1, ds1_low)
        dcarried = expand(weight) * dmixed
        dpos_low = (dedge + dcarried).astype(BF16)
        dpos_pre = jnp.where(pos_low.astype(F32) > 0, dot(w_pos2, dpos_low), 0.0).astype(BF16)
        small = jnp.concatenate([ds1, ds2], 0).astype(BF16)
        result = dot_nt(est[k], jnp.concatenate([dpos_pre, dpos_low, small], 0))
        gc[...] += result[:, 0:128]
        ge[:, 0:16] += result[:, 128:144]
        index = cnbr_ref[pl.ds(k, 1), pl.ds(half_at, half)]
        high = lax.shift_right_logical(index, low_shift)
        spread = place(jnp.concatenate([dcarried, ds1_kept], 0), high, parts)
        dkp[...] += dot_nt(spread, ohs[k]).reshape(parts, C1 + 8, LOW_B)
        return total + ds1_kept

    ds1_total = lax.fori_loop(0, NEIGH, attend_back, jnp.zeros((GROUPS, half), F32), unroll=4)
    give_dkv = sibling(4, dkp.at[pl.ds(other, my_parts)], dkr)
    give_dkv.start()
    give_dkv.wait_recv()
    dkv = own_half(dkp, dkr)
    w_att1_exact = w1[0:C1, 0:16].astype(BF16).astype(F32)[:, 0:8]
    dqueries = exact(w_att1_exact, ds1_total)
    dkeys = -exact(w_att1_exact, dkv[C1 : C1 + 8])
    dqkv_low = jnp.concatenate([dqueries, dkeys, dkv[0:C1]], 0).astype(BF16)
    gbuf[...] = jnp.zeros_like(gbuf)
    gbuf[0:64, :] = dot_nt(pooled_ref[...].astype(BF16), dqkv_low[0:128])
    gbuf[64:128, 0:64] = dot_nt(pooled_ref[...].astype(BF16), dqkv_low[128:192])
    dpooled = dblock + dot(w_qkv, dqkv_low)

    gb[...] = jnp.zeros_like(gb)
    gb[0:16, 0:C1] = dot_nt(centre_low, (-dpooled).astype(BF16))
    dscaled = dpooled * rsum_ref[...]

    def pool_back(k, carry):
        dpin = (pin[k] * dscaled).astype(BF16)
        joined = cat[k]
        dstem = jnp.where(joined[16:48].astype(F32) > 0, dot(w_down_stem, dpin), 0.0).astype(BF16)
        gb[:, 0:96] += dot_nt(joined, jnp.concatenate([dpin, dstem], 0))
        return carry

    lax.fori_loop(0, NEIGH, pool_back, 0, unroll=4)

    left = lanes_of(64, LANES) < 64
    gd_out = gd[64:128, :]
    gbuf[64:128, :] = jnp.where(left, gbuf[64:128, :], gc[64:128, :])
    gbuf[128:160, :] = jnp.where(left[0:32], pltpu.roll(gd_out[0:32], 64, 1), gd_out[32:64])
    base = 160
    pack(gbuf, base, ga, 0, 32, OFF["w_stem"], 6, C0)
    pack(gbuf, base, gb, 0, 64, OFF["w_stem"], 6, C0)
    pack(gbuf, base, ga, 7, 32, OFF["b_stem"], 1, C0)
    pack(gbuf, base, gb, 7, 64, OFF["b_stem"], 1, C0)
    pack(gbuf, base, gb, 0, 0, OFF["w_down"], 3, C1)
    pack(gbuf, base, gb, 16, 0, OFF["w_down"] + 3 * C1, C0, C1)
    pack(gbuf, base, gb, 7, 0, OFF["b_down"], 1, C1)
    pack(gbuf, base, gc, 136, 0, OFF["w_pos"], 3, C1)
    pack(gbuf, base, gc, 143, 0, OFF["b_pos"], 1, C1)
    pack(gbuf, base, ge, 0, 0, OFF["w_att1"], C1, GROUPS)
    pack(gbuf, base, ge, 143, 0, OFF["b_att1"], 1, GROUPS)
    pack(gbuf, base, ge, 128, 8, OFF["w_att2"], GROUPS, GROUPS)
    pack(gbuf, base, ge, 143, 8, OFF["b_att2"], 1, GROUPS)
    pack(gbuf, base, gd, 0, 0, OFF["w_up"], C1, C0)
    pack(gbuf, base, gd, 128, 0, OFF["b_up"], 1, C0)
    pack(gbuf, base, ga, 16, 0, OFF["w_skip"], C0, C0)
    pack(gbuf, base, ga, 48, 64, OFF["w_head"], C0, NCLS)
    pack(gbuf, base, ga, 7, 64, OFF["b_head"], 1, NCLS)
    loss_sum = jnp.sum(loss, axis=1, keepdims=True)
    line, lane = divmod(FLAT, LANES)
    at_loss = lanes_of(1, LANES) == lane
    gbuf[base + line : base + line + 1, :] += jnp.where(at_loss, loss_sum, 0.0)

    rows = gbuf.shape[0] // n_sub
    shards = rows // 8
    give_grad = sibling(5, gbuf.at[pl.ds(pl.multiple_of((1 - sub) * rows, rows), rows)], gsib)
    give_grad.start()
    give_grad.wait_recv()
    ghalf[...] = gbuf[pl.ds(pl.multiple_of(sub * rows, rows), rows), :] + gsib[...]
    mine_at = pl.multiple_of(sub * rows + me * 8, 8)

    def shard_copy(peer, index):
        return pltpu.make_async_remote_copy(
            src_ref=ghalf.at[pl.ds(pl.multiple_of(peer * 8, 8), 8)],
            dst_ref=gsh.at[index],
            send_sem=red_send.at[peer],
            recv_sem=red_recv.at[index],
            device_id={"pts": peer},
            device_id_type=MESH,
        )

    def sum_copy(peer, index):
        at = pl.multiple_of(sub * rows + index * 8, 8)
        return pltpu.make_async_remote_copy(
            src_ref=gfull.at[pl.ds(at, 8)],
            dst_ref=gfull.at[pl.ds(at, 8)],
            send_sem=gat_send.at[peer],
            recv_sem=gat_recv.at[index],
            device_id={"pts": peer},
            device_id_type=MESH,
        )

    holds = None if n_pts <= shards else me < shards

    def when(condition, run):
        if condition is None:
            run()
        else:
            pl.when(condition)(run)

    def each_peer(run, limited):
        def body(step, carry):
            peer = lax.rem(me + step, n_pts)
            when(None if holds is None or not limited else peer < shards, lambda: run(peer))
            return carry

        lax.fori_loop(1, n_pts, body, 0)

    each_peer(lambda peer: shard_copy(peer, me).start(), True)

    def reduce():
        gsh[me] = ghalf[pl.ds(pl.multiple_of(me * 8, 8), 8), :]
        each_peer(lambda peer: shard_copy(peer, peer).wait_recv(), False)
        gfull[pl.ds(mine_at, 8), :] = jnp.sum(gsh[...], axis=0)
        each_peer(lambda peer: sum_copy(peer, me).start(), False)

    when(holds, reduce)
    each_peer(lambda peer: sum_copy(peer, peer).wait_recv(), True)
    half_rows = gfull.at[pl.ds(pl.multiple_of(sub * rows, rows), rows)]
    give_full = sibling(6, half_rows, half_rows)
    give_full.start()

    each_peer(lambda peer: block_copy(peer, me).wait_send(), False)
    each_peer(lambda peer: mat_copy(peer, me).wait_send(), False)
    each_peer(lambda peer: shard_copy(peer, me).wait_send(), True)
    when(holds, lambda: each_peer(lambda peer: sum_copy(peer, me).wait_send(), False))
    for copy in (forward, give_pooled, give_block, give_dup, give_dkv, give_grad, give_full):
        copy.wait_send()
    give_full.wait_recv()
    out_ref[...] = gfull[...]


def orthonormal_pair(matrix, width=8):
    size = matrix.shape[0]
    left = lanes_of(size, 2 * size) < size
    column = lanes_of(1, 2 * size)
    left_row = column < size
    place_row = jnp.where(left_row, column, column - size)

    def spread(values, halves, at):
        return jnp.where(halves, values[:, at : at + 1], values[:, size + at : size + at + 1])

    for repeat in range(2):
        for first in range(0, size, width):
            span = range(width)
            pivots = [spread(matrix, left, first + i) for i in span]
            products = [jnp.sum(pivot * matrix, axis=0, keepdims=True) for pivot in pivots]
            gram = [
                [spread(products[i], left_row, first + l) if l >= i else None for l in span]
                for i in span
            ]
            taken = 0.0
            for i in span:
                inverse = 1.0 / gram[i][i]
                for l in range(i + 1, width):
                    part = gram[i][l] * inverse
                    pivots[l] = pivots[l] - part * pivots[i]
                    products[l] = products[l] - part * products[i]
                    for m in range(l, width):
                        gram[l][m] = gram[l][m] - part * gram[i][m]
                factor = jnp.where(place_row > first + i, products[i] * inverse, 0.0)
                taken = taken + pivots[i] * factor
            matrix = matrix - taken
        matrix = matrix * lax.rsqrt(jnp.sum(matrix * matrix, axis=0, keepdims=True))
    return matrix


def soap_kernel(
    grads_ref,
    owner_ref,
    step_ref,
    weight_ref,
    first_ref,
    second_ref,
    left_ref,
    right_ref,
    basis_l_ref,
    basis_r_ref,
    average_ref,
    weight_out,
    first_out,
    second_out,
    left_out,
    right_out,
    basis_l_out,
    basis_r_out,
    average_out,
    flat_out,
    scalars_out,
):
    me = lax.axis_index("pts")
    grads = grads_ref[...]
    line, lane = divmod(FLAT, LANES)
    place_row = rows_of(256, LANES)
    at_loss = (place_row == 160 + line) & (lanes_of(256, LANES) == lane)
    loss = jnp.sum(jnp.where(at_loss, grads, 0.0))
    cleaned = jnp.where(at_loss, 0.0, grads)
    squares = jnp.sum(jnp.sum(cleaned * cleaned, axis=0, keepdims=True), axis=1, keepdims=True)
    norm = jnp.sqrt(squares)
    factor = jnp.minimum(1.0, CLIP_NORM / norm)
    flat_out[...] = cleaned[160:216] * factor
    at = lanes_of(8, LANES)
    scalars_out[...] = jnp.where(at == 0, loss, jnp.where(at == 1, norm, 0.0))
    folded = cleaned[128:160]
    stacked = [
        cleaned[0:64, 0:64],
        cleaned[0:64, 64:128],
        cleaned[64:128, 0:64],
        cleaned[64:128, 64:128],
        jnp.concatenate([folded[:, 0:64], folded[:, 64:128]], 0),
    ]
    grad = jnp.zeros((C1, C1), F32)
    owned = 0.0
    for position in range(NMATS):
        flag = jnp.where(owner_ref[position] == me, 1.0, 0.0)
        grad = grad + flag * stacked[position]
        owned = owned + flag
    grad = grad * factor
    count = jnp.full((1, 1), step_ref[0].astype(F32), F32)
    one_scale = 1.0 - jnp.exp(count * math.log(BETA_ONE))
    two_scale = 1.0 - jnp.exp(count * math.log(BETA_TWO))
    basis_l = basis_l_ref[...]
    basis_r = basis_r_ref[...]
    left_new = BETA_TWO * left_ref[...] + (1.0 - BETA_TWO) * exact(grad, grad, ((1,), (1,)))
    right_new = BETA_TWO * right_ref[...] + (1.0 - BETA_TWO) * exact(grad, grad, ((0,), (0,)))
    both = orthonormal_pair(
        jnp.concatenate([exact(left_new, basis_l), exact(right_new, basis_r)], 1)
    )
    basis_l_new = both[:, 0:C1]
    basis_r_new = both[:, C1 : 2 * C1]
    rotated = exact(exact(basis_l, grad, ((0,), (0,))), basis_r)
    first_new = BETA_ONE * first_ref[...] + (1.0 - BETA_ONE) * rotated
    second_new = BETA_TWO * second_ref[...] + (1.0 - BETA_TWO) * rotated * rotated
    scaled = first_new / one_scale / (jnp.sqrt(second_new / two_scale) + ADAM_EPS)
    weight = weight_ref[...]
    weight_new = weight - LEARN_RATE * (
        exact(exact(basis_l, scaled), basis_r, ((1,), (1,))) + WEIGHT_DECAY * weight
    )
    plain = exact(exact(basis_l, first_new), basis_r, ((1,), (1,)))
    first_rotated = exact(exact(basis_l_new, plain, ((0,), (0,))), basis_r_new)
    average_new = EMA_KEEP * average_ref[...] + (1.0 - EMA_KEEP) * weight_new
    held = owned > 0.5
    weight_out[...] = jnp.where(held, weight_new, 0.0)
    first_out[...] = jnp.where(held, first_rotated, 0.0)
    second_out[...] = jnp.where(held, second_new, 0.0)
    left_out[...] = jnp.where(held, left_new, 0.0)
    right_out[...] = jnp.where(held, right_new, 0.0)
    basis_l_out[...] = jnp.where(held, basis_l_new, 0.0)
    basis_r_out[...] = jnp.where(held, basis_r_new, 0.0)
    average_out[...] = jnp.where(held, average_new, 0.0)


def adam_update(weight, grad, first, second, average, count):
    first_new = BETA_ONE * first + (1.0 - BETA_ONE) * grad
    second_new = BETA_TWO * second + (1.0 - BETA_TWO) * grad * grad
    scaled = (
        first_new
        / (1.0 - BETA_ONE**count)
        / (jnp.sqrt(second_new / (1.0 - BETA_TWO**count)) + ADAM_EPS)
    )
    weight_new = weight - LEARN_RATE * (scaled + WEIGHT_DECAY * weight)
    return (weight_new, first_new, second_new, EMA_KEEP * average + (1.0 - EMA_KEEP) * weight_new)


def local(
    points,
    route,
    labels,
    interp_src,
    pool_nbr,
    sample,
    coarse_nbr,
    owner,
    step,
    flat,
    flat_mom,
    flat_sec,
    flat_ema,
    mats,
    mats_mom,
    mats_sec,
    mats_left,
    mats_right,
    mats_basis_l,
    mats_basis_r,
    mats_ema,
):
    n_pts = lax.axis_size("pts")
    n_sub = lax.axis_size("sub")
    fine = points.shape[0]
    coarse = sample.shape[0]
    cap = n_sub * fine // n_pts
    slots = n_pts * cap
    sources = n_sub * n_pts
    half = coarse // n_sub
    parts = coarse // LOW_B
    my_parts = parts // n_sub
    flat2 = jnp.pad(flat, (0, FLAT_ROWS * LANES - FLAT)).reshape(FLAT_ROWS, LANES)
    vmem = pl.BlockSpec(memory_space=pltpu.VMEM)
    smem = pl.BlockSpec(memory_space=pltpu.SMEM)
    dma = pltpu.SemaphoreType.DMA
    scratch = [
        VMEM((6, fine), BF16),
        VMEM((1, fine), I32),
        VMEM((1, fine), I32),
        VMEM((3, fine), I32),
        VMEM((NEIGH, coarse), I32),
        VMEM((1, coarse), I32),
        VMEM((NEIGH, coarse), I32),
        pltpu.SMEM((NMATS,), I32),
        VMEM((C1, C1), F32),
        VMEM((16, fine), F32),
        VMEM((n_pts * 16, cap), F32),
        VMEM((n_pts, 16, cap), BF16),
        VMEM((sources, 16, cap), BF16),
        VMEM((32, LANES), BF16),
        VMEM((n_pts, 32, LANES), BF16),
        VMEM((sources * 8, cap), BF16),
        VMEM((8, coarse), F32),
        VMEM((NEIGH, C1, half), F32),
        VMEM((NEIGH, 48, half), BF16),
        VMEM((C1, half), F32),
        VMEM((C1, half), F32),
        VMEM((parts, CH, LOW_B), BF16),
        VMEM((parts, CH, LOW_B), BF16),
        VMEM((NEIGH, 144, half), BF16),
        VMEM((NEIGH, LOW_B, half), BF16),
        VMEM((NEIGH, C1, half), F32),
        VMEM((NEIGH, GROUPS, half), F32),
        VMEM((C1, half), F32),
        VMEM((C1, half), F32),
        VMEM((16, slots), F32),
        VMEM((parts, C0, LOW_B), F32),
        VMEM((my_parts, C0, LOW_B), F32),
        VMEM((parts, C1 + 8, LOW_B), F32),
        VMEM((my_parts, C1 + 8, LOW_B), F32),
        VMEM((LANES, LANES), F32),
        VMEM((LANES, LANES), F32),
        VMEM((LANES, LANES), F32),
        VMEM((LANES, LANES), F32),
        VMEM((LANES, LANES), F32),
        VMEM((LANES, LANES), F32),
        VMEM((LANES, LANES), F32),
        VMEM((LANES, LANES), F32),
        VMEM((LANES, LANES), F32),
        VMEM((80, LANES), F32),
        VMEM((48, LANES), F32),
        VMEM((144, LANES), F32),
        VMEM((144, LANES), F32),
        VMEM((144, LANES), F32),
        VMEM((256, LANES), F32),
        VMEM((128, LANES), F32),
        VMEM((128, LANES), F32),
        VMEM((n_pts, 8, LANES), F32),
        VMEM((256, LANES), F32),
        dma((n_pts,)),
        dma((n_pts,)),
        dma((n_pts,)),
        dma((n_pts,)),
        dma((n_pts,)),
        dma((n_pts,)),
        dma((n_pts,)),
        dma((n_pts,)),
        dma((8,)),
        dma((8,)),
        dma((9,)),
    ]
    reduced = pl.pallas_call(
        functools.partial(main_kernel, n_pts, n_sub),
        out_shape=jax.ShapeDtypeStruct((256, LANES), F32),
        in_specs=[pl.BlockSpec(memory_space=pltpu.HBM)] * 9 + [vmem],
        out_specs=vmem,
        scratch_shapes=scratch,
        compiler_params=pltpu.CompilerParams(
            collective_id=0, has_side_effects=True, vmem_limit_bytes=60 * 1024 * 1024
        ),
    )(
        points.T,
        route.reshape(1, fine),
        labels.reshape(1, fine),
        interp_src.T,
        pool_nbr.T,
        sample.reshape(1, coarse),
        coarse_nbr.T,
        owner,
        mats[0],
        flat2,
    )
    square = jax.ShapeDtypeStruct((C1, C1), F32)
    results = pl.pallas_call(
        soap_kernel,
        out_shape=[square] * 8
        + [
            jax.ShapeDtypeStruct((56, LANES), F32),
            jax.ShapeDtypeStruct((8, LANES), F32),
        ],
        in_specs=[vmem] + [smem] * 2 + [vmem] * 8,
        out_specs=[vmem] * 10,
    )(
        reduced,
        owner,
        step,
        mats[0],
        mats_mom[0],
        mats_sec[0],
        mats_left[0],
        mats_right[0],
        mats_basis_l[0],
        mats_basis_r[0],
        mats_ema[0],
    )
    flat_grad = results[8].reshape(-1)[:FLAT]
    count = step[0].astype(F32)
    flat_out = adam_update(flat, flat_grad, flat_mom, flat_sec, flat_ema, count)
    return (results[9][0, 0], results[9][0, 1]) + flat_out + tuple(
        result[None] for result in results[:8]
    )


def solution(mesh):
    placed = (
        P(("pts", "sub"), None),
        P(("pts", "sub")),
        P(("pts", "sub")),
        P(("pts", "sub"), None),
        P("pts", None),
        P("pts"),
        P("pts", None),
        P(),
        P(),
        P(),
        P(),
        P(),
        P(),
    ) + (P("pts", None, None),) * 8
    return jax.shard_map(
        local,
        mesh=mesh,
        in_specs=placed,
        out_specs=(P(),) * 6 + (P("pts", None, None),) * 8,
        check_vma=False,
    )
```

```python
import functools
import math

import jax
import jax.numpy as jnp
from jax import lax
from jax.experimental import pallas as pl
from jax.experimental.pallas import tpu as pltpu
from jax.sharding import PartitionSpec as P

C0 = 32
C1 = 64
NEIGH = 16
NCLS = 13
GROUPS = 8
NMATS = 5

HIGHEST = lax.Precision.HIGHEST
CLIP_NORM = 0.01
BETA_ONE = 0.9
BETA_TWO = 0.95
ADAM_EPS = 1e-08
LEARN_RATE = 0.1
WEIGHT_DECAY = 0.01
EMA_KEEP = 0.9
INTERP_EPS = 0.01

F32 = jnp.float32
BF16 = jnp.bfloat16
I32 = jnp.int32
MESH = pl.DeviceIdType.MESH
VMEM = pltpu.VMEM

LANES = 128
FLAT_ROWS = 64
LOW_B = 256
CH = 80
NEG = -1e30


def offsets():
    shapes = [
        ("w_stem", (6, C0)),
        ("b_stem", (C0,)),
        ("w_down", (3 + C0, C1)),
        ("b_down", (C1,)),
        ("w_pos", (3, C1)),
        ("b_pos", (C1,)),
        ("w_att1", (C1, GROUPS)),
        ("b_att1", (GROUPS,)),
        ("w_att2", (GROUPS, GROUPS)),
        ("b_att2", (GROUPS,)),
        ("w_up", (C1, C0)),
        ("b_up", (C0,)),
        ("w_skip", (C0, C0)),
        ("w_head", (C0, NCLS)),
        ("b_head", (NCLS,)),
    ]
    found = {}
    total = 0
    for name, shape in shapes:
        found[name] = total
        total += math.prod(shape)
    return found, total


OFF, FLAT = offsets()


def dot(left, right):
    return lax.dot_general(left, right, (((1,), (0,)), ((), ())), preferred_element_type=F32)


def dot_nt(left, right):
    return lax.dot_general(left, right, (((1,), (1,)), ((), ())), preferred_element_type=F32)


def exact(left, right, dims=((1,), (0,))):
    return lax.dot_general(
        left, right, (dims, ((), ())), precision=HIGHEST, preferred_element_type=F32
    )


def relu(values):
    return jnp.maximum(values, 0.0)


def rows_of(count, length):
    return lax.broadcasted_iota(I32, (count, length), 0)


def lanes_of(count, length):
    return lax.broadcasted_iota(I32, (count, length), 1)


def onehot(low, count):
    hit = rows_of(count, low.shape[1]) == low
    return jnp.where(hit, 1.0, 0.0).astype(BF16)


def pick(spread, high, parts):
    each = spread.shape[0] // parts
    found = spread[0:each]
    for part in range(1, parts):
        found = jnp.where(high == part, spread[part * each : (part + 1) * each], found)
    return found


def place(values, high, parts):
    return jnp.concatenate(
        [jnp.where(high == part, values, 0.0) for part in range(parts)], 0
    ).astype(BF16)


def unpack(flat_ref, out_ref, offset, rows, width, at):
    stride = LANES // width if LANES % width == 0 else rows
    for first in range(min(stride, rows)):
        count = (rows - first + stride - 1) // stride
        padded = -(-count // 8) * 8
        line, lane = divmod(offset + first * width, LANES)
        values = flat_ref[line : line + padded, :]
        if lane:
            values = pltpu.roll(values, LANES - lane, 1)
        if lane + width > LANES:
            following = pltpu.roll(flat_ref[line + 1 : line + 1 + padded, :], LANES - lane, 1)
            values = jnp.where(lanes_of(padded, LANES) < LANES - lane, values, following)
        values = jnp.where(lanes_of(padded, LANES) < width, values, 0.0)
        if count == 1:
            out_ref[at + first : at + first + 1, :] = values[0:1]
        else:
            out_ref[pl.ds(at + first, count, stride=stride), :] = values[0:count]


def pack(out_ref, base, source_ref, row, lane_from, offset, rows, width):
    stride = LANES // width if LANES % width == 0 else rows
    for first in range(min(stride, rows)):
        count = (rows - first + stride - 1) // stride
        line, lane = divmod(offset + first * width, LANES)
        if count == 1:
            values = source_ref[row + first : row + first + 1, :]
        else:
            values = source_ref[pl.ds(row + first, count, stride=stride), :]
        shift = (lane - lane_from) % LANES
        padded = -(-count // 8) * 8
        if padded != count:
            values = jnp.concatenate([values, jnp.zeros((padded - count, LANES), F32)], 0)
        if shift:
            values = pltpu.roll(values, shift, 1)
        values = values[0:count]
        at = lanes_of(count, LANES)
        here = jnp.where((at >= lane) & (at < lane + width), values, 0.0)
        out_ref[base + line : base + line + count, :] += here
        if lane + width > LANES:
            there = jnp.where(at < lane + width - LANES, values, 0.0)
            out_ref[base + line + 1 : base + line + 1 + count, :] += there


def main_kernel(
    n_pts,
    n_sub,
    pts_hbm,
    route_hbm,
    labels_hbm,
    src_hbm,
    pool_hbm,
    sample_hbm,
    cnbr_hbm,
    owner_hbm,
    mats_hbm,
    flat_ref,
    out_ref,
    pts_ref,
    route_ref,
    labels_ref,
    src_ref,
    pool_ref,
    sample_ref,
    cnbr_ref,
    owner_ref,
    mats_ref,
    data,
    sacc,
    sendb,
    recv,
    matmine,
    matall,
    tabb,
    cen,
    pin,
    cat,
    pooled_ref,
    rsum_ref,
    ctab,
    btab,
    near,
    est,
    gst,
    ohs,
    car,
    sc,
    mixed_ref,
    blk_ref,
    slot,
    fin,
    fgr,
    skp,
    foh,
    fsrc,
    fwt,
    dcp,
    dcr,
    dkp,
    dkr,
    wst,
    wd,
    wp,
    w1,
    w2,
    wu,
    wsk,
    wh,
    bias,
    ga,
    gb,
    gc,
    gd,
    ge,
    gbuf,
    gsib,
    ghalf,
    gsh,
    gfull,
    a2a_send,
    a2a_recv,
    mat_send,
    mat_recv,
    red_send,
    red_recv,
    gat_send,
    gat_recv,
    sib_send,
    sib_recv,
    load_sem,
):
    fine = route_ref.shape[1]
    coarse = sample_ref.shape[1]
    cap = sendb.shape[2]
    slots = n_pts * cap
    half = coarse // n_sub
    edges = NEIGH * half
    sources = n_sub * n_pts
    parts = coarse // LOW_B
    my_parts = parts // n_sub
    shift = cap.bit_length() - 1
    low_shift = LOW_B.bit_length() - 1
    span = 512
    me = lax.axis_index("pts")
    sub = lax.axis_index("sub")
    half_at = pl.multiple_of(sub * half, half)

    far_refs = (pts_hbm, route_hbm, labels_hbm, src_hbm, mats_hbm, sample_hbm, pool_hbm, cnbr_hbm, owner_hbm)
    near_refs = (pts_ref, route_ref, labels_ref, src_ref, mats_ref, sample_ref, pool_ref, cnbr_ref, owner_ref)
    loads = [
        pltpu.make_async_copy(source, target, load_sem.at[number])
        for number, (source, target) in enumerate(zip(far_refs, near_refs))
    ]
    for load in loads:
        load.start()

    barrier = pltpu.get_barrier_semaphore()

    def greet(step, carry):
        peer = lax.rem(me + step, n_pts)
        pl.semaphore_signal(barrier, inc=1, device_id={"pts": peer}, device_id_type=MESH)
        return carry

    lax.fori_loop(1, n_pts, greet, 0)
    pl.semaphore_signal(barrier, inc=1, device_id={"sub": 1 - sub}, device_id_type=MESH)

    def sibling(number, source, target):
        return pltpu.make_async_remote_copy(
            src_ref=source,
            dst_ref=target,
            send_sem=sib_send.at[number],
            recv_sem=sib_recv.at[number],
            device_id={"sub": 1 - sub},
            device_id_type=MESH,
        )

    for load in loads[0:5]:
        load.wait()
    data[0:6, :] = pts_ref[...].astype(F32)
    data[6:8, :] = jnp.zeros((2, fine), F32)
    source_rows = src_ref[...]
    data[8:11, :] = lax.shift_right_logical(source_rows, 5).astype(F32)
    data[11:14, :] = (source_rows & 31).astype(F32)
    data[14:15, :] = (labels_ref[...] + 1).astype(F32)
    data[15:16, :] = jnp.zeros((1, fine), F32)
    sacc[...] = jnp.zeros_like(sacc)
    counts = jnp.zeros((16, 32), F32)
    for chunk in range(fine // span):
        lanes = slice(chunk * span, (chunk + 1) * span)
        route = route_ref[:, lanes]
        high = lax.shift_right_logical(route, shift)
        spread = place(data[:, lanes], high, n_pts)
        sacc[...] += dot_nt(spread, onehot(route & (cap - 1), cap))
        classes = onehot(labels_ref[:, lanes], 16)
        counts = counts + dot_nt(jnp.ones((16, span), BF16), jnp.concatenate([classes, classes], 0))
    count_high = jnp.floor(counts * (1.0 / 128.0))
    count_low = counts - 128.0 * count_high
    digits = jnp.where(lanes_of(16, 32) < 16, count_low, count_high)
    digits = jnp.where(rows_of(16, 32) == 15, digits, 0.0)
    data[:, 0:cap] = jnp.zeros((16, cap), F32)
    data[:, 0:32] = digits
    sendb[...] = (sacc[...].reshape(n_pts, 16, cap) + data[:, 0:cap][None]).astype(BF16)
    matrix = mats_ref[...]
    matmine[...] = jnp.concatenate([matrix[0:32], matrix[32:64]], 1).astype(BF16)

    pl.semaphore_wait(barrier, n_pts)

    def block_copy(peer, index):
        return pltpu.make_async_remote_copy(
            src_ref=sendb.at[peer],
            dst_ref=recv.at[sub * n_pts + index],
            send_sem=a2a_send.at[peer],
            recv_sem=a2a_recv.at[index],
            device_id={"pts": peer},
            device_id_type=MESH,
        )

    def mat_copy(peer, index):
        return pltpu.make_async_remote_copy(
            src_ref=matmine,
            dst_ref=matall.at[index],
            send_sem=mat_send.at[peer],
            recv_sem=mat_recv.at[index],
            device_id={"pts": peer},
            device_id_type=MESH,
        )

    def send_blocks(step, carry):
        block_copy(lax.rem(me + step, n_pts), me).start()
        return carry

    def send_mats(step, carry):
        mat_copy(lax.rem(me + step, n_pts), me).start()
        return carry

    lax.fori_loop(1, n_pts, send_blocks, 0)
    recv[sub * n_pts + me] = sendb[me]
    matall[me] = matmine[...]

    for ref in (wst, wd, wp, w1, w2, wu, wsk, wh, bias):
        ref[...] = jnp.zeros_like(ref)
    unpack(flat_ref, wst, OFF["w_stem"], 6, C0, 0)
    unpack(flat_ref, wd, OFF["w_down"], 3, C1, 0)
    unpack(flat_ref, wd, OFF["w_down"] + 3 * C1, C0, C1, 16)
    unpack(flat_ref, wp, OFF["w_pos"], 3, C1, 8)
    unpack(flat_ref, w1, OFF["w_att1"], C1, GROUPS, 0)
    unpack(flat_ref, w2, OFF["w_att2"], GROUPS, GROUPS, 0)
    unpack(flat_ref, wu, OFF["w_up"], C1, C0, 0)
    unpack(flat_ref, wsk, OFF["w_skip"], C0, C0, 0)
    unpack(flat_ref, wh, OFF["w_head"], C0, NCLS, 0)
    names = ("b_stem", "b_down", "b_pos", "b_att1", "b_att2", "b_up", "b_head")
    widths = (C0, C1, C1, GROUPS, GROUPS, C0, NCLS)
    for position, (name, width) in enumerate(zip(names, widths)):
        unpack(flat_ref, bias, OFF[name], 1, width, position)
    columns = bias[...].T
    b_stem = columns[0:C0, 0:1]
    b_down = columns[0:C1, 1:2]
    b_pos = columns[0:C1, 2:3]
    b_att1 = columns[0:GROUPS, 3:4]
    b_att2 = columns[0:GROUPS, 4:5]
    b_up = columns[0:C0, 5:6]
    b_head = jnp.where(rows_of(16, 1) < NCLS, columns[0:16, 6:7], NEG)
    w_stem_t = wst[...].T[0:C0, 0:16].astype(BF16)
    w_down_t = wd[...].T[0:C1, 0:48].astype(BF16)
    w_pos_t = wp[...].T[0:C1, 0:16].astype(BF16)
    w_att1_t = w1[...].T[0:GROUPS, 0:C1].astype(BF16)
    w_att2_t = w2[...].T[0:GROUPS, 0:16].astype(BF16)
    w_up_t = wu[...].T[0:C0, 0:C1].astype(BF16)
    w_skip_t = wsk[...].T[0:C0, 0:C0].astype(BF16)
    w_head_t = wh[...].T[0:16, 0:C0].astype(BF16)
    w_down_stem = wd[16:48, 0:C1].astype(BF16)
    w_att1 = w1[0:C1, 0:16].astype(BF16)
    w_att2 = w2[0:GROUPS, 0:16].astype(BF16)
    w_up = wu[0:C1, 0:C0].astype(BF16)
    w_skip = wsk[0:C0, 0:C0].astype(BF16)
    w_head = wh[0:C0, 0:16].astype(BF16)

    def wait_blocks(step, carry):
        peer = lax.rem(me + step, n_pts)
        block_copy(peer, peer).wait_recv()
        return carry

    lax.fori_loop(1, n_pts, wait_blocks, 0)
    lax.fori_loop(1, n_pts, send_mats, 0)
    for load in loads[5:]:
        load.wait()
    mine = recv.at[pl.ds(sub * n_pts, n_pts)]
    forward = sibling(0, mine, mine)
    forward.start()
    for source in range(n_pts):
        slot[:, source * cap : (source + 1) * cap] = recv[sub * n_pts + source].astype(F32)
    forward.wait_recv()

    table = recv[...].astype(F32)[:, 0:8, :].reshape(sources * 8, cap)
    ones_row = (rows_of(sources * 8, cap) & 7) == 7
    tabb[...] = jnp.where(ones_row, 1.0, table).astype(BF16)
    count_row = jnp.sum(recv[...].astype(F32)[:, 8:16, :], axis=0)[7:8, 0:32]
    count_at = jnp.broadcast_to(count_row, (16, 32))
    low_hit = lanes_of(16, 32) == rows_of(16, 32)
    high_hit = lanes_of(16, 32) == rows_of(16, 32) + 16
    class_counts = jnp.sum(
        jnp.where(low_hit, count_at, 0.0) + jnp.where(high_hit, 128.0 * count_at, 0.0),
        axis=1,
        keepdims=True,
    )
    total_fine = float(fine * n_pts * n_sub)
    class_w = jnp.where(
        rows_of(16, 1) < NCLS, total_fine / (NCLS * class_counts) * (1.0 / total_fine), 0.0
    )

    def gather_points(index):
        hot = onehot(index & (cap - 1), cap)
        high = jnp.broadcast_to(lax.shift_right_logical(index, shift), (8, index.shape[1]))
        return pick(dot(tabb[...], hot), high, sources)

    zeros8 = jnp.zeros((8, span), F32)
    for chunk in range(coarse // span):
        lanes = slice(chunk * span, (chunk + 1) * span)
        found = gather_points(sample_ref[:, lanes])
        cen[:, lanes] = jnp.where(rows_of(8, span) < 6, found, 0.0)
    centre = cen[:, pl.ds(half_at, half)]
    centre_low = jnp.concatenate([centre, zeros8], 0).astype(BF16)
    w_xyz_t = jnp.where(lanes_of(C1, 16) < 3, wd[...].T[0:C1, 0:16], 0.0).astype(BF16)
    pool_base = b_down - dot(w_xyz_t, centre_low)

    def at_edge(k):
        return pl.ds(pl.multiple_of(k * half, half), half)

    def every_edge(step, unroll):
        def run(k, carry):
            step(k, at_edge(k))
            return carry

        lax.fori_loop(0, NEIGH, run, 0, unroll=unroll)

    def pool_gather(k, lanes):
        found = gather_points(pool_ref[pl.ds(k, 1), pl.ds(half_at, half)])
        cat[0:16, lanes] = jnp.concatenate([found, zeros8], 0).astype(BF16)

    def pool_stem(k, lanes):
        cat[16:48, lanes] = relu(dot(w_stem_t, cat[0:16, lanes]) + b_stem).astype(BF16)

    def pool_project(k, lanes):
        pin[:, lanes] = dot(w_down_t, cat[:, lanes]).astype(BF16).astype(F32) + pool_base

    every_edge(pool_gather, 4)
    every_edge(pool_stem, 16)
    every_edge(pool_project, 16)

    def tree(combine, values):
        while len(values) > 1:
            paired = [combine(values[i], values[i + 1]) for i in range(0, len(values) - 1, 2)]
            values = paired + ([values[-1]] if len(values) % 2 else [])
        return values[0]

    wide = 256

    def log_sum(r, carry):
        rows = pl.ds(pl.multiple_of(r * 8, 8), 8)
        for start in range(0, half, wide):
            spots = [slice(k * half + start, k * half + start + wide) for k in range(NEIGH)]
            values = [pin[rows, spot] for spot in spots]
            most = tree(jnp.maximum, values)
            values = [jnp.exp(value - most) for value in values]
            for spot, value in zip(spots, values):
                pin[rows, spot] = value
            total = tree(jnp.add, values)
            pooled_ref[rows, start : start + wide] = most + jnp.log(total)
            rsum_ref[rows, start : start + wide] = 1.0 / total
        return carry

    lax.fori_loop(0, C1 // 8, log_sum, 0, unroll=2)

    def table_rows(values, target):
        for part in range(my_parts):
            lanes = slice(part * LOW_B, (part + 1) * LOW_B)
            stacked = jnp.concatenate(
                [values[:, lanes], centre[:, lanes], jnp.zeros((8, LOW_B), F32)], 0
            )
            target[sub * my_parts + part] = stacked.astype(BF16)

    table_rows(pooled_ref[...], ctab)
    my_ctab = ctab.at[pl.ds(sub * my_parts, my_parts)]
    give_pooled = sibling(1, my_ctab, my_ctab)
    give_pooled.start()

    def wait_mats(step, carry):
        peer = lax.rem(me + step, n_pts)
        mat_copy(peer, peer).wait_recv()
        return carry

    lax.fori_loop(1, n_pts, wait_mats, 0)

    def layer(position):
        folded = matall[owner_ref[position]].astype(F32)
        return jnp.concatenate([folded[:, 0:C1], folded[:, C1 : 2 * C1]], 0)

    w_query, w_key, w_value, w_pos2_32, w_out_32 = [layer(position) for position in range(NMATS)]
    w_qkv = jnp.concatenate([w_query, w_key, w_value], 1).astype(BF16)
    w_query_t = w_query.T.astype(BF16)
    w_pos2 = w_pos2_32.astype(BF16)
    w_pos2_t = w_pos2_32.T
    w_edge_t = jnp.concatenate(
        [
            jnp.concatenate([-w_key.T, w_pos2_t], 1),
            jnp.concatenate([w_value.T, w_pos2_t], 1),
        ],
        0,
    ).astype(BF16)
    w_out = w_out_32.astype(BF16)
    w_out_t = w_out_32.T.astype(BF16)
    queries = dot(w_query_t, pooled_ref[...].astype(BF16))

    def at_slot(step):
        return pl.ds(pl.multiple_of(step * span, span), span)

    def every_slot(step, unroll):
        def run(j, carry):
            step(j, at_slot(j))
            return carry

        lax.fori_loop(0, slots // span, run, 0, unroll=unroll)

    def fine_points(j, lanes):
        ones = jnp.where(rows_of(8, span) == 7, 1.0, slot[0:8, lanes])
        fin[0:16, lanes] = jnp.concatenate([ones, zeros8], 0).astype(BF16)

    def fine_stem(j, lanes):
        fin[16:48, lanes] = relu(dot(w_stem_t, fin[0:16, lanes]) + b_stem).astype(BF16)

    def fine_skip(j, lanes):
        skp[:, lanes] = dot(w_skip_t, fin[16:48, lanes])

    every_slot(fine_points, 4)
    every_slot(fine_stem, 8)
    every_slot(fine_skip, 8)
    give_pooled.wait_recv()

    def attend_gather(k, lanes):
        index = cnbr_ref[pl.ds(k, 1), pl.ds(half_at, half)]
        hot = onehot(index & (LOW_B - 1), LOW_B)
        ohs[:, lanes] = hot
        high = lax.shift_right_logical(index, low_shift)
        found = pick(dot(ctab[...].reshape(parts * CH, LOW_B), hot), high, parts)
        near[:, lanes] = found[0:C1].astype(BF16)
        offset = jnp.where(rows_of(8, half) == 7, 1.0, centre - found[C1 : C1 + 8])
        est[128:144, lanes] = jnp.concatenate([zeros8, offset], 0).astype(BF16)

    def attend_pos(k, lanes):
        est[64:128, lanes] = relu(dot(w_pos_t, est[128:144, lanes]) + b_pos).astype(BF16)

    def attend_edge(k, lanes):
        both = dot(w_edge_t, jnp.concatenate([near[:, lanes], est[64:128, lanes]], 0))
        est[0:64, lanes] = (queries + both[0:C1]).astype(BF16)
        car[:, lanes] = both[C1 : 2 * C1]

    def attend_act(k, lanes):
        act = relu(dot(w_att1_t, est[0:64, lanes]) + b_att1)
        offset = est[128:144, lanes].astype(F32)[8:16]
        est[128:144, lanes] = jnp.concatenate([act, offset], 0).astype(BF16)

    def attend_score(k, lanes):
        sc[:, lanes] = dot(w_att2_t, est[128:144, lanes]) + b_att2

    every_edge(attend_gather, 4)
    every_edge(attend_pos, 16)
    every_edge(attend_edge, 16)
    every_edge(attend_act, 16)
    every_edge(attend_score, 16)

    for start in range(0, half, wide):
        spots = [slice(k * half + start, k * half + start + wide) for k in range(NEIGH)]
        values = [sc[:, spot] for spot in spots]
        most = tree(jnp.maximum, values)
        values = [jnp.exp(value - most) for value in values]
        scale = 1.0 / tree(jnp.add, values)
        for spot, value in zip(spots, values):
            sc[:, spot] = value * scale

    for g in range(GROUPS):
        rows = slice(8 * g, 8 * g + 8)
        for start in range(0, half, wide):
            spots = [slice(k * half + start, k * half + start + wide) for k in range(NEIGH)]
            terms = [
                jnp.broadcast_to(sc[g : g + 1, spot], (8, wide)) * car[rows, spot]
                for spot in spots
            ]
            mixed_ref[rows, start : start + wide] = tree(jnp.add, terms)

    block = pooled_ref[...] + dot(w_out_t, mixed_ref[...].astype(BF16))
    blk_ref[...] = block
    table_rows(block, btab)
    my_btab = btab.at[pl.ds(sub * my_parts, my_parts)]
    give_block = sibling(2, my_btab, my_btab)
    give_block.start()

    def source_of(lanes, i):
        index = (32.0 * slot[8 + i : 9 + i, lanes] + slot[11 + i : 12 + i, lanes]).astype(I32)
        return index & (LOW_B - 1), lax.shift_right_logical(index, low_shift)

    def fine_hot(j, lanes):
        for i in range(3):
            foh[i, :, lanes] = onehot(source_of(lanes, i)[0], LOW_B)

    every_slot(fine_hot, 2)
    give_block.wait_recv()

    def fine_gather(j, lanes):
        points = slot[0:8, lanes]
        inverses = []
        for i in range(3):
            high = source_of(lanes, i)[1]
            found = pick(dot(btab[...].reshape(parts * CH, LOW_B), foh[i, :, lanes]), high, parts)
            fsrc[i, :, lanes] = found[0:C1].astype(BF16)
            diff = jnp.where(rows_of(8, span) < 3, points - found[C1 : C1 + 8], 0.0)
            inverses.append(1.0 / (jnp.sum(diff * diff, axis=0, keepdims=True) + INTERP_EPS))
        norm = 1.0 / (inverses[0] + inverses[1] + inverses[2])
        for i in range(3):
            fwt[i : i + 1, lanes] = inverses[i] * norm

    def fine_join(j, lanes):
        terms = [fwt[i : i + 1, lanes] * dot(w_up_t, fsrc[i, :, lanes]) for i in range(3)]
        interp = (terms[0] + terms[1] + terms[2] + b_up).astype(BF16).astype(F32)
        fin[48:80, lanes] = relu(interp + skp[:, lanes]).astype(BF16)

    def fine_loss(j, loss):
        lanes = at_slot(j)
        logits = dot(w_head_t, fin[48:80, lanes]) + b_head
        label = slot[14:15, lanes].astype(I32)
        hit = jnp.where(rows_of(16, span) + 1 == label, 1.0, 0.0)
        row_w = jnp.sum(hit * class_w, axis=0, keepdims=True)
        peak = jnp.max(logits, axis=0, keepdims=True)
        raised = jnp.exp(logits - peak)
        total = jnp.sum(raised, axis=0, keepdims=True)
        named = jnp.sum(hit * logits, axis=0, keepdims=True)
        fgr[64:80, lanes] = (row_w * (raised * (1.0 / total) - hit)).astype(BF16)
        return loss + row_w * (peak + jnp.log(total) - named)

    def fine_fused(j, lanes):
        kept = fin[48:80, lanes].astype(F32) > 0
        fgr[0:32, lanes] = jnp.where(kept, dot(w_head, fgr[64:80, lanes]), 0.0).astype(BF16)

    def fine_scatter(j, lanes):
        dfused = fgr[0:32, lanes].astype(F32)
        total = 0.0
        for i in range(3):
            spread = place(fwt[i : i + 1, lanes] * dfused, source_of(lanes, i)[1], parts)
            total = total + dot_nt(spread, foh[i, :, lanes])
        dcp[...] += total.reshape(parts, C0, LOW_B)

    def fine_back(j, lanes):
        kept = fin[16:48, lanes].astype(F32) > 0
        fgr[32:64, lanes] = jnp.where(kept, dot(w_skip, fgr[0:32, lanes]), 0.0).astype(BF16)

    every_slot(fine_gather, 8)
    every_slot(fine_join, 8)
    loss = lax.fori_loop(0, slots // span, fine_loss, jnp.zeros((1, span), F32), unroll=4)
    every_slot(fine_fused, 8)
    dcp[...] = jnp.zeros_like(dcp)
    every_slot(fine_scatter, 2)

    other = (1 - sub) * my_parts
    own = sub * my_parts
    give_dup = sibling(3, dcp.at[pl.ds(other, my_parts)], dcr)
    give_dup.start()
    every_slot(fine_back, 8)
    ga[...] = jnp.zeros_like(ga)
    for start in range(0, slots, 4 * span):
        lanes = slice(start, start + 4 * span)
        ga[:, 0:80] += dot_nt(fin[:, lanes], fgr[:, lanes])
    give_dup.wait_recv()

    def own_half(partial, received):
        return jnp.concatenate(
            [partial[own + part] + received[part] for part in range(my_parts)], 1
        )

    dup_low = own_half(dcp, dcr).astype(BF16)
    dblock = dot(w_up, dup_low)
    dbranch_low = dblock.astype(BF16)
    dmixed = dot(w_out, dbranch_low)

    def group_sum(values):
        return jnp.concatenate(
            [
                jnp.sum(values[8 * g : 8 * g + 8], axis=0, keepdims=True)
                for g in range(GROUPS)
            ],
            0,
        )

    def expand(values):
        return jnp.concatenate(
            [jnp.broadcast_to(values[g : g + 1], (8, values.shape[1])) for g in range(GROUPS)], 0
        )

    centred = group_sum(dmixed * mixed_ref[...])

    def back_score(k, lanes):
        ds2 = sc[:, lanes] * (group_sum(dmixed * car[:, lanes]) - centred)
        gst[128:144, lanes] = jnp.concatenate([ds2, zeros8], 0).astype(BF16)

    def back_act(k, lanes):
        scores = gst[128:144, lanes]
        kept = est[128:144, lanes].astype(F32)[0:8] > 0
        ds1 = jnp.where(kept, dot(w_att2, scores), 0.0)
        ds2 = scores.astype(F32)[0:8]
        gst[128:144, lanes] = jnp.concatenate([ds1, ds2], 0).astype(BF16)

    def back_edge(k, lanes):
        small = gst[128:144, lanes]
        dcarried = expand(sc[:, lanes]) * dmixed
        gst[64:128, lanes] = (dot(w_att1, small) + dcarried).astype(BF16)
        index = cnbr_ref[pl.ds(k, 1), pl.ds(half_at, half)]
        high = lax.shift_right_logical(index, low_shift)
        spread = place(jnp.concatenate([dcarried, small.astype(F32)[0:8]], 0), high, parts)
        dkp[...] += dot_nt(spread, ohs[:, lanes]).reshape(parts, C1 + 8, LOW_B)

    def back_pos(k, lanes):
        kept = est[64:128, lanes].astype(F32) > 0
        gst[0:64, lanes] = jnp.where(kept, dot(w_pos2, gst[64:128, lanes]), 0.0).astype(BF16)

    every_edge(back_score, 16)
    every_edge(back_act, 16)
    dkp[...] = jnp.zeros_like(dkp)
    every_edge(back_edge, 16)
    give_dkv = sibling(4, dkp.at[pl.ds(other, my_parts)], dkr)
    give_dkv.start()
    every_edge(back_pos, 16)
    inputs = jnp.concatenate(
        [blk_ref[...].astype(BF16), mixed_ref[...].astype(BF16), jnp.ones((16, half), BF16)], 0
    )
    grads = jnp.concatenate([dup_low, jnp.zeros((C0, half), BF16), dbranch_low], 0)
    gd[...] = dot_nt(inputs, grads)
    gc[...] = jnp.zeros_like(gc)
    ge[...] = jnp.zeros_like(ge)
    for start in range(0, edges, 4 * span):
        lanes = slice(start, start + 4 * span)
        result = dot_nt(est[:, lanes], gst[:, lanes])
        gc[...] += result[:, 0:128]
        ge[:, 0:16] += result[:, 128:144]
    ds1_total = tree(
        jnp.add,
        [gst[128:144, k * half : (k + 1) * half].astype(F32)[0:8] for k in range(NEIGH)],
    )
    w_att1_exact = w1[0:C1, 0:16].astype(BF16).astype(F32)[:, 0:8]
    dqueries = exact(w_att1_exact, ds1_total)
    give_dkv.wait_recv()
    dkv = own_half(dkp, dkr)
    dkeys = -exact(w_att1_exact, dkv[C1 : C1 + 8])
    dqkv_low = jnp.concatenate([dqueries, dkeys, dkv[0:C1]], 0).astype(BF16)
    gbuf[...] = jnp.zeros_like(gbuf)
    gbuf[0:64, :] = dot_nt(pooled_ref[...].astype(BF16), dqkv_low[0:128])
    gbuf[64:128, 0:64] = dot_nt(pooled_ref[...].astype(BF16), dqkv_low[128:192])
    dpooled = dblock + dot(w_qkv, dqkv_low)

    gb[...] = jnp.zeros_like(gb)
    gb[0:16, 0:C1] = dot_nt(centre_low, (-dpooled).astype(BF16))
    dscaled = dpooled * rsum_ref[...]

    def pool_back(k, lanes):
        dpin = (pin[:, lanes] * dscaled).astype(BF16)
        gst[0:64, lanes] = dpin
        kept = cat[16:48, lanes].astype(F32) > 0
        gst[64:96, lanes] = jnp.where(kept, dot(w_down_stem, dpin), 0.0).astype(BF16)

    every_edge(pool_back, 16)
    for start in range(0, edges, 4 * span):
        lanes = slice(start, start + 4 * span)
        gb[:, 0:96] += dot_nt(cat[:, lanes], gst[0:96, lanes])

    left = lanes_of(64, LANES) < 64
    gd_out = gd[64:128, :]
    gbuf[64:128, :] = jnp.where(left, gbuf[64:128, :], gc[64:128, :])
    gbuf[128:160, :] = jnp.where(left[0:32], pltpu.roll(gd_out[0:32], 64, 1), gd_out[32:64])
    base = 160
    pack(gbuf, base, ga, 0, 32, OFF["w_stem"], 6, C0)
    pack(gbuf, base, gb, 0, 64, OFF["w_stem"], 6, C0)
    pack(gbuf, base, ga, 7, 32, OFF["b_stem"], 1, C0)
    pack(gbuf, base, gb, 7, 64, OFF["b_stem"], 1, C0)
    pack(gbuf, base, gb, 0, 0, OFF["w_down"], 3, C1)
    pack(gbuf, base, gb, 16, 0, OFF["w_down"] + 3 * C1, C0, C1)
    pack(gbuf, base, gb, 7, 0, OFF["b_down"], 1, C1)
    pack(gbuf, base, gc, 136, 0, OFF["w_pos"], 3, C1)
    pack(gbuf, base, gc, 143, 0, OFF["b_pos"], 1, C1)
    pack(gbuf, base, ge, 0, 0, OFF["w_att1"], C1, GROUPS)
    pack(gbuf, base, ge, 143, 0, OFF["b_att1"], 1, GROUPS)
    pack(gbuf, base, ge, 128, 8, OFF["w_att2"], GROUPS, GROUPS)
    pack(gbuf, base, ge, 143, 8, OFF["b_att2"], 1, GROUPS)
    pack(gbuf, base, gd, 0, 0, OFF["w_up"], C1, C0)
    pack(gbuf, base, gd, 128, 0, OFF["b_up"], 1, C0)
    pack(gbuf, base, ga, 16, 0, OFF["w_skip"], C0, C0)
    pack(gbuf, base, ga, 48, 64, OFF["w_head"], C0, NCLS)
    pack(gbuf, base, ga, 7, 64, OFF["b_head"], 1, NCLS)
    loss_sum = jnp.sum(loss, axis=1, keepdims=True)
    line, lane = divmod(FLAT, LANES)
    at_loss = lanes_of(1, LANES) == lane
    gbuf[base + line : base + line + 1, :] += jnp.where(at_loss, loss_sum, 0.0)

    rows = gbuf.shape[0] // n_sub
    shards = rows // 8
    give_grad = sibling(5, gbuf.at[pl.ds(pl.multiple_of((1 - sub) * rows, rows), rows)], gsib)
    give_grad.start()
    give_grad.wait_recv()
    ghalf[...] = gbuf[pl.ds(pl.multiple_of(sub * rows, rows), rows), :] + gsib[...]
    mine_at = pl.multiple_of(sub * rows + me * 8, 8)

    def shard_copy(peer, index):
        return pltpu.make_async_remote_copy(
            src_ref=ghalf.at[pl.ds(pl.multiple_of(peer * 8, 8), 8)],
            dst_ref=gsh.at[index],
            send_sem=red_send.at[peer],
            recv_sem=red_recv.at[index],
            device_id={"pts": peer},
            device_id_type=MESH,
        )

    def sum_copy(peer, index):
        at = pl.multiple_of(sub * rows + index * 8, 8)
        return pltpu.make_async_remote_copy(
            src_ref=gfull.at[pl.ds(at, 8)],
            dst_ref=gfull.at[pl.ds(at, 8)],
            send_sem=gat_send.at[peer],
            recv_sem=gat_recv.at[index],
            device_id={"pts": peer},
            device_id_type=MESH,
        )

    holds = None if n_pts <= shards else me < shards

    def when(condition, run):
        if condition is None:
            run()
        else:
            pl.when(condition)(run)

    def each_peer(run, limited):
        def body(step, carry):
            peer = lax.rem(me + step, n_pts)
            when(None if holds is None or not limited else peer < shards, lambda: run(peer))
            return carry

        lax.fori_loop(1, n_pts, body, 0)

    each_peer(lambda peer: shard_copy(peer, me).start(), True)

    def reduce():
        gsh[me] = ghalf[pl.ds(pl.multiple_of(me * 8, 8), 8), :]
        each_peer(lambda peer: shard_copy(peer, peer).wait_recv(), False)
        gfull[pl.ds(mine_at, 8), :] = jnp.sum(gsh[...], axis=0)
        each_peer(lambda peer: sum_copy(peer, me).start(), False)

    when(holds, reduce)
    each_peer(lambda peer: sum_copy(peer, peer).wait_recv(), True)
    half_rows = gfull.at[pl.ds(pl.multiple_of(sub * rows, rows), rows)]
    give_full = sibling(6, half_rows, half_rows)
    give_full.start()

    each_peer(lambda peer: block_copy(peer, me).wait_send(), False)
    each_peer(lambda peer: mat_copy(peer, me).wait_send(), False)
    each_peer(lambda peer: shard_copy(peer, me).wait_send(), True)
    when(holds, lambda: each_peer(lambda peer: sum_copy(peer, me).wait_send(), False))
    for copy in (forward, give_pooled, give_block, give_dup, give_dkv, give_grad, give_full):
        copy.wait_send()
    give_full.wait_recv()
    out_ref[...] = gfull[...]


def orthonormal_pair(matrix, width=8):
    size = matrix.shape[0]
    left = lanes_of(size, 2 * size) < size
    column = lanes_of(1, 2 * size)
    left_row = column < size
    place_row = jnp.where(left_row, column, column - size)

    def spread(values, halves, at):
        return jnp.where(halves, values[:, at : at + 1], values[:, size + at : size + at + 1])

    for repeat in range(2):
        for first in range(0, size, width):
            span = range(width)
            pivots = [spread(matrix, left, first + i) for i in span]
            products = [jnp.sum(pivot * matrix, axis=0, keepdims=True) for pivot in pivots]
            gram = [
                [spread(products[i], left_row, first + l) if l >= i else None for l in span]
                for i in span
            ]
            taken = 0.0
            for i in span:
                inverse = 1.0 / gram[i][i]
                for l in range(i + 1, width):
                    part = gram[i][l] * inverse
                    pivots[l] = pivots[l] - part * pivots[i]
                    products[l] = products[l] - part * products[i]
                    for m in range(l, width):
                        gram[l][m] = gram[l][m] - part * gram[i][m]
                factor = jnp.where(place_row > first + i, products[i] * inverse, 0.0)
                taken = taken + pivots[i] * factor
            matrix = matrix - taken
        matrix = matrix * lax.rsqrt(jnp.sum(matrix * matrix, axis=0, keepdims=True))
    return matrix


def soap_kernel(
    grads_ref,
    owner_ref,
    step_ref,
    weight_ref,
    first_ref,
    second_ref,
    left_ref,
    right_ref,
    basis_l_ref,
    basis_r_ref,
    average_ref,
    weight_out,
    first_out,
    second_out,
    left_out,
    right_out,
    basis_l_out,
    basis_r_out,
    average_out,
    flat_out,
    scalars_out,
):
    me = lax.axis_index("pts")
    grads = grads_ref[...]
    line, lane = divmod(FLAT, LANES)
    place_row = rows_of(256, LANES)
    at_loss = (place_row == 160 + line) & (lanes_of(256, LANES) == lane)
    loss = jnp.sum(jnp.where(at_loss, grads, 0.0))
    cleaned = jnp.where(at_loss, 0.0, grads)
    squares = jnp.sum(jnp.sum(cleaned * cleaned, axis=0, keepdims=True), axis=1, keepdims=True)
    norm = jnp.sqrt(squares)
    factor = jnp.minimum(1.0, CLIP_NORM / norm)
    flat_out[...] = cleaned[160:216] * factor
    at = lanes_of(8, LANES)
    scalars_out[...] = jnp.where(at == 0, loss, jnp.where(at == 1, norm, 0.0))
    folded = cleaned[128:160]
    stacked = [
        cleaned[0:64, 0:64],
        cleaned[0:64, 64:128],
        cleaned[64:128, 0:64],
        cleaned[64:128, 64:128],
        jnp.concatenate([folded[:, 0:64], folded[:, 64:128]], 0),
    ]
    grad = jnp.zeros((C1, C1), F32)
    owned = 0.0
    for position in range(NMATS):
        flag = jnp.where(owner_ref[position] == me, 1.0, 0.0)
        grad = grad + flag * stacked[position]
        owned = owned + flag
    grad = grad * factor
    count = jnp.full((1, 1), step_ref[0].astype(F32), F32)
    one_scale = 1.0 - jnp.exp(count * math.log(BETA_ONE))
    two_scale = 1.0 - jnp.exp(count * math.log(BETA_TWO))
    basis_l = basis_l_ref[...]
    basis_r = basis_r_ref[...]
    left_new = BETA_TWO * left_ref[...] + (1.0 - BETA_TWO) * exact(grad, grad, ((1,), (1,)))
    right_new = BETA_TWO * right_ref[...] + (1.0 - BETA_TWO) * exact(grad, grad, ((0,), (0,)))
    both = orthonormal_pair(
        jnp.concatenate([exact(left_new, basis_l), exact(right_new, basis_r)], 1)
    )
    basis_l_new = both[:, 0:C1]
    basis_r_new = both[:, C1 : 2 * C1]
    rotated = exact(exact(basis_l, grad, ((0,), (0,))), basis_r)
    first_new = BETA_ONE * first_ref[...] + (1.0 - BETA_ONE) * rotated
    second_new = BETA_TWO * second_ref[...] + (1.0 - BETA_TWO) * rotated * rotated
    scaled = first_new / one_scale / (jnp.sqrt(second_new / two_scale) + ADAM_EPS)
    weight = weight_ref[...]
    weight_new = weight - LEARN_RATE * (
        exact(exact(basis_l, scaled), basis_r, ((1,), (1,))) + WEIGHT_DECAY * weight
    )
    plain = exact(exact(basis_l, first_new), basis_r, ((1,), (1,)))
    first_rotated = exact(exact(basis_l_new, plain, ((0,), (0,))), basis_r_new)
    average_new = EMA_KEEP * average_ref[...] + (1.0 - EMA_KEEP) * weight_new
    held = owned > 0.5
    weight_out[...] = jnp.where(held, weight_new, 0.0)
    first_out[...] = jnp.where(held, first_rotated, 0.0)
    second_out[...] = jnp.where(held, second_new, 0.0)
    left_out[...] = jnp.where(held, left_new, 0.0)
    right_out[...] = jnp.where(held, right_new, 0.0)
    basis_l_out[...] = jnp.where(held, basis_l_new, 0.0)
    basis_r_out[...] = jnp.where(held, basis_r_new, 0.0)
    average_out[...] = jnp.where(held, average_new, 0.0)


def adam_update(weight, grad, first, second, average, count):
    first_new = BETA_ONE * first + (1.0 - BETA_ONE) * grad
    second_new = BETA_TWO * second + (1.0 - BETA_TWO) * grad * grad
    scaled = (
        first_new
        / (1.0 - BETA_ONE**count)
        / (jnp.sqrt(second_new / (1.0 - BETA_TWO**count)) + ADAM_EPS)
    )
    weight_new = weight - LEARN_RATE * (scaled + WEIGHT_DECAY * weight)
    return (weight_new, first_new, second_new, EMA_KEEP * average + (1.0 - EMA_KEEP) * weight_new)


def local(
    points,
    route,
    labels,
    interp_src,
    pool_nbr,
    sample,
    coarse_nbr,
    owner,
    step,
    flat,
    flat_mom,
    flat_sec,
    flat_ema,
    mats,
    mats_mom,
    mats_sec,
    mats_left,
    mats_right,
    mats_basis_l,
    mats_basis_r,
    mats_ema,
):
    n_pts = lax.axis_size("pts")
    n_sub = lax.axis_size("sub")
    fine = points.shape[0]
    coarse = sample.shape[0]
    cap = n_sub * fine // n_pts
    slots = n_pts * cap
    sources = n_sub * n_pts
    half = coarse // n_sub
    edges = NEIGH * half
    parts = coarse // LOW_B
    my_parts = parts // n_sub
    flat2 = jnp.pad(flat, (0, FLAT_ROWS * LANES - FLAT)).reshape(FLAT_ROWS, LANES)
    vmem = pl.BlockSpec(memory_space=pltpu.VMEM)
    smem = pl.BlockSpec(memory_space=pltpu.SMEM)
    dma = pltpu.SemaphoreType.DMA
    scratch = [
        VMEM((6, fine), BF16),
        VMEM((1, fine), I32),
        VMEM((1, fine), I32),
        VMEM((3, fine), I32),
        VMEM((NEIGH, coarse), I32),
        VMEM((1, coarse), I32),
        VMEM((NEIGH, coarse), I32),
        pltpu.SMEM((NMATS,), I32),
        VMEM((C1, C1), F32),
        VMEM((16, fine), F32),
        VMEM((n_pts * 16, cap), F32),
        VMEM((n_pts, 16, cap), BF16),
        VMEM((sources, 16, cap), BF16),
        VMEM((32, LANES), BF16),
        VMEM((n_pts, 32, LANES), BF16),
        VMEM((sources * 8, cap), BF16),
        VMEM((8, coarse), F32),
        VMEM((C1, edges), F32),
        VMEM((48, edges), BF16),
        VMEM((C1, half), F32),
        VMEM((C1, half), F32),
        VMEM((parts, CH, LOW_B), BF16),
        VMEM((parts, CH, LOW_B), BF16),
        VMEM((C1, edges), BF16),
        VMEM((144, edges), BF16),
        VMEM((144, edges), BF16),
        VMEM((LOW_B, edges), BF16),
        VMEM((C1, edges), F32),
        VMEM((GROUPS, edges), F32),
        VMEM((C1, half), F32),
        VMEM((C1, half), F32),
        VMEM((16, slots), F32),
        VMEM((80, slots), BF16),
        VMEM((80, slots), BF16),
        VMEM((C0, slots), F32),
        VMEM((3, LOW_B, slots), BF16),
        VMEM((3, C1, slots), BF16),
        VMEM((8, slots), F32),
        VMEM((parts, C0, LOW_B), F32),
        VMEM((my_parts, C0, LOW_B), F32),
        VMEM((parts, C1 + 8, LOW_B), F32),
        VMEM((my_parts, C1 + 8, LOW_B), F32),
        VMEM((LANES, LANES), F32),
        VMEM((LANES, LANES), F32),
        VMEM((LANES, LANES), F32),
        VMEM((LANES, LANES), F32),
        VMEM((LANES, LANES), F32),
        VMEM((LANES, LANES), F32),
        VMEM((LANES, LANES), F32),
        VMEM((LANES, LANES), F32),
        VMEM((LANES, LANES), F32),
        VMEM((80, LANES), F32),
        VMEM((48, LANES), F32),
        VMEM((144, LANES), F32),
        VMEM((144, LANES), F32),
        VMEM((144, LANES), F32),
        VMEM((256, LANES), F32),
        VMEM((128, LANES), F32),
        VMEM((128, LANES), F32),
        VMEM((n_pts, 8, LANES), F32),
        VMEM((256, LANES), F32),
        dma((n_pts,)),
        dma((n_pts,)),
        dma((n_pts,)),
        dma((n_pts,)),
        dma((n_pts,)),
        dma((n_pts,)),
        dma((n_pts,)),
        dma((n_pts,)),
        dma((8,)),
        dma((8,)),
        dma((9,)),
    ]
    reduced = pl.pallas_call(
        functools.partial(main_kernel, n_pts, n_sub),
        out_shape=jax.ShapeDtypeStruct((256, LANES), F32),
        in_specs=[pl.BlockSpec(memory_space=pltpu.HBM)] * 9 + [vmem],
        out_specs=vmem,
        scratch_shapes=scratch,
        compiler_params=pltpu.CompilerParams(
            collective_id=0, has_side_effects=True, vmem_limit_bytes=60 * 1024 * 1024
        ),
    )(
        points.T,
        route.reshape(1, fine),
        labels.reshape(1, fine),
        interp_src.T,
        pool_nbr.T,
        sample.reshape(1, coarse),
        coarse_nbr.T,
        owner,
        mats[0],
        flat2,
    )
    square = jax.ShapeDtypeStruct((C1, C1), F32)
    results = pl.pallas_call(
        soap_kernel,
        out_shape=[square] * 8
        + [
            jax.ShapeDtypeStruct((56, LANES), F32),
            jax.ShapeDtypeStruct((8, LANES), F32),
        ],
        in_specs=[vmem] + [smem] * 2 + [vmem] * 8,
        out_specs=[vmem] * 10,
    )(
        reduced,
        owner,
        step,
        mats[0],
        mats_mom[0],
        mats_sec[0],
        mats_left[0],
        mats_right[0],
        mats_basis_l[0],
        mats_basis_r[0],
        mats_ema[0],
    )
    flat_grad = results[8].reshape(-1)[:FLAT]
    count = step[0].astype(F32)
    flat_out = adam_update(flat, flat_grad, flat_mom, flat_sec, flat_ema, count)
    return (results[9][0, 0], results[9][0, 1]) + flat_out + tuple(
        result[None] for result in results[:8]
    )


def solution(mesh):
    placed = (
        P(("pts", "sub"), None),
        P(("pts", "sub")),
        P(("pts", "sub")),
        P(("pts", "sub"), None),
        P("pts", None),
        P("pts"),
        P("pts", None),
        P(),
        P(),
        P(),
        P(),
        P(),
        P(),
    ) + (P("pts", None, None),) * 8
    return jax.shard_map(
        local,
        mesh=mesh,
        in_specs=placed,
        out_specs=(P(),) * 6 + (P("pts", None, None),) * 8,
        check_vma=False,
    )
```

```python
import functools
import math

import jax
import jax.numpy as jnp
from jax import lax
from jax.experimental import pallas as pl
from jax.experimental.pallas import tpu as pltpu
from jax.sharding import PartitionSpec as P

C0 = 32
C1 = 64
NEIGH = 16
NCLS = 13
GROUPS = 8
NMATS = 5

HIGHEST = lax.Precision.HIGHEST
CLIP_NORM = 0.01
BETA_ONE = 0.9
BETA_TWO = 0.95
ADAM_EPS = 1e-08
LEARN_RATE = 0.1
WEIGHT_DECAY = 0.01
EMA_KEEP = 0.9
INTERP_EPS = 0.01

F32 = jnp.float32
BF16 = jnp.bfloat16
I32 = jnp.int32
MESH = pl.DeviceIdType.MESH
VMEM = pltpu.VMEM

LANES = 128
FLAT_ROWS = 64
LOW_B = 256
CH = 80
NEG = -1e30


def offsets():
    shapes = [
        ("w_stem", (6, C0)),
        ("b_stem", (C0,)),
        ("w_down", (3 + C0, C1)),
        ("b_down", (C1,)),
        ("w_pos", (3, C1)),
        ("b_pos", (C1,)),
        ("w_att1", (C1, GROUPS)),
        ("b_att1", (GROUPS,)),
        ("w_att2", (GROUPS, GROUPS)),
        ("b_att2", (GROUPS,)),
        ("w_up", (C1, C0)),
        ("b_up", (C0,)),
        ("w_skip", (C0, C0)),
        ("w_head", (C0, NCLS)),
        ("b_head", (NCLS,)),
    ]
    found = {}
    total = 0
    for name, shape in shapes:
        found[name] = total
        total += math.prod(shape)
    return found, total


OFF, FLAT = offsets()


def dot(left, right):
    return lax.dot_general(left, right, (((1,), (0,)), ((), ())), preferred_element_type=F32)


def dot_nt(left, right):
    return lax.dot_general(left, right, (((1,), (1,)), ((), ())), preferred_element_type=F32)


def exact(left, right, dims=((1,), (0,))):
    return lax.dot_general(
        left, right, (dims, ((), ())), precision=HIGHEST, preferred_element_type=F32
    )


def relu(values):
    return jnp.maximum(values, 0.0)


def rows_of(count, length):
    return lax.broadcasted_iota(I32, (count, length), 0)


def lanes_of(count, length):
    return lax.broadcasted_iota(I32, (count, length), 1)


def onehot(low, count):
    hit = rows_of(count, low.shape[1]) == low
    return jnp.where(hit, 1.0, 0.0).astype(BF16)


def pick(spread, high, parts):
    each = spread.shape[0] // parts
    found = spread[0:each]
    for part in range(1, parts):
        found = jnp.where(high == part, spread[part * each : (part + 1) * each], found)
    return found


def place(values, high, parts):
    return jnp.concatenate(
        [jnp.where(high == part, values, 0.0) for part in range(parts)], 0
    ).astype(BF16)


def unpack(flat_ref, out_ref, offset, rows, width, at):
    stride = LANES // width if LANES % width == 0 else rows
    for first in range(min(stride, rows)):
        count = (rows - first + stride - 1) // stride
        padded = -(-count // 8) * 8
        line, lane = divmod(offset + first * width, LANES)
        values = flat_ref[line : line + padded, :]
        if lane:
            values = pltpu.roll(values, LANES - lane, 1)
        if lane + width > LANES:
            following = pltpu.roll(flat_ref[line + 1 : line + 1 + padded, :], LANES - lane, 1)
            values = jnp.where(lanes_of(padded, LANES) < LANES - lane, values, following)
        values = jnp.where(lanes_of(padded, LANES) < width, values, 0.0)
        if count == 1:
            out_ref[at + first : at + first + 1, :] = values[0:1]
        else:
            out_ref[pl.ds(at + first, count, stride=stride), :] = values[0:count]


def pack(out_ref, base, source_ref, row, lane_from, offset, rows, width):
    stride = LANES // width if LANES % width == 0 else rows
    for first in range(min(stride, rows)):
        count = (rows - first + stride - 1) // stride
        line, lane = divmod(offset + first * width, LANES)
        if count == 1:
            values = source_ref[row + first : row + first + 1, :]
        else:
            values = source_ref[pl.ds(row + first, count, stride=stride), :]
        shift = (lane - lane_from) % LANES
        padded = -(-count // 8) * 8
        if padded != count:
            values = jnp.concatenate([values, jnp.zeros((padded - count, LANES), F32)], 0)
        if shift:
            values = pltpu.roll(values, shift, 1)
        values = values[0:count]
        at = lanes_of(count, LANES)
        here = jnp.where((at >= lane) & (at < lane + width), values, 0.0)
        out_ref[base + line : base + line + count, :] += here
        if lane + width > LANES:
            there = jnp.where(at < lane + width - LANES, values, 0.0)
            out_ref[base + line + 1 : base + line + 1 + count, :] += there


def main_kernel(
    n_pts,
    n_sub,
    pts_hbm,
    route_hbm,
    labels_hbm,
    src_hbm,
    pool_hbm,
    sample_hbm,
    cnbr_hbm,
    owner_hbm,
    mats_hbm,
    flat_hbm,
    out_ref,
    pts_ref,
    route_ref,
    labels_ref,
    src_ref,
    pool_ref,
    sample_ref,
    cnbr_ref,
    owner_ref,
    mats_ref,
    flat_line,
    flat_ref,
    data,
    sacc,
    sendb,
    recv,
    matmine,
    matall,
    tabb,
    cen,
    pin,
    cat,
    pooled_ref,
    rsum_ref,
    ctab,
    btab,
    near,
    est,
    gst,
    ohs,
    car,
    sc,
    mixed_ref,
    blk_ref,
    slot,
    fin,
    fgr,
    skp,
    foh,
    fsrc,
    fwt,
    dcp,
    dcr,
    dkp,
    dkr,
    wst,
    wd,
    wp,
    w1,
    w2,
    wu,
    wsk,
    wh,
    bias,
    ga,
    gb,
    gc,
    gd,
    ge,
    gbuf,
    gsib,
    ghalf,
    gsh,
    gfull,
    a2a_send,
    a2a_recv,
    mat_send,
    mat_recv,
    red_send,
    red_recv,
    gat_send,
    gat_recv,
    sib_send,
    sib_recv,
    load_sem,
):
    fine = route_ref.shape[1]
    coarse = sample_ref.shape[1]
    cap = sendb.shape[2]
    slots = n_pts * cap
    half = coarse // n_sub
    edges = NEIGH * half
    sources = n_sub * n_pts
    parts = coarse // LOW_B
    my_parts = parts // n_sub
    shift = cap.bit_length() - 1
    low_shift = LOW_B.bit_length() - 1
    span = 512
    me = lax.axis_index("pts")
    sub = lax.axis_index("sub")
    half_at = pl.multiple_of(sub * half, half)

    far_refs = (pts_hbm, route_hbm, labels_hbm, src_hbm, mats_hbm, sample_hbm, pool_hbm, cnbr_hbm, owner_hbm)
    near_refs = (pts_ref, route_ref, labels_ref, src_ref, mats_ref, sample_ref, pool_ref, cnbr_ref, owner_ref)
    loads = [
        pltpu.make_async_copy(source, target, load_sem.at[number])
        for number, (source, target) in enumerate(zip(far_refs, near_refs))
    ]
    loads.append(
        pltpu.make_async_copy(flat_hbm, flat_line, load_sem.at[len(loads)])
    )
    for load in loads:
        load.start()

    barrier = pltpu.get_barrier_semaphore()

    powers = [2**k for k in range(n_pts.bit_length() - 1)]
    my_bits = [lax.bitwise_and(lax.shift_right_logical(me, k), 1) for k in range(len(powers))]

    def partner(step):
        step = n_pts - step
        found = 0
        for k, power in enumerate(powers):
            bit = lax.bitwise_and(my_bits[k] + lax.shift_right_logical(step, k), 1)
            found = found + power * bit
        return found

    def greet(step, carry):
        peer = partner(step)
        pl.semaphore_signal(barrier, inc=1, device_id={"pts": peer}, device_id_type=MESH)
        return carry

    lax.fori_loop(1, n_pts, greet, 0)
    pl.semaphore_signal(barrier, inc=1, device_id={"sub": 1 - sub}, device_id_type=MESH)

    def sibling(number, source, target):
        return pltpu.make_async_remote_copy(
            src_ref=source,
            dst_ref=target,
            send_sem=sib_send.at[number],
            recv_sem=sib_recv.at[number],
            device_id={"sub": 1 - sub},
            device_id_type=MESH,
        )

    for load in loads[0:5] + loads[9:]:
        load.wait()
    data[0:6, :] = pts_ref[...].astype(F32)
    data[6:8, :] = jnp.zeros((2, fine), F32)
    source_rows = src_ref[...]
    data[8:11, :] = lax.shift_right_logical(source_rows, 5).astype(F32)
    data[11:14, :] = (source_rows & 31).astype(F32)
    data[14:15, :] = (labels_ref[...] + 1).astype(F32)
    data[15:16, :] = jnp.zeros((1, fine), F32)
    sacc[...] = jnp.zeros_like(sacc)
    counts = jnp.zeros((16, 32), F32)
    for chunk in range(fine // span):
        lanes = slice(chunk * span, (chunk + 1) * span)
        route = route_ref[:, lanes]
        high = lax.shift_right_logical(route, shift)
        spread = place(data[:, lanes], high, n_pts)
        sacc[...] += dot_nt(spread, onehot(route & (cap - 1), cap))
        classes = onehot(labels_ref[:, lanes], 16)
        counts = counts + dot_nt(jnp.ones((16, span), BF16), jnp.concatenate([classes, classes], 0))
    count_high = jnp.floor(counts * (1.0 / 128.0))
    count_low = counts - 128.0 * count_high
    digits = jnp.where(lanes_of(16, 32) < 16, count_low, count_high)
    digits = jnp.where(rows_of(16, 32) == 15, digits, 0.0)
    data[:, 0:cap] = jnp.zeros((16, cap), F32)
    data[:, 0:32] = digits
    sendb[...] = (sacc[...].reshape(n_pts, 16, cap) + data[:, 0:cap][None]).astype(BF16)
    matrix = mats_ref[...]
    matmine[...] = jnp.concatenate([matrix[0:32], matrix[32:64]], 1).astype(BF16)

    pl.semaphore_wait(barrier, n_pts)

    def block_copy(peer, index):
        return pltpu.make_async_remote_copy(
            src_ref=sendb.at[peer],
            dst_ref=recv.at[sub * n_pts + index],
            send_sem=a2a_send.at[peer],
            recv_sem=a2a_recv.at[index],
            device_id={"pts": peer},
            device_id_type=MESH,
        )

    def mat_copy(peer, index):
        return pltpu.make_async_remote_copy(
            src_ref=matmine,
            dst_ref=matall.at[index],
            send_sem=mat_send.at[peer],
            recv_sem=mat_recv.at[index],
            device_id={"pts": peer},
            device_id_type=MESH,
        )

    def send_blocks(step, carry):
        block_copy(partner(step), me).start()
        return carry

    def send_mats(step, carry):
        mat_copy(partner(step), me).start()
        return carry

    lax.fori_loop(1, n_pts, send_blocks, 0)
    recv[sub * n_pts + me] = sendb[me]
    matall[me] = matmine[...]

    for ref in (wst, wd, wp, w1, w2, wu, wsk, wh, bias):
        ref[...] = jnp.zeros_like(ref)
    padded = jnp.pad(flat_line[...], (0, FLAT_ROWS * LANES - FLAT))
    flat_ref[...] = padded.reshape(FLAT_ROWS, LANES)
    unpack(flat_ref, wst, OFF["w_stem"], 6, C0, 0)
    unpack(flat_ref, wd, OFF["w_down"], 3, C1, 0)
    unpack(flat_ref, wd, OFF["w_down"] + 3 * C1, C0, C1, 16)
    unpack(flat_ref, wp, OFF["w_pos"], 3, C1, 8)
    unpack(flat_ref, w1, OFF["w_att1"], C1, GROUPS, 0)
    unpack(flat_ref, w2, OFF["w_att2"], GROUPS, GROUPS, 0)
    unpack(flat_ref, wu, OFF["w_up"], C1, C0, 0)
    unpack(flat_ref, wsk, OFF["w_skip"], C0, C0, 0)
    unpack(flat_ref, wh, OFF["w_head"], C0, NCLS, 0)
    names = ("b_stem", "b_down", "b_pos", "b_att1", "b_att2", "b_up", "b_head")
    widths = (C0, C1, C1, GROUPS, GROUPS, C0, NCLS)
    for position, (name, width) in enumerate(zip(names, widths)):
        unpack(flat_ref, bias, OFF[name], 1, width, position)
    columns = bias[...].T
    b_stem = columns[0:C0, 0:1]
    b_down = columns[0:C1, 1:2]
    b_pos = columns[0:C1, 2:3]
    b_att1 = columns[0:GROUPS, 3:4]
    b_att2 = columns[0:GROUPS, 4:5]
    b_up = columns[0:C0, 5:6]
    b_head = jnp.where(rows_of(16, 1) < NCLS, columns[0:16, 6:7], NEG)
    w_stem_t = wst[...].T[0:C0, 0:16].astype(BF16)
    w_down_t = wd[...].T[0:C1, 0:48].astype(BF16)
    w_pos_t = wp[...].T[0:C1, 0:16].astype(BF16)
    w_att1_t = w1[...].T[0:GROUPS, 0:C1].astype(BF16)
    w_att2_t = w2[...].T[0:GROUPS, 0:16].astype(BF16)
    w_up_t = wu[...].T[0:C0, 0:C1].astype(BF16)
    w_skip_t = wsk[...].T[0:C0, 0:C0].astype(BF16)
    w_head_t = wh[...].T[0:16, 0:C0].astype(BF16)
    w_down_stem = wd[16:48, 0:C1].astype(BF16)
    w_att1 = w1[0:C1, 0:16].astype(BF16)
    w_att2 = w2[0:GROUPS, 0:16].astype(BF16)
    w_up = wu[0:C1, 0:C0].astype(BF16)
    w_skip = wsk[0:C0, 0:C0].astype(BF16)
    w_head = wh[0:C0, 0:16].astype(BF16)

    def wait_blocks(step, carry):
        peer = partner(step)
        block_copy(peer, peer).wait_recv()
        return carry

    lax.fori_loop(1, n_pts, wait_blocks, 0)
    lax.fori_loop(1, n_pts, send_mats, 0)
    for load in loads[5:9]:
        load.wait()
    mine = recv.at[pl.ds(sub * n_pts, n_pts)]
    forward = sibling(0, mine, mine)
    forward.start()
    for source in range(n_pts):
        slot[:, source * cap : (source + 1) * cap] = recv[sub * n_pts + source].astype(F32)
    forward.wait_recv()

    table = recv[...].astype(F32)[:, 0:8, :].reshape(sources * 8, cap)
    ones_row = (rows_of(sources * 8, cap) & 7) == 7
    tabb[...] = jnp.where(ones_row, 1.0, table).astype(BF16)
    count_row = jnp.sum(recv[...].astype(F32)[:, 8:16, :], axis=0)[7:8, 0:32]
    count_at = jnp.broadcast_to(count_row, (16, 32))
    low_hit = lanes_of(16, 32) == rows_of(16, 32)
    high_hit = lanes_of(16, 32) == rows_of(16, 32) + 16
    class_counts = jnp.sum(
        jnp.where(low_hit, count_at, 0.0) + jnp.where(high_hit, 128.0 * count_at, 0.0),
        axis=1,
        keepdims=True,
    )
    total_fine = float(fine * n_pts * n_sub)
    class_w = jnp.where(
        rows_of(16, 1) < NCLS, total_fine / (NCLS * class_counts) * (1.0 / total_fine), 0.0
    )

    def gather_points(index):
        hot = onehot(index & (cap - 1), cap)
        high = jnp.broadcast_to(lax.shift_right_logical(index, shift), (8, index.shape[1]))
        return pick(dot(tabb[...], hot), high, sources)

    zeros8 = jnp.zeros((8, span), F32)
    for chunk in range(coarse // span):
        lanes = slice(chunk * span, (chunk + 1) * span)
        found = gather_points(sample_ref[:, lanes])
        cen[:, lanes] = jnp.where(rows_of(8, span) < 6, found, 0.0)
    centre = cen[:, pl.ds(half_at, half)]
    centre_low = jnp.concatenate([centre, zeros8], 0).astype(BF16)
    w_xyz_t = jnp.where(lanes_of(C1, 16) < 3, wd[...].T[0:C1, 0:16], 0.0).astype(BF16)
    pool_base = b_down - dot(w_xyz_t, centre_low)

    def at_edge(k):
        return pl.ds(pl.multiple_of(k * half, half), half)

    def every_edge(step, unroll):
        def run(k, carry):
            step(k, at_edge(k))
            return carry

        lax.fori_loop(0, NEIGH, run, 0, unroll=unroll)

    def pool_gather(k, lanes):
        found = gather_points(pool_ref[pl.ds(k, 1), pl.ds(half_at, half)])
        cat[0:16, lanes] = jnp.concatenate([found, zeros8], 0).astype(BF16)

    def pool_stem(k, lanes):
        cat[16:48, lanes] = relu(dot(w_stem_t, cat[0:16, lanes]) + b_stem).astype(BF16)

    def pool_project(k, lanes):
        pin[:, lanes] = dot(w_down_t, cat[:, lanes]).astype(BF16).astype(F32) + pool_base

    every_edge(pool_gather, 4)
    every_edge(pool_stem, 16)
    every_edge(pool_project, 16)

    def tree(combine, values):
        while len(values) > 1:
            paired = [combine(values[i], values[i + 1]) for i in range(0, len(values) - 1, 2)]
            values = paired + ([values[-1]] if len(values) % 2 else [])
        return values[0]

    wide = 256

    def log_sum(r, carry):
        rows = pl.ds(pl.multiple_of(r * 8, 8), 8)
        for start in range(0, half, wide):
            spots = [slice(k * half + start, k * half + start + wide) for k in range(NEIGH)]
            values = [pin[rows, spot] for spot in spots]
            most = tree(jnp.maximum, values)
            values = [jnp.exp(value - most) for value in values]
            for spot, value in zip(spots, values):
                pin[rows, spot] = value
            total = tree(jnp.add, values)
            pooled_ref[rows, start : start + wide] = most + jnp.log(total)
            rsum_ref[rows, start : start + wide] = 1.0 / total
        return carry

    lax.fori_loop(0, C1 // 8, log_sum, 0, unroll=2)

    def table_rows(values, target):
        for part in range(my_parts):
            lanes = slice(part * LOW_B, (part + 1) * LOW_B)
            stacked = jnp.concatenate(
                [values[:, lanes], centre[:, lanes], jnp.zeros((8, LOW_B), F32)], 0
            )
            target[sub * my_parts + part] = stacked.astype(BF16)

    table_rows(pooled_ref[...], ctab)
    my_ctab = ctab.at[pl.ds(sub * my_parts, my_parts)]
    give_pooled = sibling(1, my_ctab, my_ctab)
    give_pooled.start()

    def wait_mats(step, carry):
        peer = partner(step)
        mat_copy(peer, peer).wait_recv()
        return carry

    lax.fori_loop(1, n_pts, wait_mats, 0)

    def layer(position):
        folded = matall[owner_ref[position]].astype(F32)
        return jnp.concatenate([folded[:, 0:C1], folded[:, C1 : 2 * C1]], 0)

    w_query, w_key, w_value, w_pos2_32, w_out_32 = [layer(position) for position in range(NMATS)]
    w_qkv = jnp.concatenate([w_query, w_key, w_value], 1).astype(BF16)
    w_query_t = w_query.T.astype(BF16)
    w_pos2 = w_pos2_32.astype(BF16)
    w_pos2_t = w_pos2_32.T
    w_edge_t = jnp.concatenate(
        [
            jnp.concatenate([-w_key.T, w_pos2_t], 1),
            jnp.concatenate([w_value.T, w_pos2_t], 1),
        ],
        0,
    ).astype(BF16)
    w_out = w_out_32.astype(BF16)
    w_out_t = w_out_32.T.astype(BF16)
    queries = dot(w_query_t, pooled_ref[...].astype(BF16))

    def at_slot(step):
        return pl.ds(pl.multiple_of(step * span, span), span)

    def every_slot(step, unroll):
        def run(j, carry):
            step(j, at_slot(j))
            return carry

        lax.fori_loop(0, slots // span, run, 0, unroll=unroll)

    def fine_points(j, lanes):
        ones = jnp.where(rows_of(8, span) == 7, 1.0, slot[0:8, lanes])
        fin[0:16, lanes] = jnp.concatenate([ones, zeros8], 0).astype(BF16)

    def fine_stem(j, lanes):
        fin[16:48, lanes] = relu(dot(w_stem_t, fin[0:16, lanes]) + b_stem).astype(BF16)

    def fine_skip(j, lanes):
        skp[:, lanes] = dot(w_skip_t, fin[16:48, lanes])

    every_slot(fine_points, 4)
    every_slot(fine_stem, 8)
    every_slot(fine_skip, 8)
    give_pooled.wait_recv()

    def attend_gather(k, lanes):
        index = cnbr_ref[pl.ds(k, 1), pl.ds(half_at, half)]
        hot = onehot(index & (LOW_B - 1), LOW_B)
        ohs[:, lanes] = hot
        high = lax.shift_right_logical(index, low_shift)
        found = pick(dot(ctab[...].reshape(parts * CH, LOW_B), hot), high, parts)
        near[:, lanes] = found[0:C1].astype(BF16)
        offset = jnp.where(rows_of(8, half) == 7, 1.0, centre - found[C1 : C1 + 8])
        est[128:144, lanes] = jnp.concatenate([zeros8, offset], 0).astype(BF16)

    def attend_pos(k, lanes):
        est[64:128, lanes] = relu(dot(w_pos_t, est[128:144, lanes]) + b_pos).astype(BF16)

    def attend_edge(k, lanes):
        both = dot(w_edge_t, jnp.concatenate([near[:, lanes], est[64:128, lanes]], 0))
        est[0:64, lanes] = (queries + both[0:C1]).astype(BF16)
        car[:, lanes] = both[C1 : 2 * C1]

    def attend_act(k, lanes):
        act = relu(dot(w_att1_t, est[0:64, lanes]) + b_att1)
        offset = est[128:144, lanes].astype(F32)[8:16]
        est[128:144, lanes] = jnp.concatenate([act, offset], 0).astype(BF16)

    def attend_score(k, lanes):
        sc[:, lanes] = dot(w_att2_t, est[128:144, lanes]) + b_att2

    every_edge(attend_gather, 4)
    every_edge(attend_pos, 16)
    every_edge(attend_edge, 16)
    every_edge(attend_act, 16)
    every_edge(attend_score, 16)

    for start in range(0, half, wide):
        spots = [slice(k * half + start, k * half + start + wide) for k in range(NEIGH)]
        values = [sc[:, spot] for spot in spots]
        most = tree(jnp.maximum, values)
        values = [jnp.exp(value - most) for value in values]
        scale = 1.0 / tree(jnp.add, values)
        for spot, value in zip(spots, values):
            sc[:, spot] = value * scale

    for g in range(GROUPS):
        rows = slice(8 * g, 8 * g + 8)
        for start in range(0, half, wide):
            spots = [slice(k * half + start, k * half + start + wide) for k in range(NEIGH)]
            terms = [
                jnp.broadcast_to(sc[g : g + 1, spot], (8, wide)) * car[rows, spot]
                for spot in spots
            ]
            mixed_ref[rows, start : start + wide] = tree(jnp.add, terms)

    block = pooled_ref[...] + dot(w_out_t, mixed_ref[...].astype(BF16))
    blk_ref[...] = block
    table_rows(block, btab)
    my_btab = btab.at[pl.ds(sub * my_parts, my_parts)]
    give_block = sibling(2, my_btab, my_btab)
    give_block.start()

    def source_of(lanes, i):
        index = (32.0 * slot[8 + i : 9 + i, lanes] + slot[11 + i : 12 + i, lanes]).astype(I32)
        return index & (LOW_B - 1), lax.shift_right_logical(index, low_shift)

    def fine_hot(j, lanes):
        for i in range(3):
            foh[i, :, lanes] = onehot(source_of(lanes, i)[0], LOW_B)

    every_slot(fine_hot, 2)
    give_block.wait_recv()

    def fine_gather(j, lanes):
        points = slot[0:8, lanes]
        inverses = []
        for i in range(3):
            high = source_of(lanes, i)[1]
            found = pick(dot(btab[...].reshape(parts * CH, LOW_B), foh[i, :, lanes]), high, parts)
            fsrc[i, :, lanes] = found[0:C1].astype(BF16)
            diff = jnp.where(rows_of(8, span) < 3, points - found[C1 : C1 + 8], 0.0)
            inverses.append(1.0 / (jnp.sum(diff * diff, axis=0, keepdims=True) + INTERP_EPS))
        norm = 1.0 / (inverses[0] + inverses[1] + inverses[2])
        for i in range(3):
            fwt[i : i + 1, lanes] = inverses[i] * norm

    def fine_join(j, lanes):
        terms = [fwt[i : i + 1, lanes] * dot(w_up_t, fsrc[i, :, lanes]) for i in range(3)]
        interp = (terms[0] + terms[1] + terms[2] + b_up).astype(BF16).astype(F32)
        fin[48:80, lanes] = relu(interp + skp[:, lanes]).astype(BF16)

    def fine_loss(j, loss):
        lanes = at_slot(j)
        logits = dot(w_head_t, fin[48:80, lanes]) + b_head
        label = slot[14:15, lanes].astype(I32)
        hit = jnp.where(rows_of(16, span) + 1 == label, 1.0, 0.0)
        row_w = jnp.sum(hit * class_w, axis=0, keepdims=True)
        peak = jnp.max(logits, axis=0, keepdims=True)
        raised = jnp.exp(logits - peak)
        total = jnp.sum(raised, axis=0, keepdims=True)
        named = jnp.sum(hit * logits, axis=0, keepdims=True)
        fgr[64:80, lanes] = (row_w * (raised * (1.0 / total) - hit)).astype(BF16)
        return loss + row_w * (peak + jnp.log(total) - named)

    def fine_fused(j, lanes):
        kept = fin[48:80, lanes].astype(F32) > 0
        fgr[0:32, lanes] = jnp.where(kept, dot(w_head, fgr[64:80, lanes]), 0.0).astype(BF16)

    def fine_scatter(j, lanes):
        dfused = fgr[0:32, lanes].astype(F32)
        total = 0.0
        for i in range(3):
            spread = place(fwt[i : i + 1, lanes] * dfused, source_of(lanes, i)[1], parts)
            total = total + dot_nt(spread, foh[i, :, lanes])
        dcp[...] += total.reshape(parts, C0, LOW_B)

    def fine_back(j, lanes):
        kept = fin[16:48, lanes].astype(F32) > 0
        fgr[32:64, lanes] = jnp.where(kept, dot(w_skip, fgr[0:32, lanes]), 0.0).astype(BF16)

    every_slot(fine_gather, 8)
    every_slot(fine_join, 8)
    loss = lax.fori_loop(0, slots // span, fine_loss, jnp.zeros((1, span), F32), unroll=4)
    every_slot(fine_fused, 8)
    dcp[...] = jnp.zeros_like(dcp)
    every_slot(fine_scatter, 2)

    other = (1 - sub) * my_parts
    own = sub * my_parts
    give_dup = sibling(3, dcp.at[pl.ds(other, my_parts)], dcr)
    give_dup.start()
    every_slot(fine_back, 8)
    ga[...] = jnp.zeros_like(ga)
    for start in range(0, slots, 4 * span):
        lanes = slice(start, start + 4 * span)
        ga[:, 0:80] += dot_nt(fin[:, lanes], fgr[:, lanes])
    give_dup.wait_recv()

    def own_half(partial, received):
        return jnp.concatenate(
            [partial[own + part] + received[part] for part in range(my_parts)], 1
        )

    dup_low = own_half(dcp, dcr).astype(BF16)
    dblock = dot(w_up, dup_low)
    dbranch_low = dblock.astype(BF16)
    dmixed = dot(w_out, dbranch_low)

    def group_sum(values):
        return jnp.concatenate(
            [
                jnp.sum(values[8 * g : 8 * g + 8], axis=0, keepdims=True)
                for g in range(GROUPS)
            ],
            0,
        )

    def expand(values):
        return jnp.concatenate(
            [jnp.broadcast_to(values[g : g + 1], (8, values.shape[1])) for g in range(GROUPS)], 0
        )

    centred = group_sum(dmixed * mixed_ref[...])

    def back_score(k, lanes):
        ds2 = sc[:, lanes] * (group_sum(dmixed * car[:, lanes]) - centred)
        gst[128:144, lanes] = jnp.concatenate([ds2, zeros8], 0).astype(BF16)

    def back_act(k, lanes):
        scores = gst[128:144, lanes]
        kept = est[128:144, lanes].astype(F32)[0:8] > 0
        ds1 = jnp.where(kept, dot(w_att2, scores), 0.0)
        ds2 = scores.astype(F32)[0:8]
        gst[128:144, lanes] = jnp.concatenate([ds1, ds2], 0).astype(BF16)

    def back_edge(k, lanes):
        small = gst[128:144, lanes]
        dcarried = expand(sc[:, lanes]) * dmixed
        gst[64:128, lanes] = (dot(w_att1, small) + dcarried).astype(BF16)
        index = cnbr_ref[pl.ds(k, 1), pl.ds(half_at, half)]
        high = lax.shift_right_logical(index, low_shift)
        spread = place(jnp.concatenate([dcarried, small.astype(F32)[0:8]], 0), high, parts)
        dkp[...] += dot_nt(spread, ohs[:, lanes]).reshape(parts, C1 + 8, LOW_B)

    def back_pos(k, lanes):
        kept = est[64:128, lanes].astype(F32) > 0
        gst[0:64, lanes] = jnp.where(kept, dot(w_pos2, gst[64:128, lanes]), 0.0).astype(BF16)

    every_edge(back_score, 16)
    every_edge(back_act, 16)
    dkp[...] = jnp.zeros_like(dkp)
    every_edge(back_edge, 16)
    give_dkv = sibling(4, dkp.at[pl.ds(other, my_parts)], dkr)
    give_dkv.start()
    every_edge(back_pos, 16)
    inputs = jnp.concatenate(
        [blk_ref[...].astype(BF16), mixed_ref[...].astype(BF16), jnp.ones((16, half), BF16)], 0
    )
    grads = jnp.concatenate([dup_low, jnp.zeros((C0, half), BF16), dbranch_low], 0)
    gd[...] = dot_nt(inputs, grads)
    gc[...] = jnp.zeros_like(gc)
    ge[...] = jnp.zeros_like(ge)
    for start in range(0, edges, 4 * span):
        lanes = slice(start, start + 4 * span)
        result = dot_nt(est[:, lanes], gst[:, lanes])
        gc[...] += result[:, 0:128]
        ge[:, 0:16] += result[:, 128:144]
    ds1_total = tree(
        jnp.add,
        [gst[128:144, k * half : (k + 1) * half].astype(F32)[0:8] for k in range(NEIGH)],
    )
    w_att1_exact = w1[0:C1, 0:16].astype(BF16).astype(F32)[:, 0:8]
    dqueries = exact(w_att1_exact, ds1_total)
    give_dkv.wait_recv()
    dkv = own_half(dkp, dkr)
    dkeys = -exact(w_att1_exact, dkv[C1 : C1 + 8])
    dqkv_low = jnp.concatenate([dqueries, dkeys, dkv[0:C1]], 0).astype(BF16)
    gbuf[...] = jnp.zeros_like(gbuf)
    gbuf[0:64, :] = dot_nt(pooled_ref[...].astype(BF16), dqkv_low[0:128])
    gbuf[64:128, 0:64] = dot_nt(pooled_ref[...].astype(BF16), dqkv_low[128:192])
    dpooled = dblock + dot(w_qkv, dqkv_low)

    gb[...] = jnp.zeros_like(gb)
    gb[0:16, 0:C1] = dot_nt(centre_low, (-dpooled).astype(BF16))
    dscaled = dpooled * rsum_ref[...]

    def pool_back(k, lanes):
        dpin = (pin[:, lanes] * dscaled).astype(BF16)
        gst[0:64, lanes] = dpin
        kept = cat[16:48, lanes].astype(F32) > 0
        gst[64:96, lanes] = jnp.where(kept, dot(w_down_stem, dpin), 0.0).astype(BF16)

    every_edge(pool_back, 16)
    for start in range(0, edges, 4 * span):
        lanes = slice(start, start + 4 * span)
        gb[:, 0:96] += dot_nt(cat[:, lanes], gst[0:96, lanes])

    left = lanes_of(64, LANES) < 64
    gd_out = gd[64:128, :]
    gbuf[64:128, :] = jnp.where(left, gbuf[64:128, :], gc[64:128, :])
    gbuf[128:160, :] = jnp.where(left[0:32], pltpu.roll(gd_out[0:32], 64, 1), gd_out[32:64])
    base = 160
    pack(gbuf, base, ga, 0, 32, OFF["w_stem"], 6, C0)
    pack(gbuf, base, gb, 0, 64, OFF["w_stem"], 6, C0)
    pack(gbuf, base, ga, 7, 32, OFF["b_stem"], 1, C0)
    pack(gbuf, base, gb, 7, 64, OFF["b_stem"], 1, C0)
    pack(gbuf, base, gb, 0, 0, OFF["w_down"], 3, C1)
    pack(gbuf, base, gb, 16, 0, OFF["w_down"] + 3 * C1, C0, C1)
    pack(gbuf, base, gb, 7, 0, OFF["b_down"], 1, C1)
    pack(gbuf, base, gc, 136, 0, OFF["w_pos"], 3, C1)
    pack(gbuf, base, gc, 143, 0, OFF["b_pos"], 1, C1)
    pack(gbuf, base, ge, 0, 0, OFF["w_att1"], C1, GROUPS)
    pack(gbuf, base, ge, 143, 0, OFF["b_att1"], 1, GROUPS)
    pack(gbuf, base, ge, 128, 8, OFF["w_att2"], GROUPS, GROUPS)
    pack(gbuf, base, ge, 143, 8, OFF["b_att2"], 1, GROUPS)
    pack(gbuf, base, gd, 0, 0, OFF["w_up"], C1, C0)
    pack(gbuf, base, gd, 128, 0, OFF["b_up"], 1, C0)
    pack(gbuf, base, ga, 16, 0, OFF["w_skip"], C0, C0)
    pack(gbuf, base, ga, 48, 64, OFF["w_head"], C0, NCLS)
    pack(gbuf, base, ga, 7, 64, OFF["b_head"], 1, NCLS)
    loss_sum = jnp.sum(loss, axis=1, keepdims=True)
    line, lane = divmod(FLAT, LANES)
    at_loss = lanes_of(1, LANES) == lane
    gbuf[base + line : base + line + 1, :] += jnp.where(at_loss, loss_sum, 0.0)

    rows = gbuf.shape[0] // n_sub
    shards = rows // 8
    give_grad = sibling(5, gbuf.at[pl.ds(pl.multiple_of((1 - sub) * rows, rows), rows)], gsib)
    give_grad.start()
    give_grad.wait_recv()
    ghalf[...] = gbuf[pl.ds(pl.multiple_of(sub * rows, rows), rows), :] + gsib[...]
    mine_at = pl.multiple_of(sub * rows + me * 8, 8)

    def shard_copy(peer, index):
        return pltpu.make_async_remote_copy(
            src_ref=ghalf.at[pl.ds(pl.multiple_of(peer * 8, 8), 8)],
            dst_ref=gsh.at[index],
            send_sem=red_send.at[peer],
            recv_sem=red_recv.at[index],
            device_id={"pts": peer},
            device_id_type=MESH,
        )

    def sum_copy(peer, index):
        at = pl.multiple_of(sub * rows + index * 8, 8)
        return pltpu.make_async_remote_copy(
            src_ref=gfull.at[pl.ds(at, 8)],
            dst_ref=gfull.at[pl.ds(at, 8)],
            send_sem=gat_send.at[peer],
            recv_sem=gat_recv.at[index],
            device_id={"pts": peer},
            device_id_type=MESH,
        )

    holds = None if n_pts <= shards else me < shards

    def when(condition, run):
        if condition is None:
            run()
        else:
            pl.when(condition)(run)

    def each_peer(run, limited):
        def body(step, carry):
            peer = partner(step)
            when(None if holds is None or not limited else peer < shards, lambda: run(peer))
            return carry

        lax.fori_loop(1, n_pts, body, 0)

    each_peer(lambda peer: shard_copy(peer, me).start(), True)

    def reduce():
        gsh[me] = ghalf[pl.ds(pl.multiple_of(me * 8, 8), 8), :]
        each_peer(lambda peer: shard_copy(peer, peer).wait_recv(), False)
        gfull[pl.ds(mine_at, 8), :] = jnp.sum(gsh[...], axis=0)
        each_peer(lambda peer: sum_copy(peer, me).start(), False)

    when(holds, reduce)
    each_peer(lambda peer: sum_copy(peer, peer).wait_recv(), True)
    half_rows = gfull.at[pl.ds(pl.multiple_of(sub * rows, rows), rows)]
    give_full = sibling(6, half_rows, half_rows)
    give_full.start()

    each_peer(lambda peer: block_copy(peer, me).wait_send(), False)
    each_peer(lambda peer: mat_copy(peer, me).wait_send(), False)
    each_peer(lambda peer: shard_copy(peer, me).wait_send(), True)
    when(holds, lambda: each_peer(lambda peer: sum_copy(peer, me).wait_send(), False))
    for copy in (forward, give_pooled, give_block, give_dup, give_dkv, give_grad, give_full):
        copy.wait_send()
    give_full.wait_recv()
    out_ref[...] = gfull[...]


def normalised(matrix):
    return matrix * lax.rsqrt(jnp.sum(matrix * matrix, axis=0, keepdims=True))


def gram_schmidt_pair(matrix, width=8):
    size = matrix.shape[0]
    left = lanes_of(size, 2 * size) < size
    column = lanes_of(1, 2 * size)
    left_row = column < size
    place_row = jnp.where(left_row, column, column - size)

    def spread(values, halves, at):
        return jnp.where(halves, values[:, at : at + 1], values[:, size + at : size + at + 1])

    for first in range(0, size, width):
        span = range(width)
        pivots = [spread(matrix, left, first + i) for i in span]
        products = [jnp.sum(pivot * matrix, axis=0, keepdims=True) for pivot in pivots]
        gram = [
            [spread(products[i], left_row, first + l) if l >= i else None for l in span]
            for i in span
        ]
        taken = 0.0
        for i in span:
            inverse = 1.0 / gram[i][i]
            for l in range(i + 1, width):
                part = gram[i][l] * inverse
                pivots[l] = pivots[l] - part * pivots[i]
                products[l] = products[l] - part * products[i]
                for m in range(l, width):
                    gram[l][m] = gram[l][m] - part * gram[i][m]
            factor = jnp.where(place_row > first + i, products[i] * inverse, 0.0)
            taken = taken + pivots[i] * factor
        matrix = matrix - taken
    return normalised(matrix)


def careful_pair(matrix):
    size = matrix.shape[0]
    lane = lanes_of(size, 2 * size)
    left = lane < size
    place = jnp.where(left, lane, lane - size)

    def column(j, matrix):
        here = jnp.where(place == j, matrix, 0.0)
        first = jnp.sum(jnp.where(left, here, 0.0), axis=1, keepdims=True)
        second = jnp.sum(jnp.where(left, 0.0, here), axis=1, keepdims=True)
        pivot = jnp.where(left, first, second)
        pivot = pivot * lax.rsqrt(jnp.sum(pivot * pivot, axis=0, keepdims=True))
        factor = jnp.sum(pivot * matrix, axis=0, keepdims=True)
        return matrix - jnp.where(place > j, pivot * factor, 0.0)

    for repeat in range(2):
        matrix = normalised(lax.fori_loop(0, size, column, matrix))
    return matrix


def departure(basis):
    size = basis.shape[0]
    same = rows_of(size, size) == lanes_of(size, size)
    return exact(basis, basis, ((0,), (0,))) - jnp.where(same, 1.0, 0.0)


def correct(basis, error):
    size = basis.shape[0]
    above = rows_of(size, size) < lanes_of(size, size)
    same = rows_of(size, size) == lanes_of(size, size)
    factor = jnp.where(above, error, jnp.where(same, 0.5 * error, 0.0))
    return basis - exact(basis, factor)


def orthonormal_pair(matrix, both_ref):
    size = matrix.shape[0]
    once = gram_schmidt_pair(matrix)
    halves = [once[:, 0:size], once[:, size : 2 * size]]
    errors = [departure(half) for half in halves]
    worst = jnp.max(jnp.maximum(jnp.abs(errors[0]), jnp.abs(errors[1])))
    halves = [correct(half, error) for half, error in zip(halves, errors)]
    halves = [correct(half, departure(half)) for half in halves]
    both_ref[...] = jnp.concatenate(halves, 1)

    @pl.when(jnp.logical_not(worst < 0.01))
    def _():
        both_ref[...] = careful_pair(matrix)

    return both_ref[...]


def soap_kernel(
    grads_ref,
    owner_ref,
    step_ref,
    weight_ref,
    first_ref,
    second_ref,
    left_ref,
    right_ref,
    basis_l_ref,
    basis_r_ref,
    average_ref,
    flat_ref,
    flat_mom_ref,
    flat_sec_ref,
    flat_ema_ref,
    weight_out,
    first_out,
    second_out,
    left_out,
    right_out,
    basis_l_out,
    basis_r_out,
    average_out,
    flat_out,
    flat_mom_out,
    flat_sec_out,
    flat_ema_out,
    loss_out,
    norm_out,
    both_ref,
):
    me = lax.axis_index("pts")
    grads = grads_ref[...]
    line, lane = divmod(FLAT, LANES)
    place_row = rows_of(256, LANES)
    at_loss = (place_row == 160 + line) & (lanes_of(256, LANES) == lane)
    loss = jnp.where(at_loss, grads, 0.0)
    loss_out[...] = jnp.sum(jnp.sum(loss, axis=0, keepdims=True), axis=1, keepdims=True)
    cleaned = jnp.where(at_loss, 0.0, grads)
    squares = jnp.sum(jnp.sum(cleaned * cleaned, axis=0, keepdims=True), axis=1, keepdims=True)
    norm = jnp.sqrt(squares)
    norm_out[...] = norm
    factor = jnp.minimum(1.0, CLIP_NORM / norm)
    count = jnp.full((1, 1), step_ref[0].astype(F32), F32)
    one_scale = 1.0 - jnp.exp(count * math.log(BETA_ONE))
    two_scale = 1.0 - jnp.exp(count * math.log(BETA_TWO))
    lines = FLAT_ROWS - 8

    def as_line(values):
        return jnp.broadcast_to(values, (lines, LANES)).reshape(lines * LANES)[0:FLAT]

    flat_grad = (cleaned[160 : 160 + lines] * factor).reshape(lines * LANES)[0:FLAT]
    flat_mom = BETA_ONE * flat_mom_ref[...] + (1.0 - BETA_ONE) * flat_grad
    flat_sec = BETA_TWO * flat_sec_ref[...] + (1.0 - BETA_TWO) * flat_grad * flat_grad
    flat_scaled = flat_mom / as_line(one_scale) / (jnp.sqrt(flat_sec / as_line(two_scale)) + ADAM_EPS)
    flat_new = flat_ref[...] - LEARN_RATE * (flat_scaled + WEIGHT_DECAY * flat_ref[...])
    flat_out[...] = flat_new
    flat_mom_out[...] = flat_mom
    flat_sec_out[...] = flat_sec
    flat_ema_out[...] = EMA_KEEP * flat_ema_ref[...] + (1.0 - EMA_KEEP) * flat_new
    folded = cleaned[128:160]
    stacked = [
        cleaned[0:64, 0:64],
        cleaned[0:64, 64:128],
        cleaned[64:128, 0:64],
        cleaned[64:128, 64:128],
        jnp.concatenate([folded[:, 0:64], folded[:, 64:128]], 0),
    ]
    grad = jnp.zeros((C1, C1), F32)
    owned = 0.0
    for position in range(NMATS):
        flag = jnp.where(owner_ref[position] == me, 1.0, 0.0)
        grad = grad + flag * stacked[position]
        owned = owned + flag
    grad = grad * factor
    basis_l = basis_l_ref[...]
    basis_r = basis_r_ref[...]
    left_new = BETA_TWO * left_ref[...] + (1.0 - BETA_TWO) * exact(grad, grad, ((1,), (1,)))
    right_new = BETA_TWO * right_ref[...] + (1.0 - BETA_TWO) * exact(grad, grad, ((0,), (0,)))
    both = orthonormal_pair(
        jnp.concatenate([exact(left_new, basis_l), exact(right_new, basis_r)], 1), both_ref
    )
    basis_l_new = both[:, 0:C1]
    basis_r_new = both[:, C1 : 2 * C1]
    rotated = exact(exact(basis_l, grad, ((0,), (0,))), basis_r)
    first_new = BETA_ONE * first_ref[...] + (1.0 - BETA_ONE) * rotated
    second_new = BETA_TWO * second_ref[...] + (1.0 - BETA_TWO) * rotated * rotated
    scaled = first_new / one_scale / (jnp.sqrt(second_new / two_scale) + ADAM_EPS)
    weight = weight_ref[...]
    weight_new = weight - LEARN_RATE * (
        exact(exact(basis_l, scaled), basis_r, ((1,), (1,))) + WEIGHT_DECAY * weight
    )
    plain = exact(exact(basis_l, first_new), basis_r, ((1,), (1,)))
    first_rotated = exact(exact(basis_l_new, plain, ((0,), (0,))), basis_r_new)
    average_new = EMA_KEEP * average_ref[...] + (1.0 - EMA_KEEP) * weight_new
    held = owned > 0.5
    weight_out[...] = jnp.where(held, weight_new, 0.0)
    first_out[...] = jnp.where(held, first_rotated, 0.0)
    second_out[...] = jnp.where(held, second_new, 0.0)
    left_out[...] = jnp.where(held, left_new, 0.0)
    right_out[...] = jnp.where(held, right_new, 0.0)
    basis_l_out[...] = jnp.where(held, basis_l_new, 0.0)
    basis_r_out[...] = jnp.where(held, basis_r_new, 0.0)
    average_out[...] = jnp.where(held, average_new, 0.0)


def local(
    points,
    route,
    labels,
    interp_src,
    pool_nbr,
    sample,
    coarse_nbr,
    owner,
    step,
    flat,
    flat_mom,
    flat_sec,
    flat_ema,
    mats,
    mats_mom,
    mats_sec,
    mats_left,
    mats_right,
    mats_basis_l,
    mats_basis_r,
    mats_ema,
):
    n_pts = lax.axis_size("pts")
    n_sub = lax.axis_size("sub")
    fine = points.shape[0]
    coarse = sample.shape[0]
    cap = n_sub * fine // n_pts
    slots = n_pts * cap
    sources = n_sub * n_pts
    half = coarse // n_sub
    edges = NEIGH * half
    parts = coarse // LOW_B
    my_parts = parts // n_sub
    vmem = pl.BlockSpec(memory_space=pltpu.VMEM)
    smem = pl.BlockSpec(memory_space=pltpu.SMEM)
    dma = pltpu.SemaphoreType.DMA
    scratch = [
        VMEM((6, fine), BF16),
        VMEM((1, fine), I32),
        VMEM((1, fine), I32),
        VMEM((3, fine), I32),
        VMEM((NEIGH, coarse), I32),
        VMEM((1, coarse), I32),
        VMEM((NEIGH, coarse), I32),
        pltpu.SMEM((NMATS,), I32),
        VMEM((C1, C1), F32),
        VMEM((FLAT,), F32),
        VMEM((FLAT_ROWS, LANES), F32),
        VMEM((16, fine), F32),
        VMEM((n_pts * 16, cap), F32),
        VMEM((n_pts, 16, cap), BF16),
        VMEM((sources, 16, cap), BF16),
        VMEM((32, LANES), BF16),
        VMEM((n_pts, 32, LANES), BF16),
        VMEM((sources * 8, cap), BF16),
        VMEM((8, coarse), F32),
        VMEM((C1, edges), F32),
        VMEM((48, edges), BF16),
        VMEM((C1, half), F32),
        VMEM((C1, half), F32),
        VMEM((parts, CH, LOW_B), BF16),
        VMEM((parts, CH, LOW_B), BF16),
        VMEM((C1, edges), BF16),
        VMEM((144, edges), BF16),
        VMEM((144, edges), BF16),
        VMEM((LOW_B, edges), BF16),
        VMEM((C1, edges), F32),
        VMEM((GROUPS, edges), F32),
        VMEM((C1, half), F32),
        VMEM((C1, half), F32),
        VMEM((16, slots), F32),
        VMEM((80, slots), BF16),
        VMEM((80, slots), BF16),
        VMEM((C0, slots), F32),
        VMEM((3, LOW_B, slots), BF16),
        VMEM((3, C1, slots), BF16),
        VMEM((8, slots), F32),
        VMEM((parts, C0, LOW_B), F32),
        VMEM((my_parts, C0, LOW_B), F32),
        VMEM((parts, C1 + 8, LOW_B), F32),
        VMEM((my_parts, C1 + 8, LOW_B), F32),
        VMEM((LANES, LANES), F32),
        VMEM((LANES, LANES), F32),
        VMEM((LANES, LANES), F32),
        VMEM((LANES, LANES), F32),
        VMEM((LANES, LANES), F32),
        VMEM((LANES, LANES), F32),
        VMEM((LANES, LANES), F32),
        VMEM((LANES, LANES), F32),
        VMEM((LANES, LANES), F32),
        VMEM((80, LANES), F32),
        VMEM((48, LANES), F32),
        VMEM((144, LANES), F32),
        VMEM((144, LANES), F32),
        VMEM((144, LANES), F32),
        VMEM((256, LANES), F32),
        VMEM((128, LANES), F32),
        VMEM((128, LANES), F32),
        VMEM((n_pts, 8, LANES), F32),
        VMEM((256, LANES), F32),
        dma((n_pts,)),
        dma((n_pts,)),
        dma((n_pts,)),
        dma((n_pts,)),
        dma((n_pts,)),
        dma((n_pts,)),
        dma((n_pts,)),
        dma((n_pts,)),
        dma((8,)),
        dma((8,)),
        dma((10,)),
    ]
    reduced = pl.pallas_call(
        functools.partial(main_kernel, n_pts, n_sub),
        out_shape=jax.ShapeDtypeStruct((256, LANES), F32),
        in_specs=[pl.BlockSpec(memory_space=pltpu.HBM)] * 10,
        out_specs=vmem,
        scratch_shapes=scratch,
        compiler_params=pltpu.CompilerParams(
            collective_id=0, has_side_effects=True, vmem_limit_bytes=60 * 1024 * 1024
        ),
    )(
        points.T,
        route.reshape(1, fine),
        labels.reshape(1, fine),
        interp_src.T,
        pool_nbr.T,
        sample.reshape(1, coarse),
        coarse_nbr.T,
        owner,
        mats[0],
        flat,
    )
    square = jax.ShapeDtypeStruct((C1, C1), F32)
    line = jax.ShapeDtypeStruct((FLAT,), F32)
    single = jax.ShapeDtypeStruct((1, 1), F32)
    results = pl.pallas_call(
        soap_kernel,
        out_shape=[square] * 8 + [line] * 4 + [single] * 2,
        in_specs=[vmem] + [smem] * 2 + [vmem] * 12,
        out_specs=[vmem] * 14,
        scratch_shapes=[VMEM((C1, 2 * C1), F32)],
    )(
        reduced,
        owner,
        step,
        mats[0],
        mats_mom[0],
        mats_sec[0],
        mats_left[0],
        mats_right[0],
        mats_basis_l[0],
        mats_basis_r[0],
        mats_ema[0],
        flat,
        flat_mom,
        flat_sec,
        flat_ema,
    )
    scalars = (results[12].reshape(()), results[13].reshape(()))
    return scalars + tuple(results[8:12]) + tuple(result[None] for result in results[:8])


def solution(mesh):
    placed = (
        P(("pts", "sub"), None),
        P(("pts", "sub")),
        P(("pts", "sub")),
        P(("pts", "sub"), None),
        P("pts", None),
        P("pts"),
        P("pts", None),
        P(),
        P(),
        P(),
        P(),
        P(),
        P(),
    ) + (P("pts", None, None),) * 8
    mapped = jax.shard_map(
        local,
        mesh=mesh,
        in_specs=placed,
        out_specs=(P(),) * 6 + (P("pts", None, None),) * 8,
        check_vma=False,
    )

    def run(*arrays):
        with jax.sharding.use_abstract_mesh(mesh.abstract_mesh):
            return mapped(*arrays)

    return run
```

```python
import functools
import math

import jax
import jax.numpy as jnp
from jax import lax
from jax.experimental import pallas as pl
from jax.experimental.pallas import tpu as pltpu
from jax.sharding import PartitionSpec as P

C0 = 32
C1 = 64
NEIGH = 16
NCLS = 13
GROUPS = 8
NMATS = 5

HIGHEST = lax.Precision.HIGHEST
CLIP_NORM = 0.01
BETA_ONE = 0.9
BETA_TWO = 0.95
ADAM_EPS = 1e-08
LEARN_RATE = 0.1
WEIGHT_DECAY = 0.01
EMA_KEEP = 0.9
INTERP_EPS = 0.01

F32 = jnp.float32
BF16 = jnp.bfloat16
I32 = jnp.int32
MESH = pl.DeviceIdType.MESH
VMEM = pltpu.VMEM

LANES = 128
FLAT_ROWS = 64
LOW_B = 256
CH = 72
NEG = -1e30


def offsets():
    shapes = [
        ("w_stem", (6, C0)),
        ("b_stem", (C0,)),
        ("w_down", (3 + C0, C1)),
        ("b_down", (C1,)),
        ("w_pos", (3, C1)),
        ("b_pos", (C1,)),
        ("w_att1", (C1, GROUPS)),
        ("b_att1", (GROUPS,)),
        ("w_att2", (GROUPS, GROUPS)),
        ("b_att2", (GROUPS,)),
        ("w_up", (C1, C0)),
        ("b_up", (C0,)),
        ("w_skip", (C0, C0)),
        ("w_head", (C0, NCLS)),
        ("b_head", (NCLS,)),
    ]
    found = {}
    total = 0
    for name, shape in shapes:
        found[name] = total
        total += math.prod(shape)
    return found, total


OFF, FLAT = offsets()


def dot(left, right):
    return lax.dot_general(left, right, (((1,), (0,)), ((), ())), preferred_element_type=F32)


def dot_nt(left, right):
    return lax.dot_general(left, right, (((1,), (1,)), ((), ())), preferred_element_type=F32)


def exact(left, right, dims=((1,), (0,))):
    return lax.dot_general(
        left, right, (dims, ((), ())), precision=HIGHEST, preferred_element_type=F32
    )


def relu(values):
    return jnp.maximum(values, 0.0)


def rows_of(count, length):
    return lax.broadcasted_iota(I32, (count, length), 0)


def lanes_of(count, length):
    return lax.broadcasted_iota(I32, (count, length), 1)


def onehot(low, count):
    hit = rows_of(count, low.shape[1]) == low
    return jnp.where(hit, 1.0, 0.0).astype(BF16)


def stored_onehot(low, iota):
    count, length = iota.shape[0], low.shape[1]
    wanted = jnp.broadcast_to(low.astype(F32), (16, length)).astype(BF16)
    held = jnp.concatenate([iota] * (length // LANES), 1).reshape(count // 16, 16, length)
    hit = held == wanted[None]
    return jnp.where(hit, jnp.ones((), BF16), jnp.zeros((), BF16)).reshape(count, length)


def pick(spread, high, parts):
    each = spread.shape[0] // parts
    found = spread[0:each]
    for part in range(1, parts):
        found = jnp.where(high == part, spread[part * each : (part + 1) * each], found)
    return found


def place(values, high, parts):
    return jnp.concatenate(
        [jnp.where(high == part, values, 0.0) for part in range(parts)], 0
    ).astype(BF16)


def unpack(flat_ref, out_ref, offset, rows, width, at):
    stride = LANES // width if LANES % width == 0 else rows
    for first in range(min(stride, rows)):
        count = (rows - first + stride - 1) // stride
        padded = -(-count // 8) * 8
        line, lane = divmod(offset + first * width, LANES)
        values = flat_ref[line : line + padded, :]
        if lane:
            values = pltpu.roll(values, LANES - lane, 1)
        if lane + width > LANES:
            following = pltpu.roll(flat_ref[line + 1 : line + 1 + padded, :], LANES - lane, 1)
            values = jnp.where(lanes_of(padded, LANES) < LANES - lane, values, following)
        values = jnp.where(lanes_of(padded, LANES) < width, values, 0.0)
        if count == 1:
            out_ref[at + first : at + first + 1, :] = values[0:1]
        else:
            out_ref[pl.ds(at + first, count, stride=stride), :] = values[0:count]


def pack(out_ref, base, source_ref, row, lane_from, offset, rows, width):
    stride = LANES // width if LANES % width == 0 else rows
    for first in range(min(stride, rows)):
        count = (rows - first + stride - 1) // stride
        line, lane = divmod(offset + first * width, LANES)
        if count == 1:
            values = source_ref[row + first : row + first + 1, :]
        else:
            values = source_ref[pl.ds(row + first, count, stride=stride), :]
        shift = (lane - lane_from) % LANES
        padded = -(-count // 8) * 8
        if padded != count:
            values = jnp.concatenate([values, jnp.zeros((padded - count, LANES), F32)], 0)
        if shift:
            values = pltpu.roll(values, shift, 1)
        values = values[0:count]
        at = lanes_of(count, LANES)
        here = jnp.where((at >= lane) & (at < lane + width), values, 0.0)
        out_ref[base + line : base + line + count, :] += here
        if lane + width > LANES:
            there = jnp.where(at < lane + width - LANES, values, 0.0)
            out_ref[base + line + 1 : base + line + 1 + count, :] += there


def main_kernel(
    n_pts,
    n_sub,
    pts_hbm,
    route_hbm,
    labels_hbm,
    src_hbm,
    pool_hbm,
    sample_hbm,
    cnbr_hbm,
    owner_hbm,
    mats_hbm,
    flat_hbm,
    out_ref,
    pts_ref,
    route_ref,
    labels_ref,
    src_ref,
    pool_ref,
    sample_ref,
    cnbr_ref,
    owner_ref,
    mats_ref,
    flat_line,
    flat_ref,
    iota_ref,
    data,
    sacc,
    sendb,
    recv,
    matmine,
    matall,
    tabb,
    cen,
    pin,
    cat,
    pooled_ref,
    rsum_ref,
    ctab,
    btab,
    near,
    est,
    gst,
    ohs,
    car,
    sc,
    mixed_ref,
    blk_ref,
    slot,
    fin,
    fgr,
    skp,
    foh,
    fsrc,
    fwt,
    dcp,
    dcr,
    dkp,
    dkr,
    wst,
    wd,
    wp,
    w1,
    w2,
    wu,
    wsk,
    wh,
    bias,
    ga,
    gb,
    gc,
    gd,
    ge,
    gbuf,
    gsib,
    ghalf,
    gsh,
    gfull,
    a2a_send,
    a2a_recv,
    mat_send,
    mat_recv,
    red_send,
    red_recv,
    gat_send,
    gat_recv,
    sib_send,
    sib_recv,
    load_sem,
):
    fine = route_ref.shape[1]
    coarse = sample_ref.shape[1]
    cap = sendb.shape[2]
    slots = n_pts * cap
    half = coarse // n_sub
    edges = NEIGH * half
    sources = n_sub * n_pts
    parts = coarse // LOW_B
    my_parts = parts // n_sub
    shift = cap.bit_length() - 1
    low_shift = LOW_B.bit_length() - 1
    span = 512
    me = lax.axis_index("pts")
    sub = lax.axis_index("sub")
    half_at = pl.multiple_of(sub * half, half)

    far_refs = (pts_hbm, route_hbm, labels_hbm, src_hbm, mats_hbm, sample_hbm, pool_hbm, cnbr_hbm, owner_hbm)
    near_refs = (pts_ref, route_ref, labels_ref, src_ref, mats_ref, sample_ref, pool_ref, cnbr_ref, owner_ref)
    loads = [
        pltpu.make_async_copy(source, target, load_sem.at[number])
        for number, (source, target) in enumerate(zip(far_refs, near_refs))
    ]
    loads.append(
        pltpu.make_async_copy(flat_hbm, flat_line, load_sem.at[len(loads)])
    )
    for load in loads:
        load.start()

    barrier = pltpu.get_barrier_semaphore()

    powers = [2**k for k in range(n_pts.bit_length() - 1)]
    my_bits = [lax.bitwise_and(lax.shift_right_logical(me, k), 1) for k in range(len(powers))]

    def partner(step):
        step = n_pts - step
        found = 0
        for k, power in enumerate(powers):
            bit = lax.bitwise_and(my_bits[k] + lax.shift_right_logical(step, k), 1)
            found = found + power * bit
        return found

    def greet(step, carry):
        peer = partner(step)
        pl.semaphore_signal(barrier, inc=1, device_id={"pts": peer}, device_id_type=MESH)
        return carry

    lax.fori_loop(1, n_pts, greet, 0)
    pl.semaphore_signal(barrier, inc=1, device_id={"sub": 1 - sub}, device_id_type=MESH)

    def sibling(number, source, target):
        return pltpu.make_async_remote_copy(
            src_ref=source,
            dst_ref=target,
            send_sem=sib_send.at[number],
            recv_sem=sib_recv.at[number],
            device_id={"sub": 1 - sub},
            device_id_type=MESH,
        )

    iota_ref[...] = rows_of(LOW_B, LANES).astype(F32).astype(BF16)
    for load in loads[0:5] + loads[9:]:
        load.wait()
    data[0:6, :] = pts_ref[...].astype(F32)
    data[6:8, :] = jnp.zeros((2, fine), F32)
    source_rows = src_ref[...]
    data[8:11, :] = lax.shift_right_logical(source_rows, 5).astype(F32)
    data[11:14, :] = (source_rows & 31).astype(F32)
    data[14:15, :] = (labels_ref[...] + 1).astype(F32)
    data[15:16, :] = jnp.zeros((1, fine), F32)
    sacc[...] = jnp.zeros_like(sacc)
    counts = jnp.zeros((16, 32), F32)
    for chunk in range(fine // span):
        lanes = slice(chunk * span, (chunk + 1) * span)
        route = route_ref[:, lanes]
        high = lax.shift_right_logical(route, shift)
        spread = place(data[:, lanes], high, n_pts)
        sacc[...] += dot_nt(spread, onehot(route & (cap - 1), cap))
        classes = onehot(labels_ref[:, lanes], 16)
        counts = counts + dot_nt(jnp.ones((16, span), BF16), jnp.concatenate([classes, classes], 0))
    count_high = jnp.floor(counts * (1.0 / 128.0))
    count_low = counts - 128.0 * count_high
    digits = jnp.where(lanes_of(16, 32) < 16, count_low, count_high)
    digits = jnp.where(rows_of(16, 32) == 15, digits, 0.0)
    data[:, 0:cap] = jnp.zeros((16, cap), F32)
    data[:, 0:32] = digits
    sendb[...] = (sacc[...].reshape(n_pts, 16, cap) + data[:, 0:cap][None]).astype(BF16)
    matrix = mats_ref[...]
    matmine[...] = jnp.concatenate([matrix[0:32], matrix[32:64]], 1).astype(BF16)

    pl.semaphore_wait(barrier, n_pts)

    def block_copy(peer, index):
        return pltpu.make_async_remote_copy(
            src_ref=sendb.at[peer],
            dst_ref=recv.at[sub * n_pts + index],
            send_sem=a2a_send.at[peer],
            recv_sem=a2a_recv.at[index],
            device_id={"pts": peer},
            device_id_type=MESH,
        )

    def mat_copy(peer, index):
        return pltpu.make_async_remote_copy(
            src_ref=matmine,
            dst_ref=matall.at[index],
            send_sem=mat_send.at[peer],
            recv_sem=mat_recv.at[index],
            device_id={"pts": peer},
            device_id_type=MESH,
        )

    def send_blocks(step, carry):
        block_copy(partner(step), me).start()
        return carry

    def send_mats(step, carry):
        mat_copy(partner(step), me).start()
        return carry

    lax.fori_loop(1, n_pts, send_blocks, 0)
    recv[sub * n_pts + me] = sendb[me]
    matall[me] = matmine[...]

    for ref in (wst, wd, wp, w1, w2, wu, wsk, wh, bias):
        ref[...] = jnp.zeros_like(ref)
    padded = jnp.pad(flat_line[...], (0, FLAT_ROWS * LANES - FLAT))
    flat_ref[...] = padded.reshape(FLAT_ROWS, LANES)
    unpack(flat_ref, wst, OFF["w_stem"], 6, C0, 0)
    unpack(flat_ref, wd, OFF["w_down"], 3, C1, 0)
    unpack(flat_ref, wd, OFF["w_down"] + 3 * C1, C0, C1, 16)
    unpack(flat_ref, wp, OFF["w_pos"], 3, C1, 8)
    unpack(flat_ref, w1, OFF["w_att1"], C1, GROUPS, 0)
    unpack(flat_ref, w2, OFF["w_att2"], GROUPS, GROUPS, 0)
    unpack(flat_ref, wu, OFF["w_up"], C1, C0, 0)
    unpack(flat_ref, wsk, OFF["w_skip"], C0, C0, 0)
    unpack(flat_ref, wh, OFF["w_head"], C0, NCLS, 0)
    names = ("b_stem", "b_down", "b_pos", "b_att1", "b_att2", "b_up", "b_head")
    widths = (C0, C1, C1, GROUPS, GROUPS, C0, NCLS)
    for position, (name, width) in enumerate(zip(names, widths)):
        unpack(flat_ref, bias, OFF[name], 1, width, position)
    columns = bias[...].T
    b_stem = columns[0:C0, 0:1]
    b_down = columns[0:C1, 1:2]
    b_pos = columns[0:C1, 2:3]
    b_att1 = columns[0:GROUPS, 3:4]
    b_att2 = columns[0:GROUPS, 4:5]
    b_up = columns[0:C0, 5:6]
    b_head = jnp.where(rows_of(16, 1) < NCLS, columns[0:16, 6:7], NEG)
    w_stem_t = wst[...].T[0:C0, 0:16].astype(BF16)
    w_down_t = wd[...].T[0:C1, 0:48].astype(BF16)
    w_pos_t = wp[...].T[0:C1, 0:16].astype(BF16)
    w_att1_t = w1[...].T[0:GROUPS, 0:C1].astype(BF16)
    w_att2_t = w2[...].T[0:GROUPS, 0:16].astype(BF16)
    w_up_t = wu[...].T[0:C0, 0:C1].astype(BF16)
    w_skip_t = wsk[...].T[0:C0, 0:C0].astype(BF16)
    w_head_t = wh[...].T[0:16, 0:C0].astype(BF16)
    w_down_stem = wd[16:48, 0:C1].astype(BF16)
    w_att1 = w1[0:C1, 0:16].astype(BF16)
    w_att2 = w2[0:GROUPS, 0:16].astype(BF16)
    w_up = wu[0:C1, 0:C0].astype(BF16)
    w_skip = wsk[0:C0, 0:C0].astype(BF16)
    w_head = wh[0:C0, 0:16].astype(BF16)

    def wait_blocks(step, carry):
        peer = partner(step)
        block_copy(peer, peer).wait_recv()
        return carry

    lax.fori_loop(1, n_pts, wait_blocks, 0)
    lax.fori_loop(1, n_pts, send_mats, 0)
    for load in loads[5:9]:
        load.wait()
    mine = recv.at[pl.ds(sub * n_pts, n_pts)]
    forward = sibling(0, mine, mine)
    forward.start()
    for source in range(n_pts):
        slot[:, source * cap : (source + 1) * cap] = recv[sub * n_pts + source].astype(F32)
    forward.wait_recv()

    table = recv[...].astype(F32)[:, 0:8, :].reshape(sources * 8, cap)
    ones_row = (rows_of(sources * 8, cap) & 7) == 7
    tabb[...] = jnp.where(ones_row, 1.0, table).astype(BF16)
    count_row = jnp.sum(recv[...].astype(F32)[:, 8:16, :], axis=0)[7:8, 0:32]
    count_at = jnp.broadcast_to(count_row, (16, 32))
    low_hit = lanes_of(16, 32) == rows_of(16, 32)
    high_hit = lanes_of(16, 32) == rows_of(16, 32) + 16
    class_counts = jnp.sum(
        jnp.where(low_hit, count_at, 0.0) + jnp.where(high_hit, 128.0 * count_at, 0.0),
        axis=1,
        keepdims=True,
    )
    total_fine = float(fine * n_pts * n_sub)
    class_w = jnp.where(
        rows_of(16, 1) < NCLS, total_fine / (NCLS * class_counts) * (1.0 / total_fine), 0.0
    )

    def gather_points(index):
        hot = onehot(index & (cap - 1), cap)
        high = jnp.broadcast_to(lax.shift_right_logical(index, shift), (8, index.shape[1]))
        return pick(dot(tabb[...], hot), high, sources)

    zeros8 = jnp.zeros((8, span), F32)
    for chunk in range(coarse // span):
        lanes = slice(chunk * span, (chunk + 1) * span)
        found = gather_points(sample_ref[:, lanes])
        cen[:, lanes] = jnp.where(rows_of(8, span) < 6, found, 0.0)
    centre = cen[:, pl.ds(half_at, half)]
    centre_low = jnp.concatenate([centre, zeros8], 0).astype(BF16)
    w_xyz_t = jnp.where(lanes_of(C1, 16) < 3, wd[...].T[0:C1, 0:16], 0.0).astype(BF16)
    pool_base = b_down - dot(w_xyz_t, centre_low)

    def at_edge(k):
        return pl.ds(pl.multiple_of(k * half, half), half)

    def every_edge(step, unroll):
        def run(k, carry):
            step(k, at_edge(k))
            return carry

        lax.fori_loop(0, NEIGH, run, 0, unroll=unroll)

    def pool_gather(k, lanes):
        found = gather_points(pool_ref[pl.ds(k, 1), pl.ds(half_at, half)])
        cat[0:16, lanes] = jnp.concatenate([found, zeros8], 0).astype(BF16)

    def pool_stem(k, lanes):
        cat[16:48, lanes] = relu(dot(w_stem_t, cat[0:16, lanes]) + b_stem).astype(BF16)

    def pool_project(k, lanes):
        pin[:, lanes] = dot(w_down_t, cat[:, lanes]).astype(BF16).astype(F32) + pool_base

    every_edge(pool_gather, 4)
    every_edge(pool_stem, 16)
    every_edge(pool_project, 16)

    def tree(combine, values):
        while len(values) > 1:
            paired = [combine(values[i], values[i + 1]) for i in range(0, len(values) - 1, 2)]
            values = paired + ([values[-1]] if len(values) % 2 else [])
        return values[0]

    wide = 256

    def log_sum(r, carry):
        rows = pl.ds(pl.multiple_of(r * 8, 8), 8)
        for start in range(0, half, wide):
            spots = [slice(k * half + start, k * half + start + wide) for k in range(NEIGH)]
            values = [pin[rows, spot] for spot in spots]
            most = tree(jnp.maximum, values)
            values = [jnp.exp(value - most) for value in values]
            for spot, value in zip(spots, values):
                pin[rows, spot] = value
            total = tree(jnp.add, values)
            pooled_ref[rows, start : start + wide] = most + jnp.log(total)
            rsum_ref[rows, start : start + wide] = 1.0 / total
        return carry

    lax.fori_loop(0, C1 // 8, log_sum, 0, unroll=2)

    def table_rows(values, target):
        rows = []
        for part in range(my_parts):
            lanes = slice(part * LOW_B, (part + 1) * LOW_B)
            rows = rows + [values[:, lanes], centre[:, lanes]]
        target[sub] = jnp.concatenate(rows, 0).astype(BF16)

    table_rows(pooled_ref[...], ctab)
    my_ctab = ctab.at[sub]
    give_pooled = sibling(1, my_ctab, my_ctab)
    give_pooled.start()

    def wait_mats(step, carry):
        peer = partner(step)
        mat_copy(peer, peer).wait_recv()
        return carry

    lax.fori_loop(1, n_pts, wait_mats, 0)

    def layer(position):
        folded = matall[owner_ref[position]].astype(F32)
        return jnp.concatenate([folded[:, 0:C1], folded[:, C1 : 2 * C1]], 0)

    w_query, w_key, w_value, w_pos2_32, w_out_32 = [layer(position) for position in range(NMATS)]
    w_qkv = jnp.concatenate([w_query, w_key, w_value], 1).astype(BF16)
    w_query_t = w_query.T.astype(BF16)
    w_pos2 = w_pos2_32.astype(BF16)
    w_pos2_t = w_pos2_32.T
    w_edge_t = jnp.concatenate(
        [
            jnp.concatenate([-w_key.T, w_pos2_t], 1),
            jnp.concatenate([w_value.T, w_pos2_t], 1),
        ],
        0,
    ).astype(BF16)
    w_out = w_out_32.astype(BF16)
    w_out_t = w_out_32.T.astype(BF16)
    queries = dot(w_query_t, pooled_ref[...].astype(BF16))

    def at_slot(step):
        return pl.ds(pl.multiple_of(step * span, span), span)

    def every_slot(step, unroll):
        def run(j, carry):
            step(j, at_slot(j))
            return carry

        lax.fori_loop(0, slots // span, run, 0, unroll=unroll)

    def fine_points(j, lanes):
        ones = jnp.where(rows_of(8, span) == 7, 1.0, slot[0:8, lanes])
        fin[0:16, lanes] = jnp.concatenate([ones, zeros8], 0).astype(BF16)

    def fine_stem(j, lanes):
        fin[16:48, lanes] = relu(dot(w_stem_t, fin[0:16, lanes]) + b_stem).astype(BF16)

    def fine_skip(j, lanes):
        skp[:, lanes] = dot(w_skip_t, fin[16:48, lanes])

    every_slot(fine_points, 4)
    every_slot(fine_stem, 8)
    every_slot(fine_skip, 8)
    give_pooled.wait_recv()

    def attend_gather(k, lanes):
        index = cnbr_ref[pl.ds(k, 1), pl.ds(half_at, half)]
        hot = stored_onehot(index & (LOW_B - 1), iota_ref[...])
        ohs[:, lanes] = hot
        high = lax.shift_right_logical(index, low_shift)
        found = pick(dot(ctab[...].reshape(parts * CH, LOW_B), hot), high, parts)
        near[:, lanes] = found[0:C1].astype(BF16)
        offset = jnp.where(rows_of(8, half) == 7, 1.0, centre - found[C1 : C1 + 8])
        est[128:144, lanes] = jnp.concatenate([zeros8, offset], 0).astype(BF16)

    def attend_pos(k, lanes):
        est[64:128, lanes] = relu(dot(w_pos_t, est[128:144, lanes]) + b_pos).astype(BF16)

    def attend_edge(k, lanes):
        both = dot(w_edge_t, jnp.concatenate([near[:, lanes], est[64:128, lanes]], 0))
        est[0:64, lanes] = (queries + both[0:C1]).astype(BF16)
        car[:, lanes] = both[C1 : 2 * C1]

    def attend_act(k, lanes):
        act = relu(dot(w_att1_t, est[0:64, lanes]) + b_att1)
        offset = est[128:144, lanes].astype(F32)[8:16]
        est[128:144, lanes] = jnp.concatenate([act, offset], 0).astype(BF16)

    def attend_score(k, lanes):
        sc[:, lanes] = dot(w_att2_t, est[128:144, lanes]) + b_att2

    every_edge(attend_gather, 16)
    every_edge(attend_pos, 16)
    every_edge(attend_edge, 16)
    every_edge(attend_act, 16)
    every_edge(attend_score, 16)

    for start in range(0, half, wide):
        spots = [slice(k * half + start, k * half + start + wide) for k in range(NEIGH)]
        values = [sc[:, spot] for spot in spots]
        most = tree(jnp.maximum, values)
        values = [jnp.exp(value - most) for value in values]
        scale = 1.0 / tree(jnp.add, values)
        for spot, value in zip(spots, values):
            sc[:, spot] = value * scale

    for g in range(GROUPS):
        rows = slice(8 * g, 8 * g + 8)
        for start in range(0, half, wide):
            spots = [slice(k * half + start, k * half + start + wide) for k in range(NEIGH)]
            terms = [
                jnp.broadcast_to(sc[g : g + 1, spot], (8, wide)) * car[rows, spot]
                for spot in spots
            ]
            mixed_ref[rows, start : start + wide] = tree(jnp.add, terms)

    block = pooled_ref[...] + dot(w_out_t, mixed_ref[...].astype(BF16))
    blk_ref[...] = block
    table_rows(block, btab)
    my_btab = btab.at[sub]
    give_block = sibling(2, my_btab, my_btab)
    give_block.start()

    def source_of(lanes, i):
        index = (32.0 * slot[8 + i : 9 + i, lanes] + slot[11 + i : 12 + i, lanes]).astype(I32)
        return index & (LOW_B - 1), lax.shift_right_logical(index, low_shift)

    def fine_hot(j, lanes):
        for i in range(3):
            foh[i, :, lanes] = stored_onehot(source_of(lanes, i)[0], iota_ref[...])

    every_slot(fine_hot, 2)
    give_block.wait_recv()

    def fine_gather(j, lanes):
        points = slot[0:8, lanes]
        inverses = []
        for i in range(3):
            high = source_of(lanes, i)[1]
            found = pick(dot(btab[...].reshape(parts * CH, LOW_B), foh[i, :, lanes]), high, parts)
            fsrc[i, :, lanes] = found[0:C1].astype(BF16)
            diff = jnp.where(rows_of(8, span) < 3, points - found[C1 : C1 + 8], 0.0)
            inverses.append(1.0 / (jnp.sum(diff * diff, axis=0, keepdims=True) + INTERP_EPS))
        norm = 1.0 / (inverses[0] + inverses[1] + inverses[2])
        for i in range(3):
            fwt[i : i + 1, lanes] = inverses[i] * norm

    def fine_join(j, lanes):
        terms = [fwt[i : i + 1, lanes] * dot(w_up_t, fsrc[i, :, lanes]) for i in range(3)]
        interp = (terms[0] + terms[1] + terms[2] + b_up).astype(BF16).astype(F32)
        fin[48:80, lanes] = relu(interp + skp[:, lanes]).astype(BF16)

    def fine_loss(j, loss):
        lanes = at_slot(j)
        logits = dot(w_head_t, fin[48:80, lanes]) + b_head
        label = slot[14:15, lanes].astype(I32)
        hit = jnp.where(rows_of(16, span) + 1 == label, 1.0, 0.0)
        row_w = jnp.sum(hit * class_w, axis=0, keepdims=True)
        peak = jnp.max(logits, axis=0, keepdims=True)
        raised = jnp.exp(logits - peak)
        total = jnp.sum(raised, axis=0, keepdims=True)
        named = jnp.sum(hit * logits, axis=0, keepdims=True)
        fgr[64:80, lanes] = (row_w * (raised * (1.0 / total) - hit)).astype(BF16)
        return loss + row_w * (peak + jnp.log(total) - named)

    def fine_fused(j, lanes):
        kept = fin[48:80, lanes].astype(F32) > 0
        fgr[0:32, lanes] = jnp.where(kept, dot(w_head, fgr[64:80, lanes]), 0.0).astype(BF16)

    def fine_scatter(j, lanes):
        dfused = fgr[0:32, lanes].astype(F32)
        total = 0.0
        for i in range(3):
            spread = place(fwt[i : i + 1, lanes] * dfused, source_of(lanes, i)[1], parts)
            total = total + dot_nt(spread, foh[i, :, lanes])
        dcp[...] += total.reshape(parts, C0, LOW_B)

    def fine_back(j, lanes):
        kept = fin[16:48, lanes].astype(F32) > 0
        fgr[32:64, lanes] = jnp.where(kept, dot(w_skip, fgr[0:32, lanes]), 0.0).astype(BF16)

    every_slot(fine_gather, 8)
    every_slot(fine_join, 8)
    loss = lax.fori_loop(0, slots // span, fine_loss, jnp.zeros((1, span), F32), unroll=4)
    every_slot(fine_fused, 8)
    dcp[...] = jnp.zeros_like(dcp)
    every_slot(fine_scatter, 4)

    other = (1 - sub) * my_parts
    own = sub * my_parts
    give_dup = sibling(3, dcp.at[pl.ds(other, my_parts)], dcr)
    give_dup.start()
    every_slot(fine_back, 8)
    ga[...] = jnp.zeros_like(ga)
    for start in range(0, slots, 4 * span):
        lanes = slice(start, start + 4 * span)
        ga[:, 0:80] += dot_nt(fin[:, lanes], fgr[:, lanes])
    give_dup.wait_recv()

    def own_half(partial, received):
        return jnp.concatenate(
            [partial[own + part] + received[part] for part in range(my_parts)], 1
        )

    dup_low = own_half(dcp, dcr).astype(BF16)
    dblock = dot(w_up, dup_low)
    dbranch_low = dblock.astype(BF16)
    dmixed = dot(w_out, dbranch_low)

    def group_sum(values):
        return jnp.concatenate(
            [
                jnp.sum(values[8 * g : 8 * g + 8], axis=0, keepdims=True)
                for g in range(GROUPS)
            ],
            0,
        )

    def expand(values):
        return jnp.concatenate(
            [jnp.broadcast_to(values[g : g + 1], (8, values.shape[1])) for g in range(GROUPS)], 0
        )

    centred = group_sum(dmixed * mixed_ref[...])

    def back_score(k, lanes):
        ds2 = sc[:, lanes] * (group_sum(dmixed * car[:, lanes]) - centred)
        gst[128:144, lanes] = jnp.concatenate([ds2, zeros8], 0).astype(BF16)

    def back_act(k, lanes):
        scores = gst[128:144, lanes]
        kept = est[128:144, lanes].astype(F32)[0:8] > 0
        ds1 = jnp.where(kept, dot(w_att2, scores), 0.0)
        ds2 = scores.astype(F32)[0:8]
        gst[128:144, lanes] = jnp.concatenate([ds1, ds2], 0).astype(BF16)

    def back_edge(k, lanes):
        small = gst[128:144, lanes]
        dcarried = expand(sc[:, lanes]) * dmixed
        gst[64:128, lanes] = (dot(w_att1, small) + dcarried).astype(BF16)
        index = cnbr_ref[pl.ds(k, 1), pl.ds(half_at, half)]
        high = lax.shift_right_logical(index, low_shift)
        spread = place(jnp.concatenate([dcarried, small.astype(F32)[0:8]], 0), high, parts)
        dkp[...] += dot_nt(spread, ohs[:, lanes]).reshape(parts, C1 + 8, LOW_B)

    def back_pos(k, lanes):
        kept = est[64:128, lanes].astype(F32) > 0
        gst[0:64, lanes] = jnp.where(kept, dot(w_pos2, gst[64:128, lanes]), 0.0).astype(BF16)

    every_edge(back_score, 16)
    every_edge(back_act, 16)
    dkp[...] = jnp.zeros_like(dkp)
    every_edge(back_edge, 16)
    give_dkv = sibling(4, dkp.at[pl.ds(other, my_parts)], dkr)
    give_dkv.start()
    every_edge(back_pos, 16)
    inputs = jnp.concatenate(
        [blk_ref[...].astype(BF16), mixed_ref[...].astype(BF16), jnp.ones((16, half), BF16)], 0
    )
    grads = jnp.concatenate([dup_low, jnp.zeros((C0, half), BF16), dbranch_low], 0)
    gd[...] = dot_nt(inputs, grads)
    gc[...] = jnp.zeros_like(gc)
    ge[...] = jnp.zeros_like(ge)
    for start in range(0, edges, 4 * span):
        lanes = slice(start, start + 4 * span)
        result = dot_nt(est[:, lanes], gst[:, lanes])
        gc[...] += result[:, 0:128]
        ge[:, 0:16] += result[:, 128:144]
    ds1_total = tree(
        jnp.add,
        [gst[128:144, k * half : (k + 1) * half].astype(F32)[0:8] for k in range(NEIGH)],
    )
    w_att1_exact = w1[0:C1, 0:16].astype(BF16).astype(F32)[:, 0:8]
    dqueries = exact(w_att1_exact, ds1_total)
    give_dkv.wait_recv()
    dkv = own_half(dkp, dkr)
    dkeys = -exact(w_att1_exact, dkv[C1 : C1 + 8])
    dqkv_low = jnp.concatenate([dqueries, dkeys, dkv[0:C1]], 0).astype(BF16)
    gbuf[...] = jnp.zeros_like(gbuf)
    gbuf[0:64, :] = dot_nt(pooled_ref[...].astype(BF16), dqkv_low[0:128])
    gbuf[64:128, 0:64] = dot_nt(pooled_ref[...].astype(BF16), dqkv_low[128:192])
    dpooled = dblock + dot(w_qkv, dqkv_low)

    gb[...] = jnp.zeros_like(gb)
    gb[0:16, 0:C1] = dot_nt(centre_low, (-dpooled).astype(BF16))
    dscaled = dpooled * rsum_ref[...]

    def pool_back(k, lanes):
        dpin = (pin[:, lanes] * dscaled).astype(BF16)
        gst[0:64, lanes] = dpin
        kept = cat[16:48, lanes].astype(F32) > 0
        gst[64:96, lanes] = jnp.where(kept, dot(w_down_stem, dpin), 0.0).astype(BF16)

    every_edge(pool_back, 16)
    for start in range(0, edges, 4 * span):
        lanes = slice(start, start + 4 * span)
        gb[:, 0:96] += dot_nt(cat[:, lanes], gst[0:96, lanes])

    left = lanes_of(64, LANES) < 64
    gd_out = gd[64:128, :]
    gbuf[64:128, :] = jnp.where(left, gbuf[64:128, :], gc[64:128, :])
    gbuf[128:160, :] = jnp.where(left[0:32], pltpu.roll(gd_out[0:32], 64, 1), gd_out[32:64])
    base = 160
    pack(gbuf, base, ga, 0, 32, OFF["w_stem"], 6, C0)
    pack(gbuf, base, gb, 0, 64, OFF["w_stem"], 6, C0)
    pack(gbuf, base, ga, 7, 32, OFF["b_stem"], 1, C0)
    pack(gbuf, base, gb, 7, 64, OFF["b_stem"], 1, C0)
    pack(gbuf, base, gb, 0, 0, OFF["w_down"], 3, C1)
    pack(gbuf, base, gb, 16, 0, OFF["w_down"] + 3 * C1, C0, C1)
    pack(gbuf, base, gb, 7, 0, OFF["b_down"], 1, C1)
    pack(gbuf, base, gc, 136, 0, OFF["w_pos"], 3, C1)
    pack(gbuf, base, gc, 143, 0, OFF["b_pos"], 1, C1)
    pack(gbuf, base, ge, 0, 0, OFF["w_att1"], C1, GROUPS)
    pack(gbuf, base, ge, 143, 0, OFF["b_att1"], 1, GROUPS)
    pack(gbuf, base, ge, 128, 8, OFF["w_att2"], GROUPS, GROUPS)
    pack(gbuf, base, ge, 143, 8, OFF["b_att2"], 1, GROUPS)
    pack(gbuf, base, gd, 0, 0, OFF["w_up"], C1, C0)
    pack(gbuf, base, gd, 128, 0, OFF["b_up"], 1, C0)
    pack(gbuf, base, ga, 16, 0, OFF["w_skip"], C0, C0)
    pack(gbuf, base, ga, 48, 64, OFF["w_head"], C0, NCLS)
    pack(gbuf, base, ga, 7, 64, OFF["b_head"], 1, NCLS)
    loss_sum = jnp.sum(loss, axis=1, keepdims=True)
    line, lane = divmod(FLAT, LANES)
    at_loss = lanes_of(1, LANES) == lane
    gbuf[base + line : base + line + 1, :] += jnp.where(at_loss, loss_sum, 0.0)

    rows = gbuf.shape[0] // n_sub
    shards = rows // 8
    give_grad = sibling(5, gbuf.at[pl.ds(pl.multiple_of((1 - sub) * rows, rows), rows)], gsib)
    give_grad.start()
    give_grad.wait_recv()
    ghalf[...] = gbuf[pl.ds(pl.multiple_of(sub * rows, rows), rows), :] + gsib[...]
    mine_at = pl.multiple_of(sub * rows + me * 8, 8)

    def shard_copy(peer, index):
        return pltpu.make_async_remote_copy(
            src_ref=ghalf.at[pl.ds(pl.multiple_of(peer * 8, 8), 8)],
            dst_ref=gsh.at[index],
            send_sem=red_send.at[peer],
            recv_sem=red_recv.at[index],
            device_id={"pts": peer},
            device_id_type=MESH,
        )

    def sum_copy(peer, index):
        at = pl.multiple_of(sub * rows + index * 8, 8)
        return pltpu.make_async_remote_copy(
            src_ref=gfull.at[pl.ds(at, 8)],
            dst_ref=gfull.at[pl.ds(at, 8)],
            send_sem=gat_send.at[peer],
            recv_sem=gat_recv.at[index],
            device_id={"pts": peer},
            device_id_type=MESH,
        )

    holds = None if n_pts <= shards else me < shards

    def when(condition, run):
        if condition is None:
            run()
        else:
            pl.when(condition)(run)

    def each_peer(run, limited):
        def body(step, carry):
            peer = partner(step)
            when(None if holds is None or not limited else peer < shards, lambda: run(peer))
            return carry

        lax.fori_loop(1, n_pts, body, 0)

    each_peer(lambda peer: shard_copy(peer, me).start(), True)

    def reduce():
        gsh[me] = ghalf[pl.ds(pl.multiple_of(me * 8, 8), 8), :]
        each_peer(lambda peer: shard_copy(peer, peer).wait_recv(), False)
        gfull[pl.ds(mine_at, 8), :] = jnp.sum(gsh[...], axis=0)
        each_peer(lambda peer: sum_copy(peer, me).start(), False)

    when(holds, reduce)
    each_peer(lambda peer: sum_copy(peer, peer).wait_recv(), True)
    half_rows = gfull.at[pl.ds(pl.multiple_of(sub * rows, rows), rows)]
    give_full = sibling(6, half_rows, half_rows)
    give_full.start()

    each_peer(lambda peer: block_copy(peer, me).wait_send(), False)
    each_peer(lambda peer: mat_copy(peer, me).wait_send(), False)
    each_peer(lambda peer: shard_copy(peer, me).wait_send(), True)
    when(holds, lambda: each_peer(lambda peer: sum_copy(peer, me).wait_send(), False))
    for copy in (forward, give_pooled, give_block, give_dup, give_dkv, give_grad, give_full):
        copy.wait_send()
    give_full.wait_recv()
    out_ref[...] = gfull[...]


def normalised(matrix):
    return matrix * lax.rsqrt(jnp.sum(matrix * matrix, axis=0, keepdims=True))


def gram_schmidt_pair(matrix, width=8):
    size = matrix.shape[0]
    left = lanes_of(size, 2 * size) < size
    column = lanes_of(1, 2 * size)
    left_row = column < size
    place_row = jnp.where(left_row, column, column - size)

    def spread(values, halves, at):
        return jnp.where(halves, values[:, at : at + 1], values[:, size + at : size + at + 1])

    for first in range(0, size, width):
        span = range(width)
        pivots = [spread(matrix, left, first + i) for i in span]
        products = [jnp.sum(pivot * matrix, axis=0, keepdims=True) for pivot in pivots]
        gram = [
            [spread(products[i], left_row, first + l) if l >= i else None for l in span]
            for i in span
        ]
        taken = 0.0
        for i in span:
            inverse = 1.0 / gram[i][i]
            for l in range(i + 1, width):
                part = gram[i][l] * inverse
                pivots[l] = pivots[l] - part * pivots[i]
                products[l] = products[l] - part * products[i]
                for m in range(l, width):
                    gram[l][m] = gram[l][m] - part * gram[i][m]
            factor = jnp.where(place_row > first + i, products[i] * inverse, 0.0)
            taken = taken + pivots[i] * factor
        matrix = matrix - taken
    return normalised(matrix)


def careful_pair(matrix):
    size = matrix.shape[0]
    lane = lanes_of(size, 2 * size)
    left = lane < size
    place = jnp.where(left, lane, lane - size)

    def column(j, matrix):
        here = jnp.where(place == j, matrix, 0.0)
        first = jnp.sum(jnp.where(left, here, 0.0), axis=1, keepdims=True)
        second = jnp.sum(jnp.where(left, 0.0, here), axis=1, keepdims=True)
        pivot = jnp.where(left, first, second)
        pivot = pivot * lax.rsqrt(jnp.sum(pivot * pivot, axis=0, keepdims=True))
        factor = jnp.sum(pivot * matrix, axis=0, keepdims=True)
        return matrix - jnp.where(place > j, pivot * factor, 0.0)

    for repeat in range(2):
        matrix = normalised(lax.fori_loop(0, size, column, matrix))
    return matrix


def departure(basis):
    size = basis.shape[0]
    same = rows_of(size, size) == lanes_of(size, size)
    return exact(basis, basis, ((0,), (0,))) - jnp.where(same, 1.0, 0.0)


def correct(basis, error):
    size = basis.shape[0]
    above = rows_of(size, size) < lanes_of(size, size)
    same = rows_of(size, size) == lanes_of(size, size)
    factor = jnp.where(above, error, jnp.where(same, 0.5 * error, 0.0))
    return basis - exact(basis, factor)


def orthonormal_pair(matrix, both_ref):
    size = matrix.shape[0]
    once = gram_schmidt_pair(matrix)
    halves = [once[:, 0:size], once[:, size : 2 * size]]
    errors = [departure(half) for half in halves]
    worst = jnp.max(jnp.maximum(jnp.abs(errors[0]), jnp.abs(errors[1])))
    halves = [correct(half, error) for half, error in zip(halves, errors)]
    both_ref[...] = jnp.concatenate(halves, 1)

    @pl.when(worst > 1e-4)
    def _():
        again = [both_ref[:, 0:size], both_ref[:, size : 2 * size]]
        both_ref[...] = jnp.concatenate([correct(half, departure(half)) for half in again], 1)

    @pl.when(jnp.logical_not(worst < 0.01))
    def _():
        both_ref[...] = careful_pair(matrix)

    return both_ref[...]


def soap_kernel(
    grads_ref,
    owner_ref,
    step_ref,
    weight_ref,
    first_ref,
    second_ref,
    left_ref,
    right_ref,
    basis_l_ref,
    basis_r_ref,
    average_ref,
    flat_ref,
    flat_mom_ref,
    flat_sec_ref,
    flat_ema_ref,
    weight_out,
    first_out,
    second_out,
    left_out,
    right_out,
    basis_l_out,
    basis_r_out,
    average_out,
    flat_out,
    flat_mom_out,
    flat_sec_out,
    flat_ema_out,
    loss_out,
    norm_out,
    both_ref,
):
    me = lax.axis_index("pts")
    grads = grads_ref[...]
    line, lane = divmod(FLAT, LANES)
    place_row = rows_of(256, LANES)
    at_loss = (place_row == 160 + line) & (lanes_of(256, LANES) == lane)
    loss = jnp.where(at_loss, grads, 0.0)
    loss_out[...] = jnp.sum(jnp.sum(loss, axis=0, keepdims=True), axis=1, keepdims=True)
    cleaned = jnp.where(at_loss, 0.0, grads)
    squares = jnp.sum(jnp.sum(cleaned * cleaned, axis=0, keepdims=True), axis=1, keepdims=True)
    norm = jnp.sqrt(squares)
    norm_out[...] = norm
    factor = jnp.minimum(1.0, CLIP_NORM / norm)
    count = jnp.full((1, 1), step_ref[0].astype(F32), F32)
    one_scale = 1.0 - jnp.exp(count * math.log(BETA_ONE))
    two_scale = 1.0 - jnp.exp(count * math.log(BETA_TWO))
    lines = FLAT_ROWS - 8

    def as_line(values):
        return jnp.broadcast_to(values, (lines, LANES)).reshape(lines * LANES)[0:FLAT]

    flat_grad = (cleaned[160 : 160 + lines] * factor).reshape(lines * LANES)[0:FLAT]
    flat_mom = BETA_ONE * flat_mom_ref[...] + (1.0 - BETA_ONE) * flat_grad
    flat_sec = BETA_TWO * flat_sec_ref[...] + (1.0 - BETA_TWO) * flat_grad * flat_grad
    flat_scaled = flat_mom / as_line(one_scale) / (jnp.sqrt(flat_sec / as_line(two_scale)) + ADAM_EPS)
    flat_new = flat_ref[...] - LEARN_RATE * (flat_scaled + WEIGHT_DECAY * flat_ref[...])
    flat_out[...] = flat_new
    flat_mom_out[...] = flat_mom
    flat_sec_out[...] = flat_sec
    flat_ema_out[...] = EMA_KEEP * flat_ema_ref[...] + (1.0 - EMA_KEEP) * flat_new
    folded = cleaned[128:160]
    stacked = [
        cleaned[0:64, 0:64],
        cleaned[0:64, 64:128],
        cleaned[64:128, 0:64],
        cleaned[64:128, 64:128],
        jnp.concatenate([folded[:, 0:64], folded[:, 64:128]], 0),
    ]
    grad = jnp.zeros((C1, C1), F32)
    owned = 0.0
    for position in range(NMATS):
        flag = jnp.where(owner_ref[position] == me, 1.0, 0.0)
        grad = grad + flag * stacked[position]
        owned = owned + flag
    grad = grad * factor
    basis_l = basis_l_ref[...]
    basis_r = basis_r_ref[...]
    left_new = BETA_TWO * left_ref[...] + (1.0 - BETA_TWO) * exact(grad, grad, ((1,), (1,)))
    right_new = BETA_TWO * right_ref[...] + (1.0 - BETA_TWO) * exact(grad, grad, ((0,), (0,)))
    both = orthonormal_pair(
        jnp.concatenate([exact(left_new, basis_l), exact(right_new, basis_r)], 1), both_ref
    )
    basis_l_new = both[:, 0:C1]
    basis_r_new = both[:, C1 : 2 * C1]
    rotated = exact(exact(basis_l, grad, ((0,), (0,))), basis_r)
    first_new = BETA_ONE * first_ref[...] + (1.0 - BETA_ONE) * rotated
    second_new = BETA_TWO * second_ref[...] + (1.0 - BETA_TWO) * rotated * rotated
    scaled = first_new / one_scale / (jnp.sqrt(second_new / two_scale) + ADAM_EPS)
    weight = weight_ref[...]
    weight_new = weight - LEARN_RATE * (
        exact(exact(basis_l, scaled), basis_r, ((1,), (1,))) + WEIGHT_DECAY * weight
    )
    plain = exact(exact(basis_l, first_new), basis_r, ((1,), (1,)))
    first_rotated = exact(exact(basis_l_new, plain, ((0,), (0,))), basis_r_new)
    average_new = EMA_KEEP * average_ref[...] + (1.0 - EMA_KEEP) * weight_new
    held = owned > 0.5
    weight_out[...] = jnp.where(held, weight_new, 0.0)
    first_out[...] = jnp.where(held, first_rotated, 0.0)
    second_out[...] = jnp.where(held, second_new, 0.0)
    left_out[...] = jnp.where(held, left_new, 0.0)
    right_out[...] = jnp.where(held, right_new, 0.0)
    basis_l_out[...] = jnp.where(held, basis_l_new, 0.0)
    basis_r_out[...] = jnp.where(held, basis_r_new, 0.0)
    average_out[...] = jnp.where(held, average_new, 0.0)


def local(
    points,
    route,
    labels,
    interp_src,
    pool_nbr,
    sample,
    coarse_nbr,
    owner,
    step,
    flat,
    flat_mom,
    flat_sec,
    flat_ema,
    mats,
    mats_mom,
    mats_sec,
    mats_left,
    mats_right,
    mats_basis_l,
    mats_basis_r,
    mats_ema,
):
    n_pts = lax.axis_size("pts")
    n_sub = lax.axis_size("sub")
    fine = points.shape[0]
    coarse = sample.shape[0]
    cap = n_sub * fine // n_pts
    slots = n_pts * cap
    sources = n_sub * n_pts
    half = coarse // n_sub
    edges = NEIGH * half
    parts = coarse // LOW_B
    my_parts = parts // n_sub
    vmem = pl.BlockSpec(memory_space=pltpu.VMEM)
    smem = pl.BlockSpec(memory_space=pltpu.SMEM)
    dma = pltpu.SemaphoreType.DMA
    scratch = [
        VMEM((6, fine), BF16),
        VMEM((1, fine), I32),
        VMEM((1, fine), I32),
        VMEM((3, fine), I32),
        VMEM((NEIGH, coarse), I32),
        VMEM((1, coarse), I32),
        VMEM((NEIGH, coarse), I32),
        pltpu.SMEM((NMATS,), I32),
        VMEM((C1, C1), F32),
        VMEM((FLAT,), F32),
        VMEM((FLAT_ROWS, LANES), F32),
        VMEM((LOW_B, LANES), BF16),
        VMEM((16, fine), F32),
        VMEM((n_pts * 16, cap), F32),
        VMEM((n_pts, 16, cap), BF16),
        VMEM((sources, 16, cap), BF16),
        VMEM((32, LANES), BF16),
        VMEM((n_pts, 32, LANES), BF16),
        VMEM((sources * 8, cap), BF16),
        VMEM((8, coarse), F32),
        VMEM((C1, edges), F32),
        VMEM((48, edges), BF16),
        VMEM((C1, half), F32),
        VMEM((C1, half), F32),
        VMEM((n_sub, my_parts * CH, LOW_B), BF16),
        VMEM((n_sub, my_parts * CH, LOW_B), BF16),
        VMEM((C1, edges), BF16),
        VMEM((144, edges), BF16),
        VMEM((144, edges), BF16),
        VMEM((LOW_B, edges), BF16),
        VMEM((C1, edges), F32),
        VMEM((GROUPS, edges), F32),
        VMEM((C1, half), F32),
        VMEM((C1, half), F32),
        VMEM((16, slots), F32),
        VMEM((80, slots), BF16),
        VMEM((80, slots), BF16),
        VMEM((C0, slots), F32),
        VMEM((3, LOW_B, slots), BF16),
        VMEM((3, C1, slots), BF16),
        VMEM((8, slots), F32),
        VMEM((parts, C0, LOW_B), F32),
        VMEM((my_parts, C0, LOW_B), F32),
        VMEM((parts, C1 + 8, LOW_B), F32),
        VMEM((my_parts, C1 + 8, LOW_B), F32),
        VMEM((LANES, LANES), F32),
        VMEM((LANES, LANES), F32),
        VMEM((LANES, LANES), F32),
        VMEM((LANES, LANES), F32),
        VMEM((LANES, LANES), F32),
        VMEM((LANES, LANES), F32),
        VMEM((LANES, LANES), F32),
        VMEM((LANES, LANES), F32),
        VMEM((LANES, LANES), F32),
        VMEM((80, LANES), F32),
        VMEM((48, LANES), F32),
        VMEM((144, LANES), F32),
        VMEM((144, LANES), F32),
        VMEM((144, LANES), F32),
        VMEM((256, LANES), F32),
        VMEM((128, LANES), F32),
        VMEM((128, LANES), F32),
        VMEM((n_pts, 8, LANES), F32),
        VMEM((256, LANES), F32),
        dma((n_pts,)),
        dma((n_pts,)),
        dma((n_pts,)),
        dma((n_pts,)),
        dma((n_pts,)),
        dma((n_pts,)),
        dma((n_pts,)),
        dma((n_pts,)),
        dma((8,)),
        dma((8,)),
        dma((10,)),
    ]
    reduced = pl.pallas_call(
        functools.partial(main_kernel, n_pts, n_sub),
        out_shape=jax.ShapeDtypeStruct((256, LANES), F32),
        in_specs=[pl.BlockSpec(memory_space=pltpu.HBM)] * 10,
        out_specs=vmem,
        scratch_shapes=scratch,
        compiler_params=pltpu.CompilerParams(
            collective_id=0, has_side_effects=True, vmem_limit_bytes=60 * 1024 * 1024
        ),
    )(
        points.T,
        route.reshape(1, fine),
        labels.reshape(1, fine),
        interp_src.T,
        pool_nbr.T,
        sample.reshape(1, coarse),
        coarse_nbr.T,
        owner,
        mats[0],
        flat,
    )
    square = jax.ShapeDtypeStruct((C1, C1), F32)
    line = jax.ShapeDtypeStruct((FLAT,), F32)
    single = jax.ShapeDtypeStruct((1, 1), F32)
    results = pl.pallas_call(
        soap_kernel,
        out_shape=[square] * 8 + [line] * 4 + [single] * 2,
        in_specs=[vmem] + [smem] * 2 + [vmem] * 12,
        out_specs=[vmem] * 14,
        scratch_shapes=[VMEM((C1, 2 * C1), F32)],
    )(
        reduced,
        owner,
        step,
        mats[0],
        mats_mom[0],
        mats_sec[0],
        mats_left[0],
        mats_right[0],
        mats_basis_l[0],
        mats_basis_r[0],
        mats_ema[0],
        flat,
        flat_mom,
        flat_sec,
        flat_ema,
    )
    scalars = (results[12].reshape(()), results[13].reshape(()))
    return scalars + tuple(results[8:12]) + tuple(result[None] for result in results[:8])


def solution(mesh):
    placed = (
        P(("pts", "sub"), None),
        P(("pts", "sub")),
        P(("pts", "sub")),
        P(("pts", "sub"), None),
        P("pts", None),
        P("pts"),
        P("pts", None),
        P(),
        P(),
        P(),
        P(),
        P(),
        P(),
    ) + (P("pts", None, None),) * 8
    mapped = jax.shard_map(
        local,
        mesh=mesh,
        in_specs=placed,
        out_specs=(P(),) * 6 + (P("pts", None, None),) * 8,
        check_vma=False,
    )

    def run(*arrays):
        with jax.sharding.use_abstract_mesh(mesh.abstract_mesh):
            return mapped(*arrays)

    return run
```

```python
import functools
import math

import jax
import jax.numpy as jnp
from jax import lax
from jax.experimental import pallas as pl
from jax.experimental.pallas import tpu as pltpu
from jax.sharding import PartitionSpec as P

C0 = 32
C1 = 64
NEIGH = 16
NCLS = 13
GROUPS = 8
NMATS = 5

HIGHEST = lax.Precision.HIGHEST
CLIP_NORM = 0.01
BETA_ONE = 0.9
BETA_TWO = 0.95
ADAM_EPS = 1e-08
LEARN_RATE = 0.1
WEIGHT_DECAY = 0.01
EMA_KEEP = 0.9
INTERP_EPS = 0.01

F32 = jnp.float32
BF16 = jnp.bfloat16
I32 = jnp.int32
MESH = pl.DeviceIdType.MESH
VMEM = pltpu.VMEM

LANES = 128
FLAT_ROWS = 64
LOW_B = 256
CH = 72
NEG = -1e30


def offsets():
    shapes = [
        ("w_stem", (6, C0)),
        ("b_stem", (C0,)),
        ("w_down", (3 + C0, C1)),
        ("b_down", (C1,)),
        ("w_pos", (3, C1)),
        ("b_pos", (C1,)),
        ("w_att1", (C1, GROUPS)),
        ("b_att1", (GROUPS,)),
        ("w_att2", (GROUPS, GROUPS)),
        ("b_att2", (GROUPS,)),
        ("w_up", (C1, C0)),
        ("b_up", (C0,)),
        ("w_skip", (C0, C0)),
        ("w_head", (C0, NCLS)),
        ("b_head", (NCLS,)),
    ]
    found = {}
    total = 0
    for name, shape in shapes:
        found[name] = total
        total += math.prod(shape)
    return found, total


OFF, FLAT = offsets()


def dot(left, right):
    return lax.dot_general(left, right, (((1,), (0,)), ((), ())), preferred_element_type=F32)


def dot_nt(left, right):
    return lax.dot_general(left, right, (((1,), (1,)), ((), ())), preferred_element_type=F32)


def exact(left, right, dims=((1,), (0,))):
    return lax.dot_general(
        left, right, (dims, ((), ())), precision=HIGHEST, preferred_element_type=F32
    )


def relu(values):
    return jnp.maximum(values, 0.0)


def rows_of(count, length):
    return lax.broadcasted_iota(I32, (count, length), 0)


def lanes_of(count, length):
    return lax.broadcasted_iota(I32, (count, length), 1)


def onehot(low, count):
    hit = rows_of(count, low.shape[1]) == low
    return jnp.where(hit, 1.0, 0.0).astype(BF16)


def stored_onehot(low, iota):
    count, length = iota.shape[0], low.shape[1]
    wanted = jnp.broadcast_to(low.astype(F32), (16, length)).astype(BF16)
    held = jnp.concatenate([iota] * (length // LANES), 1).reshape(count // 16, 16, length)
    hit = held == wanted[None]
    return jnp.where(hit, jnp.ones((), BF16), jnp.zeros((), BF16)).reshape(count, length)


def pick(spread, high, parts):
    each = spread.shape[0] // parts
    found = spread[0:each]
    for part in range(1, parts):
        found = jnp.where(high == part, spread[part * each : (part + 1) * each], found)
    return found


def place(values, high, parts):
    return jnp.concatenate(
        [jnp.where(high == part, values, 0.0) for part in range(parts)], 0
    ).astype(BF16)


def unpack(flat_ref, out_ref, offset, rows, width, at):
    stride = LANES // width if LANES % width == 0 else rows
    for first in range(min(stride, rows)):
        count = (rows - first + stride - 1) // stride
        padded = -(-count // 8) * 8
        line, lane = divmod(offset + first * width, LANES)
        values = flat_ref[line : line + padded, :]
        if lane:
            values = pltpu.roll(values, LANES - lane, 1)
        if lane + width > LANES:
            following = pltpu.roll(flat_ref[line + 1 : line + 1 + padded, :], LANES - lane, 1)
            values = jnp.where(lanes_of(padded, LANES) < LANES - lane, values, following)
        values = jnp.where(lanes_of(padded, LANES) < width, values, 0.0)
        if count == 1:
            out_ref[at + first : at + first + 1, :] = values[0:1]
        else:
            out_ref[pl.ds(at + first, count, stride=stride), :] = values[0:count]


def pack(out_ref, base, source_ref, row, lane_from, offset, rows, width):
    stride = LANES // width if LANES % width == 0 else rows
    for first in range(min(stride, rows)):
        count = (rows - first + stride - 1) // stride
        line, lane = divmod(offset + first * width, LANES)
        if count == 1:
            values = source_ref[row + first : row + first + 1, :]
        else:
            values = source_ref[pl.ds(row + first, count, stride=stride), :]
        shift = (lane - lane_from) % LANES
        padded = -(-count // 8) * 8
        if padded != count:
            values = jnp.concatenate([values, jnp.zeros((padded - count, LANES), F32)], 0)
        if shift:
            values = pltpu.roll(values, shift, 1)
        values = values[0:count]
        at = lanes_of(count, LANES)
        here = jnp.where((at >= lane) & (at < lane + width), values, 0.0)
        out_ref[base + line : base + line + count, :] += here
        if lane + width > LANES:
            there = jnp.where(at < lane + width - LANES, values, 0.0)
            out_ref[base + line + 1 : base + line + 1 + count, :] += there


def main_kernel(
    n_pts,
    n_sub,
    pts_hbm,
    route_hbm,
    labels_hbm,
    src_hbm,
    pool_hbm,
    sample_hbm,
    cnbr_hbm,
    owner_hbm,
    mats_hbm,
    flat_hbm,
    out_ref,
    pts_ref,
    route_ref,
    labels_ref,
    src_ref,
    pool_ref,
    sample_ref,
    cnbr_ref,
    owner_ref,
    mats_ref,
    flat_line,
    flat_ref,
    iota_ref,
    data,
    sacc,
    sendb,
    recv,
    matmine,
    matall,
    tabb,
    cen,
    pin,
    cat,
    pooled_ref,
    rsum_ref,
    ctab,
    btab,
    near,
    est,
    gst,
    ohs,
    car,
    sc,
    mixed_ref,
    blk_ref,
    slot,
    fin,
    fgr,
    skp,
    foh,
    fsrc,
    fwt,
    dcp,
    dcr,
    dkp,
    dkr,
    wst,
    wd,
    wp,
    w1,
    w2,
    wu,
    wsk,
    wh,
    bias,
    ga,
    gb,
    gc,
    gd,
    ge,
    gbuf,
    gsib,
    ghalf,
    gsh,
    gfull,
    a2a_send,
    a2a_recv,
    mat_send,
    mat_recv,
    red_send,
    red_recv,
    gat_send,
    gat_recv,
    sib_send,
    sib_recv,
    load_sem,
):
    fine = route_ref.shape[1]
    coarse = sample_ref.shape[1]
    cap = sendb.shape[2]
    slots = n_pts * cap
    half = coarse // n_sub
    edges = NEIGH * half
    sources = n_sub * n_pts
    parts = coarse // LOW_B
    my_parts = parts // n_sub
    shift = cap.bit_length() - 1
    low_shift = LOW_B.bit_length() - 1
    span = 512
    me = lax.axis_index("pts")
    sub = lax.axis_index("sub")
    half_at = pl.multiple_of(sub * half, half)

    far_refs = (pts_hbm, route_hbm, labels_hbm, src_hbm, mats_hbm, sample_hbm, pool_hbm, cnbr_hbm, owner_hbm)
    near_refs = (pts_ref, route_ref, labels_ref, src_ref, mats_ref, sample_ref, pool_ref, cnbr_ref, owner_ref)
    loads = [
        pltpu.make_async_copy(source, target, load_sem.at[number])
        for number, (source, target) in enumerate(zip(far_refs, near_refs))
    ]
    loads.append(
        pltpu.make_async_copy(flat_hbm, flat_line, load_sem.at[len(loads)])
    )
    for load in loads:
        load.start()

    barrier = pltpu.get_barrier_semaphore()

    powers = [2**k for k in range(n_pts.bit_length() - 1)]
    my_bits = [lax.bitwise_and(lax.shift_right_logical(me, k), 1) for k in range(len(powers))]

    def partner(step):
        step = n_pts - step
        found = 0
        for k, power in enumerate(powers):
            bit = lax.bitwise_and(my_bits[k] + lax.shift_right_logical(step, k), 1)
            found = found + power * bit
        return found

    def greet(step, carry):
        peer = partner(step)
        pl.semaphore_signal(barrier, inc=1, device_id={"pts": peer}, device_id_type=MESH)
        return carry

    lax.fori_loop(1, n_pts, greet, 0)
    pl.semaphore_signal(barrier, inc=1, device_id={"sub": 1 - sub}, device_id_type=MESH)

    def sibling(number, source, target):
        return pltpu.make_async_remote_copy(
            src_ref=source,
            dst_ref=target,
            send_sem=sib_send.at[number],
            recv_sem=sib_recv.at[number],
            device_id={"sub": 1 - sub},
            device_id_type=MESH,
        )

    iota_ref[...] = rows_of(LOW_B, LANES).astype(F32).astype(BF16)
    for load in loads[0:5] + loads[9:]:
        load.wait()
    data[0:6, :] = pts_ref[...].astype(F32)
    data[6:8, :] = jnp.zeros((2, fine), F32)
    source_rows = src_ref[...]
    data[8:11, :] = lax.shift_right_logical(source_rows, 5).astype(F32)
    data[11:14, :] = (source_rows & 31).astype(F32)
    data[14:15, :] = (labels_ref[...] + 1).astype(F32)
    data[15:16, :] = jnp.zeros((1, fine), F32)
    sacc[...] = jnp.zeros_like(sacc)
    counts = jnp.zeros((16, 32), F32)
    for chunk in range(fine // span):
        lanes = slice(chunk * span, (chunk + 1) * span)
        route = route_ref[:, lanes]
        high = lax.shift_right_logical(route, shift)
        spread = place(data[:, lanes], high, n_pts)
        sacc[...] += dot_nt(spread, onehot(route & (cap - 1), cap))
        classes = onehot(labels_ref[:, lanes], 16)
        counts = counts + dot_nt(jnp.ones((16, span), BF16), jnp.concatenate([classes, classes], 0))
    count_high = jnp.floor(counts * (1.0 / 128.0))
    count_low = counts - 128.0 * count_high
    digits = jnp.where(lanes_of(16, 32) < 16, count_low, count_high)
    digits = jnp.where(rows_of(16, 32) == 15, digits, 0.0)
    data[:, 0:cap] = jnp.zeros((16, cap), F32)
    data[:, 0:32] = digits
    sendb[...] = (sacc[...].reshape(n_pts, 16, cap) + data[:, 0:cap][None]).astype(BF16)
    matrix = mats_ref[...]
    matmine[...] = jnp.concatenate([matrix[0:32], matrix[32:64]], 1).astype(BF16)

    pl.semaphore_wait(barrier, n_pts)

    def block_copy(peer, index):
        return pltpu.make_async_remote_copy(
            src_ref=sendb.at[peer],
            dst_ref=recv.at[sub * n_pts + index],
            send_sem=a2a_send.at[peer],
            recv_sem=a2a_recv.at[index],
            device_id={"pts": peer},
            device_id_type=MESH,
        )

    def mat_copy(peer, index):
        return pltpu.make_async_remote_copy(
            src_ref=matmine,
            dst_ref=matall.at[index],
            send_sem=mat_send.at[peer],
            recv_sem=mat_recv.at[index],
            device_id={"pts": peer},
            device_id_type=MESH,
        )

    def send_blocks(step, carry):
        block_copy(partner(step), me).start()
        return carry

    def send_mats(step, carry):
        mat_copy(partner(step), me).start()
        return carry

    lax.fori_loop(1, n_pts, send_blocks, 0)
    recv[sub * n_pts + me] = sendb[me]
    matall[me] = matmine[...]

    for ref in (wst, wd, wp, w1, w2, wu, wsk, wh, bias):
        ref[...] = jnp.zeros_like(ref)
    padded = jnp.pad(flat_line[...], (0, FLAT_ROWS * LANES - FLAT))
    flat_ref[...] = padded.reshape(FLAT_ROWS, LANES)
    unpack(flat_ref, wst, OFF["w_stem"], 6, C0, 0)
    unpack(flat_ref, wd, OFF["w_down"], 3, C1, 0)
    unpack(flat_ref, wd, OFF["w_down"] + 3 * C1, C0, C1, 16)
    unpack(flat_ref, wp, OFF["w_pos"], 3, C1, 8)
    unpack(flat_ref, w1, OFF["w_att1"], C1, GROUPS, 0)
    unpack(flat_ref, w2, OFF["w_att2"], GROUPS, GROUPS, 0)
    unpack(flat_ref, wu, OFF["w_up"], C1, C0, 0)
    unpack(flat_ref, wsk, OFF["w_skip"], C0, C0, 0)
    unpack(flat_ref, wh, OFF["w_head"], C0, NCLS, 0)
    names = ("b_stem", "b_down", "b_pos", "b_att1", "b_att2", "b_up", "b_head")
    widths = (C0, C1, C1, GROUPS, GROUPS, C0, NCLS)
    for position, (name, width) in enumerate(zip(names, widths)):
        unpack(flat_ref, bias, OFF[name], 1, width, position)
    columns = bias[...].T
    b_stem = columns[0:C0, 0:1]
    b_down = columns[0:C1, 1:2]
    b_pos = columns[0:C1, 2:3]
    b_att1 = columns[0:GROUPS, 3:4]
    b_att2 = columns[0:GROUPS, 4:5]
    b_up = columns[0:C0, 5:6]
    b_head = jnp.where(rows_of(16, 1) < NCLS, columns[0:16, 6:7], NEG)
    w_stem_t = wst[...].T[0:C0, 0:16].astype(BF16)
    w_down_t = wd[...].T[0:C1, 0:48].astype(BF16)
    w_pos_t = wp[...].T[0:C1, 0:16].astype(BF16)
    w_att1_t = w1[...].T[0:GROUPS, 0:C1].astype(BF16)
    w_att2_t = w2[...].T[0:GROUPS, 0:16].astype(BF16)
    w_up_t = wu[...].T[0:C0, 0:C1].astype(BF16)
    w_skip_t = wsk[...].T[0:C0, 0:C0].astype(BF16)
    w_head_t = wh[...].T[0:16, 0:C0].astype(BF16)
    w_down_stem = wd[16:48, 0:C1].astype(BF16)
    w_att1 = w1[0:C1, 0:16].astype(BF16)
    w_att2 = w2[0:GROUPS, 0:16].astype(BF16)
    w_up = wu[0:C1, 0:C0].astype(BF16)
    w_skip = wsk[0:C0, 0:C0].astype(BF16)
    w_head = wh[0:C0, 0:16].astype(BF16)

    def wait_blocks(step, carry):
        peer = partner(step)
        block_copy(peer, peer).wait_recv()
        return carry

    lax.fori_loop(1, n_pts, wait_blocks, 0)
    lax.fori_loop(1, n_pts, send_mats, 0)
    for load in loads[5:9]:
        load.wait()
    mine = recv.at[pl.ds(sub * n_pts, n_pts)]
    forward = sibling(0, mine, mine)
    forward.start()
    for source in range(n_pts):
        slot[:, source * cap : (source + 1) * cap] = recv[sub * n_pts + source].astype(F32)
    forward.wait_recv()

    table = recv[...].astype(F32)[:, 0:8, :].reshape(sources * 8, cap)
    ones_row = (rows_of(sources * 8, cap) & 7) == 7
    tabb[...] = jnp.where(ones_row, 1.0, table).astype(BF16)
    count_row = jnp.sum(recv[...].astype(F32)[:, 8:16, :], axis=0)[7:8, 0:32]
    count_at = jnp.broadcast_to(count_row, (16, 32))
    low_hit = lanes_of(16, 32) == rows_of(16, 32)
    high_hit = lanes_of(16, 32) == rows_of(16, 32) + 16
    class_counts = jnp.sum(
        jnp.where(low_hit, count_at, 0.0) + jnp.where(high_hit, 128.0 * count_at, 0.0),
        axis=1,
        keepdims=True,
    )
    total_fine = float(fine * n_pts * n_sub)
    class_w = jnp.where(
        rows_of(16, 1) < NCLS, total_fine / (NCLS * class_counts) * (1.0 / total_fine), 0.0
    )

    def gather_points(index):
        hot = onehot(index & (cap - 1), cap)
        high = jnp.broadcast_to(lax.shift_right_logical(index, shift), (8, index.shape[1]))
        return pick(dot(tabb[...], hot), high, sources)

    zeros8 = jnp.zeros((8, span), F32)
    for chunk in range(coarse // span):
        lanes = slice(chunk * span, (chunk + 1) * span)
        found = gather_points(sample_ref[:, lanes])
        cen[:, lanes] = jnp.where(rows_of(8, span) < 6, found, 0.0)
    centre = cen[:, pl.ds(half_at, half)]
    centre_low = jnp.concatenate([centre, zeros8], 0).astype(BF16)
    w_xyz_t = jnp.where(lanes_of(C1, 16) < 3, wd[...].T[0:C1, 0:16], 0.0).astype(BF16)
    pool_base = b_down - dot(w_xyz_t, centre_low)

    def at_edge(k):
        return pl.ds(pl.multiple_of(k * half, half), half)

    def every_edge(step, unroll):
        def run(k, carry):
            step(k, at_edge(k))
            return carry

        lax.fori_loop(0, NEIGH, run, 0, unroll=unroll)

    def pool_gather(k, lanes):
        found = gather_points(pool_ref[pl.ds(k, 1), pl.ds(half_at, half)])
        cat[0:16, lanes] = jnp.concatenate([found, zeros8], 0).astype(BF16)

    def pool_stem(k, lanes):
        cat[16:48, lanes] = relu(dot(w_stem_t, cat[0:16, lanes]) + b_stem).astype(BF16)

    def pool_project(k, lanes):
        pin[:, lanes] = dot(w_down_t, cat[:, lanes]).astype(BF16).astype(F32) + pool_base

    every_edge(pool_gather, 4)
    every_edge(pool_stem, 16)
    every_edge(pool_project, 16)

    def tree(combine, values):
        while len(values) > 1:
            paired = [combine(values[i], values[i + 1]) for i in range(0, len(values) - 1, 2)]
            values = paired + ([values[-1]] if len(values) % 2 else [])
        return values[0]

    wide = 256

    def log_sum(r, carry):
        rows = pl.ds(pl.multiple_of(r * 8, 8), 8)
        for start in range(0, half, wide):
            spots = [slice(k * half + start, k * half + start + wide) for k in range(NEIGH)]
            values = [pin[rows, spot] for spot in spots]
            most = tree(jnp.maximum, values)
            values = [jnp.exp(value - most) for value in values]
            for spot, value in zip(spots, values):
                pin[rows, spot] = value
            total = tree(jnp.add, values)
            pooled_ref[rows, start : start + wide] = most + jnp.log(total)
            rsum_ref[rows, start : start + wide] = 1.0 / total
        return carry

    lax.fori_loop(0, C1 // 8, log_sum, 0, unroll=2)

    def table_rows(values, target):
        rows = []
        for part in range(my_parts):
            lanes = slice(part * LOW_B, (part + 1) * LOW_B)
            rows = rows + [values[:, lanes], centre[:, lanes]]
        target[sub] = jnp.concatenate(rows, 0).astype(BF16)

    table_rows(pooled_ref[...], ctab)
    my_ctab = ctab.at[sub]
    give_pooled = sibling(1, my_ctab, my_ctab)
    give_pooled.start()

    def wait_mats(step, carry):
        peer = partner(step)
        mat_copy(peer, peer).wait_recv()
        return carry

    lax.fori_loop(1, n_pts, wait_mats, 0)

    def layer(position):
        folded = matall[owner_ref[position]].astype(F32)
        return jnp.concatenate([folded[:, 0:C1], folded[:, C1 : 2 * C1]], 0)

    w_query, w_key, w_value, w_pos2_32, w_out_32 = [layer(position) for position in range(NMATS)]
    w_qkv = jnp.concatenate([w_query, w_key, w_value], 1).astype(BF16)
    w_query_t = w_query.T.astype(BF16)
    w_pos2 = w_pos2_32.astype(BF16)
    w_pos2_t = w_pos2_32.T
    w_edge_t = jnp.concatenate(
        [
            jnp.concatenate([-w_key.T, w_pos2_t], 1),
            jnp.concatenate([w_value.T, w_pos2_t], 1),
        ],
        0,
    ).astype(BF16)
    w_out = w_out_32.astype(BF16)
    w_out_t = w_out_32.T.astype(BF16)
    queries = dot(w_query_t, pooled_ref[...].astype(BF16))

    def at_slot(step):
        return pl.ds(pl.multiple_of(step * span, span), span)

    def every_slot(step, unroll):
        def run(j, carry):
            step(j, at_slot(j))
            return carry

        lax.fori_loop(0, slots // span, run, 0, unroll=unroll)

    def fine_points(j, lanes):
        ones = jnp.where(rows_of(8, span) == 7, 1.0, slot[0:8, lanes])
        fin[0:16, lanes] = jnp.concatenate([ones, zeros8], 0).astype(BF16)

    def fine_stem(j, lanes):
        fin[16:48, lanes] = relu(dot(w_stem_t, fin[0:16, lanes]) + b_stem).astype(BF16)

    def fine_skip(j, lanes):
        skp[:, lanes] = dot(w_skip_t, fin[16:48, lanes])

    every_slot(fine_points, 4)
    every_slot(fine_stem, 8)
    every_slot(fine_skip, 8)
    give_pooled.wait_recv()

    def attend_gather(k, lanes):
        index = cnbr_ref[pl.ds(k, 1), pl.ds(half_at, half)]
        hot = stored_onehot(index & (LOW_B - 1), iota_ref[...])
        ohs[:, lanes] = hot
        high = lax.shift_right_logical(index, low_shift)
        found = pick(dot(ctab[...].reshape(parts * CH, LOW_B), hot), high, parts)
        near[:, lanes] = found[0:C1].astype(BF16)
        offset = jnp.where(rows_of(8, half) == 7, 1.0, centre - found[C1 : C1 + 8])
        est[128:144, lanes] = jnp.concatenate([zeros8, offset], 0).astype(BF16)

    def attend_pos(k, lanes):
        est[64:128, lanes] = relu(dot(w_pos_t, est[128:144, lanes]) + b_pos).astype(BF16)

    def attend_edge(k, lanes):
        both = dot(w_edge_t, jnp.concatenate([near[:, lanes], est[64:128, lanes]], 0))
        est[0:64, lanes] = (queries + both[0:C1]).astype(BF16)
        car[:, lanes] = both[C1 : 2 * C1]

    def attend_act(k, lanes):
        act = relu(dot(w_att1_t, est[0:64, lanes]) + b_att1)
        offset = est[128:144, lanes].astype(F32)[8:16]
        est[128:144, lanes] = jnp.concatenate([act, offset], 0).astype(BF16)

    def attend_score(k, lanes):
        sc[:, lanes] = dot(w_att2_t, est[128:144, lanes]) + b_att2

    every_edge(attend_gather, 16)
    every_edge(attend_pos, 16)
    every_edge(attend_edge, 16)
    every_edge(attend_act, 16)
    every_edge(attend_score, 16)

    for start in range(0, half, wide):
        spots = [slice(k * half + start, k * half + start + wide) for k in range(NEIGH)]
        values = [sc[:, spot] for spot in spots]
        most = tree(jnp.maximum, values)
        values = [jnp.exp(value - most) for value in values]
        scale = 1.0 / tree(jnp.add, values)
        for spot, value in zip(spots, values):
            sc[:, spot] = value * scale

    for g in range(GROUPS):
        rows = slice(8 * g, 8 * g + 8)
        for start in range(0, half, wide):
            spots = [slice(k * half + start, k * half + start + wide) for k in range(NEIGH)]
            terms = [
                jnp.broadcast_to(sc[g : g + 1, spot], (8, wide)) * car[rows, spot]
                for spot in spots
            ]
            mixed_ref[rows, start : start + wide] = tree(jnp.add, terms)

    block = pooled_ref[...] + dot(w_out_t, mixed_ref[...].astype(BF16))
    blk_ref[...] = block
    table_rows(block, btab)
    my_btab = btab.at[sub]
    give_block = sibling(2, my_btab, my_btab)
    give_block.start()

    def source_of(lanes, i):
        index = (32.0 * slot[8 + i : 9 + i, lanes] + slot[11 + i : 12 + i, lanes]).astype(I32)
        return index & (LOW_B - 1), lax.shift_right_logical(index, low_shift)

    def fine_hot(j, lanes):
        for i in range(3):
            foh[i, :, lanes] = stored_onehot(source_of(lanes, i)[0], iota_ref[...])

    every_slot(fine_hot, 2)
    give_block.wait_recv()

    def fine_gather(j, lanes):
        points = slot[0:8, lanes]
        inverses = []
        for i in range(3):
            high = source_of(lanes, i)[1]
            found = pick(dot(btab[...].reshape(parts * CH, LOW_B), foh[i, :, lanes]), high, parts)
            fsrc[i, :, lanes] = found[0:C1].astype(BF16)
            diff = jnp.where(rows_of(8, span) < 3, points - found[C1 : C1 + 8], 0.0)
            inverses.append(1.0 / (jnp.sum(diff * diff, axis=0, keepdims=True) + INTERP_EPS))
        norm = 1.0 / (inverses[0] + inverses[1] + inverses[2])
        for i in range(3):
            fwt[i : i + 1, lanes] = inverses[i] * norm

    def fine_join(j, lanes):
        terms = [fwt[i : i + 1, lanes] * dot(w_up_t, fsrc[i, :, lanes]) for i in range(3)]
        interp = (terms[0] + terms[1] + terms[2] + b_up).astype(BF16).astype(F32)
        fin[48:80, lanes] = relu(interp + skp[:, lanes]).astype(BF16)

    def fine_loss(j, loss):
        lanes = at_slot(j)
        logits = dot(w_head_t, fin[48:80, lanes]) + b_head
        label = slot[14:15, lanes].astype(I32)
        hit = jnp.where(rows_of(16, span) + 1 == label, 1.0, 0.0)
        row_w = jnp.sum(hit * class_w, axis=0, keepdims=True)
        peak = jnp.max(logits, axis=0, keepdims=True)
        raised = jnp.exp(logits - peak)
        total = jnp.sum(raised, axis=0, keepdims=True)
        named = jnp.sum(hit * logits, axis=0, keepdims=True)
        fgr[64:80, lanes] = (row_w * (raised * (1.0 / total) - hit)).astype(BF16)
        return loss + row_w * (peak + jnp.log(total) - named)

    def fine_fused(j, lanes):
        kept = fin[48:80, lanes].astype(F32) > 0
        fgr[0:32, lanes] = jnp.where(kept, dot(w_head, fgr[64:80, lanes]), 0.0).astype(BF16)

    def fine_scatter(j, lanes):
        dfused = fgr[0:32, lanes].astype(F32)
        total = 0.0
        for i in range(3):
            spread = place(fwt[i : i + 1, lanes] * dfused, source_of(lanes, i)[1], parts)
            total = total + dot_nt(spread, foh[i, :, lanes])
        dcp[...] += total.reshape(parts, C0, LOW_B)

    def fine_back(j, lanes):
        kept = fin[16:48, lanes].astype(F32) > 0
        fgr[32:64, lanes] = jnp.where(kept, dot(w_skip, fgr[0:32, lanes]), 0.0).astype(BF16)

    every_slot(fine_gather, 8)
    every_slot(fine_join, 8)
    loss = lax.fori_loop(0, slots // span, fine_loss, jnp.zeros((1, span), F32), unroll=8)
    every_slot(fine_fused, 8)
    dcp[...] = jnp.zeros_like(dcp)
    every_slot(fine_scatter, 4)

    other = (1 - sub) * my_parts
    own = sub * my_parts
    give_dup = sibling(3, dcp.at[pl.ds(other, my_parts)], dcr)
    give_dup.start()
    every_slot(fine_back, 8)
    ga[...] = jnp.zeros_like(ga)
    for start in range(0, slots, 4 * span):
        lanes = slice(start, start + 4 * span)
        ga[:, 0:80] += dot_nt(fin[:, lanes], fgr[:, lanes])
    give_dup.wait_recv()

    def own_half(partial, received):
        return jnp.concatenate(
            [partial[own + part] + received[part] for part in range(my_parts)], 1
        )

    dup_low = own_half(dcp, dcr).astype(BF16)
    dblock = dot(w_up, dup_low)
    dbranch_low = dblock.astype(BF16)
    dmixed = dot(w_out, dbranch_low)

    def group_sum(values):
        return jnp.concatenate(
            [
                jnp.sum(values[8 * g : 8 * g + 8], axis=0, keepdims=True)
                for g in range(GROUPS)
            ],
            0,
        )

    def expand(values):
        return jnp.concatenate(
            [jnp.broadcast_to(values[g : g + 1], (8, values.shape[1])) for g in range(GROUPS)], 0
        )

    centred = group_sum(dmixed * mixed_ref[...])

    def back_score(k, lanes):
        ds2 = sc[:, lanes] * (group_sum(dmixed * car[:, lanes]) - centred)
        gst[128:144, lanes] = jnp.concatenate([ds2, zeros8], 0).astype(BF16)

    def back_act(k, lanes):
        scores = gst[128:144, lanes]
        kept = est[128:144, lanes].astype(F32)[0:8] > 0
        ds1 = jnp.where(kept, dot(w_att2, scores), 0.0)
        ds2 = scores.astype(F32)[0:8]
        gst[128:144, lanes] = jnp.concatenate([ds1, ds2], 0).astype(BF16)

    def back_edge(k, lanes):
        small = gst[128:144, lanes]
        dcarried = expand(sc[:, lanes]) * dmixed
        gst[64:128, lanes] = (dot(w_att1, small) + dcarried).astype(BF16)
        index = cnbr_ref[pl.ds(k, 1), pl.ds(half_at, half)]
        high = lax.shift_right_logical(index, low_shift)
        spread = place(jnp.concatenate([dcarried, small.astype(F32)[0:8]], 0), high, parts)
        dkp[...] += dot_nt(spread, ohs[:, lanes]).reshape(parts, C1 + 8, LOW_B)

    def back_pos(k, lanes):
        kept = est[64:128, lanes].astype(F32) > 0
        gst[0:64, lanes] = jnp.where(kept, dot(w_pos2, gst[64:128, lanes]), 0.0).astype(BF16)

    every_edge(back_score, 16)
    every_edge(back_act, 16)
    dkp[...] = jnp.zeros_like(dkp)
    every_edge(back_edge, 16)
    give_dkv = sibling(4, dkp.at[pl.ds(other, my_parts)], dkr)
    give_dkv.start()
    every_edge(back_pos, 16)
    inputs = jnp.concatenate(
        [blk_ref[...].astype(BF16), mixed_ref[...].astype(BF16), jnp.ones((16, half), BF16)], 0
    )
    grads = jnp.concatenate([dup_low, jnp.zeros((C0, half), BF16), dbranch_low], 0)
    gd[...] = dot_nt(inputs, grads)
    gc[...] = jnp.zeros_like(gc)
    ge[...] = jnp.zeros_like(ge)
    for start in range(0, edges, 4 * span):
        lanes = slice(start, start + 4 * span)
        result = dot_nt(est[:, lanes], gst[:, lanes])
        gc[...] += result[:, 0:128]
        ge[:, 0:16] += result[:, 128:144]
    ds1_total = tree(
        jnp.add,
        [gst[128:144, k * half : (k + 1) * half].astype(F32)[0:8] for k in range(NEIGH)],
    )
    w_att1_thrice = jnp.concatenate(
        [w1[0:C1, 0:8]] * 3 + [jnp.zeros((C1, 8), F32)], 1
    ).astype(BF16)

    def three_parts(values):
        high = values.astype(BF16).astype(F32)
        middle = (values - high).astype(BF16).astype(F32)
        low = values - high - middle
        return jnp.concatenate([high, middle, low, jnp.zeros_like(low)], 0).astype(BF16)

    dqueries = dot(w_att1_thrice, three_parts(ds1_total))
    give_dkv.wait_recv()
    dkv = own_half(dkp, dkr)
    dkeys = -dot(w_att1_thrice, three_parts(dkv[C1 : C1 + 8]))
    dqkv_low = jnp.concatenate([dqueries, dkeys, dkv[0:C1]], 0).astype(BF16)
    gbuf[...] = jnp.zeros_like(gbuf)
    gbuf[0:64, :] = dot_nt(pooled_ref[...].astype(BF16), dqkv_low[0:128])
    gbuf[64:128, 0:64] = dot_nt(pooled_ref[...].astype(BF16), dqkv_low[128:192])
    dpooled = dblock + dot(w_qkv, dqkv_low)

    gb[...] = jnp.zeros_like(gb)
    gb[0:16, 0:C1] = dot_nt(centre_low, (-dpooled).astype(BF16))
    dscaled = dpooled * rsum_ref[...]

    def pool_back(k, lanes):
        dpin = (pin[:, lanes] * dscaled).astype(BF16)
        gst[0:64, lanes] = dpin
        kept = cat[16:48, lanes].astype(F32) > 0
        gst[64:96, lanes] = jnp.where(kept, dot(w_down_stem, dpin), 0.0).astype(BF16)

    every_edge(pool_back, 16)
    for start in range(0, edges, 4 * span):
        lanes = slice(start, start + 4 * span)
        gb[:, 0:96] += dot_nt(cat[:, lanes], gst[0:96, lanes])

    left = lanes_of(64, LANES) < 64
    gd_out = gd[64:128, :]
    gbuf[64:128, :] = jnp.where(left, gbuf[64:128, :], gc[64:128, :])
    gbuf[128:160, :] = jnp.where(left[0:32], pltpu.roll(gd_out[0:32], 64, 1), gd_out[32:64])
    base = 160
    pack(gbuf, base, ga, 0, 32, OFF["w_stem"], 6, C0)
    pack(gbuf, base, gb, 0, 64, OFF["w_stem"], 6, C0)
    pack(gbuf, base, ga, 7, 32, OFF["b_stem"], 1, C0)
    pack(gbuf, base, gb, 7, 64, OFF["b_stem"], 1, C0)
    pack(gbuf, base, gb, 0, 0, OFF["w_down"], 3, C1)
    pack(gbuf, base, gb, 16, 0, OFF["w_down"] + 3 * C1, C0, C1)
    pack(gbuf, base, gb, 7, 0, OFF["b_down"], 1, C1)
    pack(gbuf, base, gc, 136, 0, OFF["w_pos"], 3, C1)
    pack(gbuf, base, gc, 143, 0, OFF["b_pos"], 1, C1)
    pack(gbuf, base, ge, 0, 0, OFF["w_att1"], C1, GROUPS)
    pack(gbuf, base, ge, 143, 0, OFF["b_att1"], 1, GROUPS)
    pack(gbuf, base, ge, 128, 8, OFF["w_att2"], GROUPS, GROUPS)
    pack(gbuf, base, ge, 143, 8, OFF["b_att2"], 1, GROUPS)
    pack(gbuf, base, gd, 0, 0, OFF["w_up"], C1, C0)
    pack(gbuf, base, gd, 128, 0, OFF["b_up"], 1, C0)
    pack(gbuf, base, ga, 16, 0, OFF["w_skip"], C0, C0)
    pack(gbuf, base, ga, 48, 64, OFF["w_head"], C0, NCLS)
    pack(gbuf, base, ga, 7, 64, OFF["b_head"], 1, NCLS)
    loss_sum = jnp.sum(loss, axis=1, keepdims=True)
    line, lane = divmod(FLAT, LANES)
    at_loss = lanes_of(1, LANES) == lane
    gbuf[base + line : base + line + 1, :] += jnp.where(at_loss, loss_sum, 0.0)

    rows = gbuf.shape[0] // n_sub
    shards = rows // 8
    give_grad = sibling(5, gbuf.at[pl.ds(pl.multiple_of((1 - sub) * rows, rows), rows)], gsib)
    give_grad.start()
    give_grad.wait_recv()
    ghalf[...] = gbuf[pl.ds(pl.multiple_of(sub * rows, rows), rows), :] + gsib[...]
    mine_at = pl.multiple_of(sub * rows + me * 8, 8)

    def shard_copy(peer, index):
        return pltpu.make_async_remote_copy(
            src_ref=ghalf.at[pl.ds(pl.multiple_of(peer * 8, 8), 8)],
            dst_ref=gsh.at[index],
            send_sem=red_send.at[peer],
            recv_sem=red_recv.at[index],
            device_id={"pts": peer},
            device_id_type=MESH,
        )

    def sum_copy(peer, index):
        at = pl.multiple_of(sub * rows + index * 8, 8)
        return pltpu.make_async_remote_copy(
            src_ref=gfull.at[pl.ds(at, 8)],
            dst_ref=gfull.at[pl.ds(at, 8)],
            send_sem=gat_send.at[peer],
            recv_sem=gat_recv.at[index],
            device_id={"pts": peer},
            device_id_type=MESH,
        )

    holds = None if n_pts <= shards else me < shards

    def when(condition, run):
        if condition is None:
            run()
        else:
            pl.when(condition)(run)

    def each_peer(run, limited):
        def body(step, carry):
            peer = partner(step)
            when(None if holds is None or not limited else peer < shards, lambda: run(peer))
            return carry

        lax.fori_loop(1, n_pts, body, 0)

    each_peer(lambda peer: shard_copy(peer, me).start(), True)

    def reduce():
        gsh[me] = ghalf[pl.ds(pl.multiple_of(me * 8, 8), 8), :]
        each_peer(lambda peer: shard_copy(peer, peer).wait_recv(), False)
        gfull[pl.ds(mine_at, 8), :] = jnp.sum(gsh[...], axis=0)
        each_peer(lambda peer: sum_copy(peer, me).start(), False)

    when(holds, reduce)
    each_peer(lambda peer: sum_copy(peer, peer).wait_recv(), True)
    half_rows = gfull.at[pl.ds(pl.multiple_of(sub * rows, rows), rows)]
    give_full = sibling(6, half_rows, half_rows)
    give_full.start()

    each_peer(lambda peer: block_copy(peer, me).wait_send(), False)
    each_peer(lambda peer: mat_copy(peer, me).wait_send(), False)
    each_peer(lambda peer: shard_copy(peer, me).wait_send(), True)
    when(holds, lambda: each_peer(lambda peer: sum_copy(peer, me).wait_send(), False))
    for copy in (forward, give_pooled, give_block, give_dup, give_dkv, give_grad, give_full):
        copy.wait_send()
    give_full.wait_recv()
    out_ref[...] = gfull[...]


def normalised(matrix):
    return matrix * lax.rsqrt(jnp.sum(matrix * matrix, axis=0, keepdims=True))


def gram_schmidt_pair(matrix, width=8):
    size = matrix.shape[0]
    left = lanes_of(size, 2 * size) < size
    column = lanes_of(1, 2 * size)
    left_row = column < size
    place_row = jnp.where(left_row, column, column - size)

    def spread(values, halves, at):
        return jnp.where(halves, values[:, at : at + 1], values[:, size + at : size + at + 1])

    for first in range(0, size, width):
        span = range(width)
        pivots = [spread(matrix, left, first + i) for i in span]
        products = [jnp.sum(pivot * matrix, axis=0, keepdims=True) for pivot in pivots]
        gram = [
            [spread(products[i], left_row, first + l) if l >= i else None for l in span]
            for i in span
        ]
        taken = 0.0
        for i in span:
            inverse = 1.0 / gram[i][i]
            for l in range(i + 1, width):
                part = gram[i][l] * inverse
                pivots[l] = pivots[l] - part * pivots[i]
                products[l] = products[l] - part * products[i]
                for m in range(l, width):
                    gram[l][m] = gram[l][m] - part * gram[i][m]
            factor = jnp.where(place_row > first + i, products[i] * inverse, 0.0)
            taken = taken + pivots[i] * factor
        matrix = matrix - taken
    return normalised(matrix)


def careful_pair(matrix):
    size = matrix.shape[0]
    lane = lanes_of(size, 2 * size)
    left = lane < size
    place = jnp.where(left, lane, lane - size)

    def column(j, matrix):
        here = jnp.where(place == j, matrix, 0.0)
        first = jnp.sum(jnp.where(left, here, 0.0), axis=1, keepdims=True)
        second = jnp.sum(jnp.where(left, 0.0, here), axis=1, keepdims=True)
        pivot = jnp.where(left, first, second)
        pivot = pivot * lax.rsqrt(jnp.sum(pivot * pivot, axis=0, keepdims=True))
        factor = jnp.sum(pivot * matrix, axis=0, keepdims=True)
        return matrix - jnp.where(place > j, pivot * factor, 0.0)

    for repeat in range(2):
        matrix = normalised(lax.fori_loop(0, size, column, matrix))
    return matrix


def departure(basis):
    size = basis.shape[0]
    same = rows_of(size, size) == lanes_of(size, size)
    return exact(basis, basis, ((0,), (0,))) - jnp.where(same, 1.0, 0.0)


def correct(basis, error):
    size = basis.shape[0]
    above = rows_of(size, size) < lanes_of(size, size)
    same = rows_of(size, size) == lanes_of(size, size)
    factor = jnp.where(above, error, jnp.where(same, 0.5 * error, 0.0))
    return basis - exact(basis, factor)


def orthonormal_pair(matrix, both_ref):
    size = matrix.shape[0]
    once = gram_schmidt_pair(matrix)
    halves = [once[:, 0:size], once[:, size : 2 * size]]
    errors = [departure(half) for half in halves]
    worst = jnp.max(jnp.maximum(jnp.abs(errors[0]), jnp.abs(errors[1])))
    halves = [correct(half, error) for half, error in zip(halves, errors)]
    both_ref[...] = jnp.concatenate(halves, 1)

    @pl.when(worst > 1e-4)
    def _():
        again = [both_ref[:, 0:size], both_ref[:, size : 2 * size]]
        both_ref[...] = jnp.concatenate([correct(half, departure(half)) for half in again], 1)

    @pl.when(jnp.logical_not(worst < 0.01))
    def _():
        both_ref[...] = careful_pair(matrix)

    return both_ref[...]


def soap_kernel(
    grads_ref,
    owner_ref,
    step_ref,
    weight_ref,
    first_ref,
    second_ref,
    left_ref,
    right_ref,
    basis_l_ref,
    basis_r_ref,
    average_ref,
    flat_ref,
    flat_mom_ref,
    flat_sec_ref,
    flat_ema_ref,
    weight_out,
    first_out,
    second_out,
    left_out,
    right_out,
    basis_l_out,
    basis_r_out,
    average_out,
    flat_out,
    flat_mom_out,
    flat_sec_out,
    flat_ema_out,
    loss_out,
    norm_out,
    both_ref,
):
    me = lax.axis_index("pts")
    grads = grads_ref[...]
    line, lane = divmod(FLAT, LANES)
    place_row = rows_of(256, LANES)
    at_loss = (place_row == 160 + line) & (lanes_of(256, LANES) == lane)
    loss = jnp.where(at_loss, grads, 0.0)
    loss_out[...] = jnp.sum(jnp.sum(loss, axis=0, keepdims=True), axis=1, keepdims=True)
    cleaned = jnp.where(at_loss, 0.0, grads)
    squares = jnp.sum(jnp.sum(cleaned * cleaned, axis=0, keepdims=True), axis=1, keepdims=True)
    norm = jnp.sqrt(squares)
    norm_out[...] = norm
    factor = jnp.minimum(1.0, CLIP_NORM / norm)
    count = jnp.full((1, 1), step_ref[0].astype(F32), F32)
    one_scale = 1.0 - jnp.exp(count * math.log(BETA_ONE))
    two_scale = 1.0 - jnp.exp(count * math.log(BETA_TWO))
    lines = FLAT_ROWS - 8

    def as_line(values):
        return jnp.broadcast_to(values, (lines, LANES)).reshape(lines * LANES)[0:FLAT]

    flat_grad = (cleaned[160 : 160 + lines] * factor).reshape(lines * LANES)[0:FLAT]
    flat_mom = BETA_ONE * flat_mom_ref[...] + (1.0 - BETA_ONE) * flat_grad
    flat_sec = BETA_TWO * flat_sec_ref[...] + (1.0 - BETA_TWO) * flat_grad * flat_grad
    flat_scaled = flat_mom / as_line(one_scale) / (jnp.sqrt(flat_sec / as_line(two_scale)) + ADAM_EPS)
    flat_new = flat_ref[...] - LEARN_RATE * (flat_scaled + WEIGHT_DECAY * flat_ref[...])
    flat_out[...] = flat_new
    flat_mom_out[...] = flat_mom
    flat_sec_out[...] = flat_sec
    flat_ema_out[...] = EMA_KEEP * flat_ema_ref[...] + (1.0 - EMA_KEEP) * flat_new
    folded = cleaned[128:160]
    stacked = [
        cleaned[0:64, 0:64],
        cleaned[0:64, 64:128],
        cleaned[64:128, 0:64],
        cleaned[64:128, 64:128],
        jnp.concatenate([folded[:, 0:64], folded[:, 64:128]], 0),
    ]
    grad = jnp.zeros((C1, C1), F32)
    owned = 0.0
    for position in range(NMATS):
        flag = jnp.where(owner_ref[position] == me, 1.0, 0.0)
        grad = grad + flag * stacked[position]
        owned = owned + flag
    raw = grad
    scale = (1.0 - BETA_TWO) * (factor * factor)
    grad = grad * factor
    basis_l = basis_l_ref[...]
    basis_r = basis_r_ref[...]
    left_new = BETA_TWO * left_ref[...] + scale * exact(raw, raw, ((1,), (1,)))
    right_new = BETA_TWO * right_ref[...] + scale * exact(raw, raw, ((0,), (0,)))
    both = orthonormal_pair(
        jnp.concatenate([exact(left_new, basis_l), exact(right_new, basis_r)], 1), both_ref
    )
    basis_l_new = both[:, 0:C1]
    basis_r_new = both[:, C1 : 2 * C1]
    rotated = exact(exact(basis_l, grad, ((0,), (0,))), basis_r)
    first_new = BETA_ONE * first_ref[...] + (1.0 - BETA_ONE) * rotated
    second_new = BETA_TWO * second_ref[...] + (1.0 - BETA_TWO) * rotated * rotated
    scaled = first_new / one_scale / (jnp.sqrt(second_new / two_scale) + ADAM_EPS)
    weight = weight_ref[...]
    weight_new = weight - LEARN_RATE * (
        exact(exact(basis_l, scaled), basis_r, ((1,), (1,))) + WEIGHT_DECAY * weight
    )
    plain = exact(exact(basis_l, first_new), basis_r, ((1,), (1,)))
    first_rotated = exact(exact(basis_l_new, plain, ((0,), (0,))), basis_r_new)
    average_new = EMA_KEEP * average_ref[...] + (1.0 - EMA_KEEP) * weight_new
    held = owned > 0.5
    weight_out[...] = jnp.where(held, weight_new, 0.0)
    first_out[...] = jnp.where(held, first_rotated, 0.0)
    second_out[...] = jnp.where(held, second_new, 0.0)
    left_out[...] = jnp.where(held, left_new, 0.0)
    right_out[...] = jnp.where(held, right_new, 0.0)
    basis_l_out[...] = jnp.where(held, basis_l_new, 0.0)
    basis_r_out[...] = jnp.where(held, basis_r_new, 0.0)
    average_out[...] = jnp.where(held, average_new, 0.0)


def local(
    points,
    route,
    labels,
    interp_src,
    pool_nbr,
    sample,
    coarse_nbr,
    owner,
    step,
    flat,
    flat_mom,
    flat_sec,
    flat_ema,
    mats,
    mats_mom,
    mats_sec,
    mats_left,
    mats_right,
    mats_basis_l,
    mats_basis_r,
    mats_ema,
):
    n_pts = lax.axis_size("pts")
    n_sub = lax.axis_size("sub")
    fine = points.shape[0]
    coarse = sample.shape[0]
    cap = n_sub * fine // n_pts
    slots = n_pts * cap
    sources = n_sub * n_pts
    half = coarse // n_sub
    edges = NEIGH * half
    parts = coarse // LOW_B
    my_parts = parts // n_sub
    vmem = pl.BlockSpec(memory_space=pltpu.VMEM)
    smem = pl.BlockSpec(memory_space=pltpu.SMEM)
    dma = pltpu.SemaphoreType.DMA
    scratch = [
        VMEM((6, fine), BF16),
        VMEM((1, fine), I32),
        VMEM((1, fine), I32),
        VMEM((3, fine), I32),
        VMEM((NEIGH, coarse), I32),
        VMEM((1, coarse), I32),
        VMEM((NEIGH, coarse), I32),
        pltpu.SMEM((NMATS,), I32),
        VMEM((C1, C1), F32),
        VMEM((FLAT,), F32),
        VMEM((FLAT_ROWS, LANES), F32),
        VMEM((LOW_B, LANES), BF16),
        VMEM((16, fine), F32),
        VMEM((n_pts * 16, cap), F32),
        VMEM((n_pts, 16, cap), BF16),
        VMEM((sources, 16, cap), BF16),
        VMEM((32, LANES), BF16),
        VMEM((n_pts, 32, LANES), BF16),
        VMEM((sources * 8, cap), BF16),
        VMEM((8, coarse), F32),
        VMEM((C1, edges), F32),
        VMEM((48, edges), BF16),
        VMEM((C1, half), F32),
        VMEM((C1, half), F32),
        VMEM((n_sub, my_parts * CH, LOW_B), BF16),
        VMEM((n_sub, my_parts * CH, LOW_B), BF16),
        VMEM((C1, edges), BF16),
        VMEM((144, edges), BF16),
        VMEM((144, edges), BF16),
        VMEM((LOW_B, edges), BF16),
        VMEM((C1, edges), F32),
        VMEM((GROUPS, edges), F32),
        VMEM((C1, half), F32),
        VMEM((C1, half), F32),
        VMEM((16, slots), F32),
        VMEM((80, slots), BF16),
        VMEM((80, slots), BF16),
        VMEM((C0, slots), F32),
        VMEM((3, LOW_B, slots), BF16),
        VMEM((3, C1, slots), BF16),
        VMEM((8, slots), F32),
        VMEM((parts, C0, LOW_B), F32),
        VMEM((my_parts, C0, LOW_B), F32),
        VMEM((parts, C1 + 8, LOW_B), F32),
        VMEM((my_parts, C1 + 8, LOW_B), F32),
        VMEM((LANES, LANES), F32),
        VMEM((LANES, LANES), F32),
        VMEM((LANES, LANES), F32),
        VMEM((LANES, LANES), F32),
        VMEM((LANES, LANES), F32),
        VMEM((LANES, LANES), F32),
        VMEM((LANES, LANES), F32),
        VMEM((LANES, LANES), F32),
        VMEM((LANES, LANES), F32),
        VMEM((80, LANES), F32),
        VMEM((48, LANES), F32),
        VMEM((144, LANES), F32),
        VMEM((144, LANES), F32),
        VMEM((144, LANES), F32),
        VMEM((256, LANES), F32),
        VMEM((128, LANES), F32),
        VMEM((128, LANES), F32),
        VMEM((n_pts, 8, LANES), F32),
        VMEM((256, LANES), F32),
        dma((n_pts,)),
        dma((n_pts,)),
        dma((n_pts,)),
        dma((n_pts,)),
        dma((n_pts,)),
        dma((n_pts,)),
        dma((n_pts,)),
        dma((n_pts,)),
        dma((8,)),
        dma((8,)),
        dma((10,)),
    ]
    reduced = pl.pallas_call(
        functools.partial(main_kernel, n_pts, n_sub),
        out_shape=jax.ShapeDtypeStruct((256, LANES), F32),
        in_specs=[pl.BlockSpec(memory_space=pltpu.HBM)] * 10,
        out_specs=vmem,
        scratch_shapes=scratch,
        compiler_params=pltpu.CompilerParams(
            collective_id=0, has_side_effects=True, vmem_limit_bytes=60 * 1024 * 1024
        ),
    )(
        points.T,
        route.reshape(1, fine),
        labels.reshape(1, fine),
        interp_src.T,
        pool_nbr.T,
        sample.reshape(1, coarse),
        coarse_nbr.T,
        owner,
        mats[0],
        flat,
    )
    square = jax.ShapeDtypeStruct((C1, C1), F32)
    line = jax.ShapeDtypeStruct((FLAT,), F32)
    single = jax.ShapeDtypeStruct((1, 1), F32)
    results = pl.pallas_call(
        soap_kernel,
        out_shape=[square] * 8 + [line] * 4 + [single] * 2,
        in_specs=[vmem] + [smem] * 2 + [vmem] * 12,
        out_specs=[vmem] * 14,
        scratch_shapes=[VMEM((C1, 2 * C1), F32)],
    )(
        reduced,
        owner,
        step,
        mats[0],
        mats_mom[0],
        mats_sec[0],
        mats_left[0],
        mats_right[0],
        mats_basis_l[0],
        mats_basis_r[0],
        mats_ema[0],
        flat,
        flat_mom,
        flat_sec,
        flat_ema,
    )
    scalars = (results[12].reshape(()), results[13].reshape(()))
    return scalars + tuple(results[8:12]) + tuple(result[None] for result in results[:8])


def solution(mesh):
    placed = (
        P(("pts", "sub"), None),
        P(("pts", "sub")),
        P(("pts", "sub")),
        P(("pts", "sub"), None),
        P("pts", None),
        P("pts"),
        P("pts", None),
        P(),
        P(),
        P(),
        P(),
        P(),
        P(),
    ) + (P("pts", None, None),) * 8
    mapped = jax.shard_map(
        local,
        mesh=mesh,
        in_specs=placed,
        out_specs=(P(),) * 6 + (P("pts", None, None),) * 8,
        check_vma=False,
    )

    def run(*arrays):
        with jax.sharding.use_abstract_mesh(mesh.abstract_mesh):
            return mapped(*arrays)

    return run
```

```python
import functools
import math

import jax
import jax.numpy as jnp
from jax import lax
from jax.experimental import pallas as pl
from jax.experimental.pallas import tpu as pltpu
from jax.sharding import PartitionSpec as P

C0 = 32
C1 = 64
NEIGH = 16
NCLS = 13
GROUPS = 8
NMATS = 5

HIGHEST = lax.Precision.HIGHEST
CLIP_NORM = 0.01
BETA_ONE = 0.9
BETA_TWO = 0.95
ADAM_EPS = 1e-08
LEARN_RATE = 0.1
WEIGHT_DECAY = 0.01
EMA_KEEP = 0.9
INTERP_EPS = 0.01

F32 = jnp.float32
BF16 = jnp.bfloat16
I32 = jnp.int32
MESH = pl.DeviceIdType.MESH
VMEM = pltpu.VMEM

LANES = 128
FLAT_ROWS = 64
LOW_B = 256
CH = 72
NEG = -1e30


def offsets():
    shapes = [
        ("w_stem", (6, C0)),
        ("b_stem", (C0,)),
        ("w_down", (3 + C0, C1)),
        ("b_down", (C1,)),
        ("w_pos", (3, C1)),
        ("b_pos", (C1,)),
        ("w_att1", (C1, GROUPS)),
        ("b_att1", (GROUPS,)),
        ("w_att2", (GROUPS, GROUPS)),
        ("b_att2", (GROUPS,)),
        ("w_up", (C1, C0)),
        ("b_up", (C0,)),
        ("w_skip", (C0, C0)),
        ("w_head", (C0, NCLS)),
        ("b_head", (NCLS,)),
    ]
    found = {}
    total = 0
    for name, shape in shapes:
        found[name] = total
        total += math.prod(shape)
    return found, total


OFF, FLAT = offsets()


def dot(left, right):
    return lax.dot_general(left, right, (((1,), (0,)), ((), ())), preferred_element_type=F32)


def dot_nt(left, right):
    return lax.dot_general(left, right, (((1,), (1,)), ((), ())), preferred_element_type=F32)


def exact(left, right, dims=((1,), (0,))):
    return lax.dot_general(
        left, right, (dims, ((), ())), precision=HIGHEST, preferred_element_type=F32
    )


def relu(values):
    return jnp.maximum(values, 0.0)


def rows_of(count, length):
    return lax.broadcasted_iota(I32, (count, length), 0)


def lanes_of(count, length):
    return lax.broadcasted_iota(I32, (count, length), 1)


def onehot(low, count):
    hit = rows_of(count, low.shape[1]) == low
    return jnp.where(hit, 1.0, 0.0).astype(BF16)


def stored_onehot(low, iota):
    count, length = iota.shape[0], low.shape[1]
    wanted = jnp.broadcast_to(low.astype(F32), (16, length)).astype(BF16)
    held = jnp.concatenate([iota] * (length // LANES), 1).reshape(count // 16, 16, length)
    hit = held == wanted[None]
    return jnp.where(hit, jnp.ones((), BF16), jnp.zeros((), BF16)).reshape(count, length)


def pick(spread, high, parts):
    each = spread.shape[0] // parts
    found = spread[0:each]
    for part in range(1, parts):
        found = jnp.where(high == part, spread[part * each : (part + 1) * each], found)
    return found


def place(values, high, parts):
    return jnp.concatenate(
        [jnp.where(high == part, values, 0.0) for part in range(parts)], 0
    ).astype(BF16)


def unpack(flat_ref, out_ref, offset, rows, width, at):
    stride = LANES // width if LANES % width == 0 else rows
    for first in range(min(stride, rows)):
        count = (rows - first + stride - 1) // stride
        padded = -(-count // 8) * 8
        line, lane = divmod(offset + first * width, LANES)
        values = flat_ref[line : line + padded, :]
        if lane:
            values = pltpu.roll(values, LANES - lane, 1)
        if lane + width > LANES:
            following = pltpu.roll(flat_ref[line + 1 : line + 1 + padded, :], LANES - lane, 1)
            values = jnp.where(lanes_of(padded, LANES) < LANES - lane, values, following)
        values = jnp.where(lanes_of(padded, LANES) < width, values, 0.0)
        if count == 1:
            out_ref[at + first : at + first + 1, :] = values[0:1]
        else:
            out_ref[pl.ds(at + first, count, stride=stride), :] = values[0:count]


def pack(out_ref, base, source_ref, row, lane_from, offset, rows, width):
    stride = LANES // width if LANES % width == 0 else rows
    for first in range(min(stride, rows)):
        count = (rows - first + stride - 1) // stride
        line, lane = divmod(offset + first * width, LANES)
        if count == 1:
            values = source_ref[row + first : row + first + 1, :]
        else:
            values = source_ref[pl.ds(row + first, count, stride=stride), :]
        shift = (lane - lane_from) % LANES
        padded = -(-count // 8) * 8
        if padded != count:
            values = jnp.concatenate([values, jnp.zeros((padded - count, LANES), F32)], 0)
        if shift:
            values = pltpu.roll(values, shift, 1)
        values = values[0:count]
        at = lanes_of(count, LANES)
        here = jnp.where((at >= lane) & (at < lane + width), values, 0.0)
        out_ref[base + line : base + line + count, :] += here
        if lane + width > LANES:
            there = jnp.where(at < lane + width - LANES, values, 0.0)
            out_ref[base + line + 1 : base + line + 1 + count, :] += there


def main_kernel(
    n_pts,
    n_sub,
    pts_hbm,
    route_hbm,
    labels_hbm,
    src_hbm,
    pool_hbm,
    sample_hbm,
    cnbr_hbm,
    owner_hbm,
    mats_hbm,
    flat_hbm,
    out_ref,
    pts_ref,
    route_ref,
    labels_ref,
    src_ref,
    pool_ref,
    sample_ref,
    cnbr_ref,
    owner_ref,
    mats_ref,
    flat_line,
    flat_ref,
    iota_ref,
    data,
    sacc,
    sendb,
    recv,
    matmine,
    matall,
    tabb,
    cen,
    pin,
    cat,
    pooled_ref,
    rsum_ref,
    ctab,
    btab,
    near,
    est,
    gst,
    ohs,
    car,
    sc,
    mixed_ref,
    blk_ref,
    slot,
    fin,
    fgr,
    skp,
    foh,
    fsrc,
    fwt,
    dcp,
    dcr,
    dkp,
    dkr,
    wst,
    wd,
    wp,
    w1,
    w2,
    wu,
    wsk,
    wh,
    bias,
    ga,
    gb,
    gc,
    gd,
    ge,
    gbuf,
    gsib,
    ghalf,
    gsh,
    gfull,
    a2a_send,
    a2a_recv,
    mat_send,
    mat_recv,
    red_send,
    red_recv,
    gat_send,
    gat_recv,
    sib_send,
    sib_recv,
    load_sem,
):
    fine = route_ref.shape[1]
    coarse = sample_ref.shape[1]
    cap = sendb.shape[2]
    slots = n_pts * cap
    half = coarse // n_sub
    edges = NEIGH * half
    sources = n_sub * n_pts
    parts = coarse // LOW_B
    my_parts = parts // n_sub
    shift = cap.bit_length() - 1
    low_shift = LOW_B.bit_length() - 1
    span = 512
    me = lax.axis_index("pts")
    sub = lax.axis_index("sub")
    half_at = pl.multiple_of(sub * half, half)

    far_refs = (pts_hbm, route_hbm, labels_hbm, src_hbm, mats_hbm, sample_hbm, pool_hbm, cnbr_hbm, owner_hbm)
    near_refs = (pts_ref, route_ref, labels_ref, src_ref, mats_ref, sample_ref, pool_ref, cnbr_ref, owner_ref)
    loads = [
        pltpu.make_async_copy(source, target, load_sem.at[number])
        for number, (source, target) in enumerate(zip(far_refs, near_refs))
    ]
    loads.append(
        pltpu.make_async_copy(flat_hbm, flat_line, load_sem.at[len(loads)])
    )
    for load in loads:
        load.start()

    barrier = pltpu.get_barrier_semaphore()

    powers = [2**k for k in range(n_pts.bit_length() - 1)]
    my_bits = [lax.bitwise_and(lax.shift_right_logical(me, k), 1) for k in range(len(powers))]

    def partner(step):
        step = n_pts - step
        found = 0
        for k, power in enumerate(powers):
            bit = lax.bitwise_and(my_bits[k] + lax.shift_right_logical(step, k), 1)
            found = found + power * bit
        return found

    def greet(step, carry):
        peer = partner(step)
        pl.semaphore_signal(barrier, inc=1, device_id={"pts": peer}, device_id_type=MESH)
        return carry

    lax.fori_loop(1, n_pts, greet, 0)
    pl.semaphore_signal(barrier, inc=1, device_id={"sub": 1 - sub}, device_id_type=MESH)

    def sibling(number, source, target):
        return pltpu.make_async_remote_copy(
            src_ref=source,
            dst_ref=target,
            send_sem=sib_send.at[number],
            recv_sem=sib_recv.at[number],
            device_id={"sub": 1 - sub},
            device_id_type=MESH,
        )

    iota_ref[...] = rows_of(LOW_B, LANES).astype(F32).astype(BF16)
    for load in loads[0:5] + loads[9:]:
        load.wait()
    data[0:6, :] = pts_ref[...].astype(F32)
    data[6:8, :] = jnp.zeros((2, fine), F32)
    source_rows = src_ref[...]
    data[8:11, :] = lax.shift_right_logical(source_rows, 5).astype(F32)
    data[11:14, :] = (source_rows & 31).astype(F32)
    data[14:15, :] = (labels_ref[...] + 1).astype(F32)
    data[15:16, :] = jnp.zeros((1, fine), F32)
    sacc[...] = jnp.zeros_like(sacc)
    counts = jnp.zeros((16, 32), F32)
    for chunk in range(fine // span):
        lanes = slice(chunk * span, (chunk + 1) * span)
        route = route_ref[:, lanes]
        high = lax.shift_right_logical(route, shift)
        spread = place(data[:, lanes], high, n_pts)
        sacc[...] += dot_nt(spread, onehot(route & (cap - 1), cap))
        classes = onehot(labels_ref[:, lanes], 16)
        counts = counts + dot_nt(jnp.ones((16, span), BF16), jnp.concatenate([classes, classes], 0))
    count_high = jnp.floor(counts * (1.0 / 128.0))
    count_low = counts - 128.0 * count_high
    digits = jnp.where(lanes_of(16, 32) < 16, count_low, count_high)
    digits = jnp.where(rows_of(16, 32) == 15, digits, 0.0)
    data[:, 0:cap] = jnp.zeros((16, cap), F32)
    data[:, 0:32] = digits
    sendb[...] = (sacc[...].reshape(n_pts, 16, cap) + data[:, 0:cap][None]).astype(BF16)
    matrix = mats_ref[...]
    matmine[...] = jnp.concatenate([matrix[0:32], matrix[32:64]], 1).astype(BF16)

    pl.semaphore_wait(barrier, n_pts)

    def block_copy(peer, index):
        return pltpu.make_async_remote_copy(
            src_ref=sendb.at[peer],
            dst_ref=recv.at[sub * n_pts + index],
            send_sem=a2a_send.at[peer],
            recv_sem=a2a_recv.at[index],
            device_id={"pts": peer},
            device_id_type=MESH,
        )

    def mat_copy(peer, index):
        return pltpu.make_async_remote_copy(
            src_ref=matmine,
            dst_ref=matall.at[index],
            send_sem=mat_send.at[peer],
            recv_sem=mat_recv.at[index],
            device_id={"pts": peer},
            device_id_type=MESH,
        )

    def send_blocks(step, carry):
        block_copy(partner(step), me).start()
        return carry

    def send_mats(step, carry):
        mat_copy(partner(step), me).start()
        return carry

    lax.fori_loop(1, n_pts, send_blocks, 0)
    recv[sub * n_pts + me] = sendb[me]
    matall[me] = matmine[...]

    for ref in (wst, wd, wp, w1, w2, wu, wsk, wh, bias):
        ref[...] = jnp.zeros_like(ref)
    padded = jnp.pad(flat_line[...], (0, FLAT_ROWS * LANES - FLAT))
    flat_ref[...] = padded.reshape(FLAT_ROWS, LANES)
    unpack(flat_ref, wst, OFF["w_stem"], 6, C0, 0)
    unpack(flat_ref, wd, OFF["w_down"], 3, C1, 0)
    unpack(flat_ref, wd, OFF["w_down"] + 3 * C1, C0, C1, 16)
    unpack(flat_ref, wp, OFF["w_pos"], 3, C1, 8)
    unpack(flat_ref, w1, OFF["w_att1"], C1, GROUPS, 0)
    unpack(flat_ref, w2, OFF["w_att2"], GROUPS, GROUPS, 0)
    unpack(flat_ref, wu, OFF["w_up"], C1, C0, 0)
    unpack(flat_ref, wsk, OFF["w_skip"], C0, C0, 0)
    unpack(flat_ref, wh, OFF["w_head"], C0, NCLS, 0)
    names = ("b_stem", "b_down", "b_pos", "b_att1", "b_att2", "b_up", "b_head")
    widths = (C0, C1, C1, GROUPS, GROUPS, C0, NCLS)
    for position, (name, width) in enumerate(zip(names, widths)):
        unpack(flat_ref, bias, OFF[name], 1, width, position)
    columns = bias[...].T
    b_stem = columns[0:C0, 0:1]
    b_down = columns[0:C1, 1:2]
    b_pos = columns[0:C1, 2:3]
    b_att1 = columns[0:GROUPS, 3:4]
    b_att2 = columns[0:GROUPS, 4:5]
    b_up = columns[0:C0, 5:6]
    b_head = jnp.where(rows_of(16, 1) < NCLS, columns[0:16, 6:7], NEG)
    w_stem_t = wst[...].T[0:C0, 0:16].astype(BF16)
    w_down_t = wd[...].T[0:C1, 0:48].astype(BF16)
    w_pos_t = wp[...].T[0:C1, 0:16].astype(BF16)
    w_att1_t = w1[...].T[0:GROUPS, 0:C1].astype(BF16)
    w_att2_t = w2[...].T[0:GROUPS, 0:16].astype(BF16)
    w_up_t = wu[...].T[0:C0, 0:C1].astype(BF16)
    w_skip_t = wsk[...].T[0:C0, 0:C0].astype(BF16)
    w_head_t = wh[...].T[0:16, 0:C0].astype(BF16)
    w_down_stem = wd[16:48, 0:C1].astype(BF16)
    w_att1 = w1[0:C1, 0:16].astype(BF16)
    w_att2 = w2[0:GROUPS, 0:16].astype(BF16)
    w_up = wu[0:C1, 0:C0].astype(BF16)
    w_skip = wsk[0:C0, 0:C0].astype(BF16)
    w_head = wh[0:C0, 0:16].astype(BF16)

    def wait_blocks(step, carry):
        peer = partner(step)
        block_copy(peer, peer).wait_recv()
        return carry

    lax.fori_loop(1, n_pts, wait_blocks, 0)
    lax.fori_loop(1, n_pts, send_mats, 0)
    for load in loads[5:9]:
        load.wait()
    mine = recv.at[pl.ds(sub * n_pts, n_pts)]
    forward = sibling(0, mine, mine)
    forward.start()
    for source in range(n_pts):
        slot[:, source * cap : (source + 1) * cap] = recv[sub * n_pts + source].astype(F32)

    def fill_table(side):
        came = recv[pl.ds(side * n_pts, n_pts)].astype(F32)
        rows = n_pts * 8
        ones_row = (rows_of(rows, cap) & 7) == 7
        filled = jnp.where(ones_row, 1.0, came[:, 0:8, :].reshape(rows, cap))
        tabb[pl.ds(pl.multiple_of(side * rows, rows), rows), :] = filled.astype(BF16)

    fill_table(sub)
    forward.wait_recv()

    fill_table(1 - sub)
    count_row = jnp.sum(recv[...].astype(F32)[:, 8:16, :], axis=0)[7:8, 0:32]
    count_at = jnp.broadcast_to(count_row, (16, 32))
    low_hit = lanes_of(16, 32) == rows_of(16, 32)
    high_hit = lanes_of(16, 32) == rows_of(16, 32) + 16
    class_counts = jnp.sum(
        jnp.where(low_hit, count_at, 0.0) + jnp.where(high_hit, 128.0 * count_at, 0.0),
        axis=1,
        keepdims=True,
    )
    total_fine = float(fine * n_pts * n_sub)
    class_w = jnp.where(
        rows_of(16, 1) < NCLS, total_fine / (NCLS * class_counts) * (1.0 / total_fine), 0.0
    )

    def gather_points(index):
        hot = stored_onehot(index & (cap - 1), iota_ref[0:cap, :])
        high = jnp.broadcast_to(lax.shift_right_logical(index, shift), (8, index.shape[1]))
        return pick(dot(tabb[...], hot), high, sources)

    zeros8 = jnp.zeros((8, span), F32)
    for chunk in range(coarse // span):
        lanes = slice(chunk * span, (chunk + 1) * span)
        found = gather_points(sample_ref[:, lanes])
        cen[:, lanes] = jnp.where(rows_of(8, span) < 6, found, 0.0)
    centre = cen[:, pl.ds(half_at, half)]
    centre_low = jnp.concatenate([centre, zeros8], 0).astype(BF16)
    w_xyz_t = jnp.where(lanes_of(C1, 16) < 3, wd[...].T[0:C1, 0:16], 0.0).astype(BF16)
    pool_base = b_down - dot(w_xyz_t, centre_low)

    def at_edge(k):
        return pl.ds(pl.multiple_of(k * half, half), half)

    def every_edge(step, unroll):
        def run(k, carry):
            step(k, at_edge(k))
            return carry

        lax.fori_loop(0, NEIGH, run, 0, unroll=unroll)

    def pool_gather(k, lanes):
        found = gather_points(pool_ref[pl.ds(k, 1), pl.ds(half_at, half)])
        cat[0:16, lanes] = jnp.concatenate([found, zeros8], 0).astype(BF16)

    def pool_stem(k, lanes):
        cat[16:48, lanes] = relu(dot(w_stem_t, cat[0:16, lanes]) + b_stem).astype(BF16)

    def pool_project(k, lanes):
        pin[:, lanes] = dot(w_down_t, cat[:, lanes]).astype(BF16).astype(F32) + pool_base

    every_edge(pool_gather, 4)
    every_edge(pool_stem, 16)
    every_edge(pool_project, 16)

    def tree(combine, values):
        while len(values) > 1:
            paired = [combine(values[i], values[i + 1]) for i in range(0, len(values) - 1, 2)]
            values = paired + ([values[-1]] if len(values) % 2 else [])
        return values[0]

    wide = 256

    def log_sum(r, carry):
        rows = pl.ds(pl.multiple_of(r * 8, 8), 8)
        for start in range(0, half, wide):
            spots = [slice(k * half + start, k * half + start + wide) for k in range(NEIGH)]
            values = [pin[rows, spot] for spot in spots]
            most = tree(jnp.maximum, values)
            values = [jnp.exp(value - most) for value in values]
            for spot, value in zip(spots, values):
                pin[rows, spot] = value
            total = tree(jnp.add, values)
            pooled_ref[rows, start : start + wide] = most + jnp.log(total)
            rsum_ref[rows, start : start + wide] = 1.0 / total
        return carry

    lax.fori_loop(0, C1 // 8, log_sum, 0, unroll=2)

    def table_rows(values, target):
        rows = []
        for part in range(my_parts):
            lanes = slice(part * LOW_B, (part + 1) * LOW_B)
            rows = rows + [values[:, lanes], centre[:, lanes]]
        target[sub] = jnp.concatenate(rows, 0).astype(BF16)

    table_rows(pooled_ref[...], ctab)
    my_ctab = ctab.at[sub]
    give_pooled = sibling(1, my_ctab, my_ctab)
    give_pooled.start()

    def wait_mats(step, carry):
        peer = partner(step)
        mat_copy(peer, peer).wait_recv()
        return carry

    lax.fori_loop(1, n_pts, wait_mats, 0)

    def layer(position):
        folded = matall[owner_ref[position]].astype(F32)
        return jnp.concatenate([folded[:, 0:C1], folded[:, C1 : 2 * C1]], 0)

    w_query, w_key, w_value, w_pos2_32, w_out_32 = [layer(position) for position in range(NMATS)]
    w_qkv = jnp.concatenate([w_query, w_key, w_value], 1).astype(BF16)
    w_query_t = w_query.T.astype(BF16)
    w_pos2 = w_pos2_32.astype(BF16)
    w_pos2_t = w_pos2_32.T
    w_edge_t = jnp.concatenate(
        [
            jnp.concatenate([-w_key.T, w_pos2_t], 1),
            jnp.concatenate([w_value.T, w_pos2_t], 1),
        ],
        0,
    ).astype(BF16)
    w_out = w_out_32.astype(BF16)
    w_out_t = w_out_32.T.astype(BF16)
    queries = dot(w_query_t, pooled_ref[...].astype(BF16))

    def at_slot(step):
        return pl.ds(pl.multiple_of(step * span, span), span)

    def every_slot(step, unroll):
        def run(j, carry):
            step(j, at_slot(j))
            return carry

        lax.fori_loop(0, slots // span, run, 0, unroll=unroll)

    def fine_points(j, lanes):
        ones = jnp.where(rows_of(8, span) == 7, 1.0, slot[0:8, lanes])
        fin[0:16, lanes] = jnp.concatenate([ones, zeros8], 0).astype(BF16)

    def fine_stem(j, lanes):
        fin[16:48, lanes] = relu(dot(w_stem_t, fin[0:16, lanes]) + b_stem).astype(BF16)

    def fine_skip(j, lanes):
        skp[:, lanes] = dot(w_skip_t, fin[16:48, lanes])

    every_slot(fine_points, 4)
    every_slot(fine_stem, 8)
    every_slot(fine_skip, 8)
    give_pooled.wait_recv()

    def attend_gather(k, lanes):
        index = cnbr_ref[pl.ds(k, 1), pl.ds(half_at, half)]
        hot = stored_onehot(index & (LOW_B - 1), iota_ref[...])
        ohs[:, lanes] = hot
        high = lax.shift_right_logical(index, low_shift)
        found = pick(dot(ctab[...].reshape(parts * CH, LOW_B), hot), high, parts)
        near[:, lanes] = found[0:C1].astype(BF16)
        offset = jnp.where(rows_of(8, half) == 7, 1.0, centre - found[C1 : C1 + 8])
        est[128:144, lanes] = jnp.concatenate([zeros8, offset], 0).astype(BF16)

    def attend_pos(k, lanes):
        est[64:128, lanes] = relu(dot(w_pos_t, est[128:144, lanes]) + b_pos).astype(BF16)

    def attend_edge(k, lanes):
        both = dot(w_edge_t, jnp.concatenate([near[:, lanes], est[64:128, lanes]], 0))
        est[0:64, lanes] = (queries + both[0:C1]).astype(BF16)
        car[:, lanes] = both[C1 : 2 * C1]

    def attend_act(k, lanes):
        act = relu(dot(w_att1_t, est[0:64, lanes]) + b_att1)
        offset = est[128:144, lanes].astype(F32)[8:16]
        est[128:144, lanes] = jnp.concatenate([act, offset], 0).astype(BF16)

    def attend_score(k, lanes):
        sc[:, lanes] = dot(w_att2_t, est[128:144, lanes]) + b_att2

    every_edge(attend_gather, 16)
    every_edge(attend_pos, 16)
    every_edge(attend_edge, 16)
    every_edge(attend_act, 16)
    every_edge(attend_score, 16)

    for start in range(0, half, wide):
        spots = [slice(k * half + start, k * half + start + wide) for k in range(NEIGH)]
        values = [sc[:, spot] for spot in spots]
        most = tree(jnp.maximum, values)
        values = [jnp.exp(value - most) for value in values]
        scale = 1.0 / tree(jnp.add, values)
        for spot, value in zip(spots, values):
            sc[:, spot] = value * scale

    for g in range(GROUPS):
        rows = slice(8 * g, 8 * g + 8)
        for start in range(0, half, wide):
            spots = [slice(k * half + start, k * half + start + wide) for k in range(NEIGH)]
            terms = [
                jnp.broadcast_to(sc[g : g + 1, spot], (8, wide)) * car[rows, spot]
                for spot in spots
            ]
            mixed_ref[rows, start : start + wide] = tree(jnp.add, terms)

    block = pooled_ref[...] + dot(w_out_t, mixed_ref[...].astype(BF16))
    blk_ref[...] = block
    table_rows(block, btab)
    my_btab = btab.at[sub]
    give_block = sibling(2, my_btab, my_btab)
    give_block.start()

    def source_of(lanes, i):
        index = (32.0 * slot[8 + i : 9 + i, lanes] + slot[11 + i : 12 + i, lanes]).astype(I32)
        return index & (LOW_B - 1), lax.shift_right_logical(index, low_shift)

    def fine_hot(j, lanes):
        for i in range(3):
            foh[i, :, lanes] = stored_onehot(source_of(lanes, i)[0], iota_ref[...])

    every_slot(fine_hot, 1)
    give_block.wait_recv()

    def fine_gather(j, lanes):
        points = slot[0:8, lanes]
        inverses = []
        for i in range(3):
            high = source_of(lanes, i)[1]
            found = pick(dot(btab[...].reshape(parts * CH, LOW_B), foh[i, :, lanes]), high, parts)
            fsrc[i, :, lanes] = found[0:C1].astype(BF16)
            diff = jnp.where(rows_of(8, span) < 3, points - found[C1 : C1 + 8], 0.0)
            inverses.append(1.0 / (jnp.sum(diff * diff, axis=0, keepdims=True) + INTERP_EPS))
        norm = 1.0 / (inverses[0] + inverses[1] + inverses[2])
        for i in range(3):
            fwt[i : i + 1, lanes] = inverses[i] * norm

    def fine_join(j, lanes):
        terms = [fwt[i : i + 1, lanes] * dot(w_up_t, fsrc[i, :, lanes]) for i in range(3)]
        interp = (terms[0] + terms[1] + terms[2] + b_up).astype(BF16).astype(F32)
        fin[48:80, lanes] = relu(interp + skp[:, lanes]).astype(BF16)

    def fine_loss(j, loss):
        lanes = at_slot(j)
        logits = dot(w_head_t, fin[48:80, lanes]) + b_head
        label = slot[14:15, lanes].astype(I32)
        hit = jnp.where(rows_of(16, span) + 1 == label, 1.0, 0.0)
        row_w = jnp.sum(hit * class_w, axis=0, keepdims=True)
        peak = jnp.max(logits, axis=0, keepdims=True)
        raised = jnp.exp(logits - peak)
        total = jnp.sum(raised, axis=0, keepdims=True)
        named = jnp.sum(hit * logits, axis=0, keepdims=True)
        fgr[64:80, lanes] = (row_w * (raised * (1.0 / total) - hit)).astype(BF16)
        return loss + row_w * (peak + jnp.log(total) - named)

    def fine_fused(j, lanes):
        kept = fin[48:80, lanes].astype(F32) > 0
        fgr[0:32, lanes] = jnp.where(kept, dot(w_head, fgr[64:80, lanes]), 0.0).astype(BF16)

    def fine_scatter(j, lanes):
        dfused = fgr[0:32, lanes].astype(F32)
        total = 0.0
        for i in range(3):
            spread = place(fwt[i : i + 1, lanes] * dfused, source_of(lanes, i)[1], parts)
            total = total + dot_nt(spread, foh[i, :, lanes])
        dcp[...] += total.reshape(parts, C0, LOW_B)

    def fine_back(j, lanes):
        kept = fin[16:48, lanes].astype(F32) > 0
        fgr[32:64, lanes] = jnp.where(kept, dot(w_skip, fgr[0:32, lanes]), 0.0).astype(BF16)

    every_slot(fine_gather, 8)
    every_slot(fine_join, 8)
    loss = lax.fori_loop(0, slots // span, fine_loss, jnp.zeros((1, span), F32), unroll=8)
    every_slot(fine_fused, 8)
    dcp[...] = jnp.zeros_like(dcp)
    every_slot(fine_scatter, 4)

    other = (1 - sub) * my_parts
    own = sub * my_parts
    give_dup = sibling(3, dcp.at[pl.ds(other, my_parts)], dcr)
    give_dup.start()
    every_slot(fine_back, 8)
    ga[...] = jnp.zeros_like(ga)
    for start in range(0, slots, 4 * span):
        lanes = slice(start, start + 4 * span)
        ga[:, 0:80] += dot_nt(fin[:, lanes], fgr[:, lanes])
    give_dup.wait_recv()

    def own_half(partial, received):
        return jnp.concatenate(
            [partial[own + part] + received[part] for part in range(my_parts)], 1
        )

    dup_low = own_half(dcp, dcr).astype(BF16)
    dblock = dot(w_up, dup_low)
    dbranch_low = dblock.astype(BF16)
    dmixed = dot(w_out, dbranch_low)

    def group_sum(values):
        return jnp.concatenate(
            [
                jnp.sum(values[8 * g : 8 * g + 8], axis=0, keepdims=True)
                for g in range(GROUPS)
            ],
            0,
        )

    def expand(values):
        return jnp.concatenate(
            [jnp.broadcast_to(values[g : g + 1], (8, values.shape[1])) for g in range(GROUPS)], 0
        )

    centred = group_sum(dmixed * mixed_ref[...])

    def back_score(k, lanes):
        ds2 = sc[:, lanes] * (group_sum(dmixed * car[:, lanes]) - centred)
        gst[128:144, lanes] = jnp.concatenate([ds2, zeros8], 0).astype(BF16)

    def back_act(k, lanes):
        scores = gst[128:144, lanes]
        kept = est[128:144, lanes].astype(F32)[0:8] > 0
        ds1 = jnp.where(kept, dot(w_att2, scores), 0.0)
        ds2 = scores.astype(F32)[0:8]
        gst[128:144, lanes] = jnp.concatenate([ds1, ds2], 0).astype(BF16)

    def back_edge(k, lanes):
        small = gst[128:144, lanes]
        dcarried = expand(sc[:, lanes]) * dmixed
        gst[64:128, lanes] = (dot(w_att1, small) + dcarried).astype(BF16)
        index = cnbr_ref[pl.ds(k, 1), pl.ds(half_at, half)]
        high = lax.shift_right_logical(index, low_shift)
        spread = place(jnp.concatenate([dcarried, small.astype(F32)[0:8]], 0), high, parts)
        dkp[...] += dot_nt(spread, ohs[:, lanes]).reshape(parts, C1 + 8, LOW_B)

    def back_pos(k, lanes):
        kept = est[64:128, lanes].astype(F32) > 0
        gst[0:64, lanes] = jnp.where(kept, dot(w_pos2, gst[64:128, lanes]), 0.0).astype(BF16)

    every_edge(back_score, 16)
    every_edge(back_act, 16)
    dkp[...] = jnp.zeros_like(dkp)
    every_edge(back_edge, 16)
    give_dkv = sibling(4, dkp.at[pl.ds(other, my_parts)], dkr)
    give_dkv.start()
    every_edge(back_pos, 16)
    inputs = jnp.concatenate(
        [blk_ref[...].astype(BF16), mixed_ref[...].astype(BF16), jnp.ones((16, half), BF16)], 0
    )
    grads = jnp.concatenate([dup_low, jnp.zeros((C0, half), BF16), dbranch_low], 0)
    gd[...] = dot_nt(inputs, grads)
    gc[...] = jnp.zeros_like(gc)
    ge[...] = jnp.zeros_like(ge)
    for start in range(0, edges, 4 * span):
        lanes = slice(start, start + 4 * span)
        result = dot_nt(est[:, lanes], gst[:, lanes])
        gc[...] += result[:, 0:128]
        ge[:, 0:16] += result[:, 128:144]
    ds1_total = tree(
        jnp.add,
        [gst[128:144, k * half : (k + 1) * half].astype(F32)[0:8] for k in range(NEIGH)],
    )
    w_att1_thrice = jnp.concatenate(
        [w1[0:C1, 0:8]] * 3 + [jnp.zeros((C1, 8), F32)], 1
    ).astype(BF16)

    def three_parts(values):
        high = values.astype(BF16).astype(F32)
        middle = (values - high).astype(BF16).astype(F32)
        low = values - high - middle
        return jnp.concatenate([high, middle, low, jnp.zeros_like(low)], 0).astype(BF16)

    dqueries = dot(w_att1_thrice, three_parts(ds1_total))
    give_dkv.wait_recv()
    dkv = own_half(dkp, dkr)
    dkeys = -dot(w_att1_thrice, three_parts(dkv[C1 : C1 + 8]))
    dqkv_low = jnp.concatenate([dqueries, dkeys, dkv[0:C1]], 0).astype(BF16)
    gbuf[...] = jnp.zeros_like(gbuf)
    gbuf[0:64, :] = dot_nt(pooled_ref[...].astype(BF16), dqkv_low[0:128])
    gbuf[64:128, 0:64] = dot_nt(pooled_ref[...].astype(BF16), dqkv_low[128:192])
    dpooled = dblock + dot(w_qkv, dqkv_low)

    gb[...] = jnp.zeros_like(gb)
    gb[0:16, 0:C1] = dot_nt(centre_low, (-dpooled).astype(BF16))
    dscaled = dpooled * rsum_ref[...]

    def pool_back(k, lanes):
        dpin = (pin[:, lanes] * dscaled).astype(BF16)
        gst[0:64, lanes] = dpin
        kept = cat[16:48, lanes].astype(F32) > 0
        gst[64:96, lanes] = jnp.where(kept, dot(w_down_stem, dpin), 0.0).astype(BF16)

    every_edge(pool_back, 16)
    for start in range(0, edges, 4 * span):
        lanes = slice(start, start + 4 * span)
        gb[:, 0:96] += dot_nt(cat[:, lanes], gst[0:96, lanes])

    left = lanes_of(64, LANES) < 64
    gd_out = gd[64:128, :]
    gbuf[64:128, :] = jnp.where(left, gbuf[64:128, :], gc[64:128, :])
    gbuf[128:160, :] = jnp.where(left[0:32], pltpu.roll(gd_out[0:32], 64, 1), gd_out[32:64])
    base = 160
    pack(gbuf, base, ga, 0, 32, OFF["w_stem"], 6, C0)
    pack(gbuf, base, gb, 0, 64, OFF["w_stem"], 6, C0)
    pack(gbuf, base, ga, 7, 32, OFF["b_stem"], 1, C0)
    pack(gbuf, base, gb, 7, 64, OFF["b_stem"], 1, C0)
    pack(gbuf, base, gb, 0, 0, OFF["w_down"], 3, C1)
    pack(gbuf, base, gb, 16, 0, OFF["w_down"] + 3 * C1, C0, C1)
    pack(gbuf, base, gb, 7, 0, OFF["b_down"], 1, C1)
    pack(gbuf, base, gc, 136, 0, OFF["w_pos"], 3, C1)
    pack(gbuf, base, gc, 143, 0, OFF["b_pos"], 1, C1)
    pack(gbuf, base, ge, 0, 0, OFF["w_att1"], C1, GROUPS)
    pack(gbuf, base, ge, 143, 0, OFF["b_att1"], 1, GROUPS)
    pack(gbuf, base, ge, 128, 8, OFF["w_att2"], GROUPS, GROUPS)
    pack(gbuf, base, ge, 143, 8, OFF["b_att2"], 1, GROUPS)
    pack(gbuf, base, gd, 0, 0, OFF["w_up"], C1, C0)
    pack(gbuf, base, gd, 128, 0, OFF["b_up"], 1, C0)
    pack(gbuf, base, ga, 16, 0, OFF["w_skip"], C0, C0)
    pack(gbuf, base, ga, 48, 64, OFF["w_head"], C0, NCLS)
    pack(gbuf, base, ga, 7, 64, OFF["b_head"], 1, NCLS)
    loss_sum = jnp.sum(loss, axis=1, keepdims=True)
    line, lane = divmod(FLAT, LANES)
    at_loss = lanes_of(1, LANES) == lane
    gbuf[base + line : base + line + 1, :] += jnp.where(at_loss, loss_sum, 0.0)

    rows = gbuf.shape[0] // n_sub
    shards = rows // 8
    give_grad = sibling(5, gbuf.at[pl.ds(pl.multiple_of((1 - sub) * rows, rows), rows)], gsib)
    give_grad.start()
    give_grad.wait_recv()
    ghalf[...] = gbuf[pl.ds(pl.multiple_of(sub * rows, rows), rows), :] + gsib[...]
    mine_at = pl.multiple_of(sub * rows + me * 8, 8)

    def shard_copy(peer, index):
        return pltpu.make_async_remote_copy(
            src_ref=ghalf.at[pl.ds(pl.multiple_of(peer * 8, 8), 8)],
            dst_ref=gsh.at[index],
            send_sem=red_send.at[peer],
            recv_sem=red_recv.at[index],
            device_id={"pts": peer},
            device_id_type=MESH,
        )

    def sum_copy(peer, index):
        at = pl.multiple_of(sub * rows + index * 8, 8)
        return pltpu.make_async_remote_copy(
            src_ref=gfull.at[pl.ds(at, 8)],
            dst_ref=gfull.at[pl.ds(at, 8)],
            send_sem=gat_send.at[peer],
            recv_sem=gat_recv.at[index],
            device_id={"pts": peer},
            device_id_type=MESH,
        )

    holds = None if n_pts <= shards else me < shards

    def when(condition, run):
        if condition is None:
            run()
        else:
            pl.when(condition)(run)

    def each_peer(run, limited):
        def body(step, carry):
            peer = partner(step)
            when(None if holds is None or not limited else peer < shards, lambda: run(peer))
            return carry

        lax.fori_loop(1, n_pts, body, 0)

    each_peer(lambda peer: shard_copy(peer, me).start(), True)

    def reduce():
        gsh[me] = ghalf[pl.ds(pl.multiple_of(me * 8, 8), 8), :]
        each_peer(lambda peer: shard_copy(peer, peer).wait_recv(), False)
        gfull[pl.ds(mine_at, 8), :] = jnp.sum(gsh[...], axis=0)
        each_peer(lambda peer: sum_copy(peer, me).start(), False)

    when(holds, reduce)
    each_peer(lambda peer: sum_copy(peer, peer).wait_recv(), True)
    half_rows = gfull.at[pl.ds(pl.multiple_of(sub * rows, rows), rows)]
    give_full = sibling(6, half_rows, half_rows)
    give_full.start()

    each_peer(lambda peer: block_copy(peer, me).wait_send(), False)
    each_peer(lambda peer: mat_copy(peer, me).wait_send(), False)
    each_peer(lambda peer: shard_copy(peer, me).wait_send(), True)
    when(holds, lambda: each_peer(lambda peer: sum_copy(peer, me).wait_send(), False))
    for copy in (forward, give_pooled, give_block, give_dup, give_dkv, give_grad, give_full):
        copy.wait_send()
    give_full.wait_recv()
    out_ref[...] = gfull[...]


def normalised(matrix):
    return matrix * lax.rsqrt(jnp.sum(matrix * matrix, axis=0, keepdims=True))


def gram_schmidt_pair(matrix, width=8):
    size = matrix.shape[0]
    left = lanes_of(size, 2 * size) < size
    column = lanes_of(1, 2 * size)
    left_row = column < size
    place_row = jnp.where(left_row, column, column - size)

    def spread(values, halves, at):
        return jnp.where(halves, values[:, at : at + 1], values[:, size + at : size + at + 1])

    for first in range(0, size, width):
        span = range(width)
        pivots = [spread(matrix, left, first + i) for i in span]
        products = [jnp.sum(pivot * matrix, axis=0, keepdims=True) for pivot in pivots]
        gram = [
            [spread(products[i], left_row, first + l) if l >= i else None for l in span]
            for i in span
        ]
        taken = 0.0
        for i in span:
            inverse = 1.0 / gram[i][i]
            for l in range(i + 1, width):
                part = gram[i][l] * inverse
                pivots[l] = pivots[l] - part * pivots[i]
                products[l] = products[l] - part * products[i]
                for m in range(l, width):
                    gram[l][m] = gram[l][m] - part * gram[i][m]
            factor = jnp.where(place_row > first + i, products[i] * inverse, 0.0)
            taken = taken + pivots[i] * factor
        matrix = matrix - taken
    return normalised(matrix)


def careful_pair(matrix):
    size = matrix.shape[0]
    lane = lanes_of(size, 2 * size)
    left = lane < size
    place = jnp.where(left, lane, lane - size)

    def column(j, matrix):
        here = jnp.where(place == j, matrix, 0.0)
        first = jnp.sum(jnp.where(left, here, 0.0), axis=1, keepdims=True)
        second = jnp.sum(jnp.where(left, 0.0, here), axis=1, keepdims=True)
        pivot = jnp.where(left, first, second)
        pivot = pivot * lax.rsqrt(jnp.sum(pivot * pivot, axis=0, keepdims=True))
        factor = jnp.sum(pivot * matrix, axis=0, keepdims=True)
        return matrix - jnp.where(place > j, pivot * factor, 0.0)

    for repeat in range(2):
        matrix = normalised(lax.fori_loop(0, size, column, matrix))
    return matrix


def departure(basis):
    size = basis.shape[0]
    same = rows_of(size, size) == lanes_of(size, size)
    return exact(basis, basis, ((0,), (0,))) - jnp.where(same, 1.0, 0.0)


def correct(basis, error):
    size = basis.shape[0]
    above = rows_of(size, size) < lanes_of(size, size)
    same = rows_of(size, size) == lanes_of(size, size)
    factor = jnp.where(above, error, jnp.where(same, 0.5 * error, 0.0))
    return basis - exact(basis, factor)


def orthonormal_pair(matrix, both_ref):
    size = matrix.shape[0]
    once = gram_schmidt_pair(matrix)
    halves = [once[:, 0:size], once[:, size : 2 * size]]
    errors = [departure(half) for half in halves]
    worst = jnp.max(jnp.maximum(jnp.abs(errors[0]), jnp.abs(errors[1])))
    halves = [correct(half, error) for half, error in zip(halves, errors)]
    both_ref[...] = jnp.concatenate(halves, 1)

    @pl.when(worst > 1e-4)
    def _():
        again = [both_ref[:, 0:size], both_ref[:, size : 2 * size]]
        both_ref[...] = jnp.concatenate([correct(half, departure(half)) for half in again], 1)

    @pl.when(jnp.logical_not(worst < 0.01))
    def _():
        both_ref[...] = careful_pair(matrix)

    return both_ref[...]


def soap_kernel(
    grads_ref,
    owner_ref,
    step_ref,
    weight_ref,
    first_ref,
    second_ref,
    left_ref,
    right_ref,
    basis_l_ref,
    basis_r_ref,
    average_ref,
    flat_ref,
    flat_mom_ref,
    flat_sec_ref,
    flat_ema_ref,
    weight_out,
    first_out,
    second_out,
    left_out,
    right_out,
    basis_l_out,
    basis_r_out,
    average_out,
    flat_out,
    flat_mom_out,
    flat_sec_out,
    flat_ema_out,
    loss_out,
    norm_out,
    both_ref,
):
    me = lax.axis_index("pts")
    grads = grads_ref[...]
    line, lane = divmod(FLAT, LANES)
    place_row = rows_of(256, LANES)
    at_loss = (place_row == 160 + line) & (lanes_of(256, LANES) == lane)
    loss = jnp.where(at_loss, grads, 0.0)
    loss_out[...] = jnp.sum(jnp.sum(loss, axis=0, keepdims=True), axis=1, keepdims=True)
    cleaned = jnp.where(at_loss, 0.0, grads)
    squares = jnp.sum(jnp.sum(cleaned * cleaned, axis=0, keepdims=True), axis=1, keepdims=True)
    norm = jnp.sqrt(squares)
    norm_out[...] = norm
    factor = jnp.minimum(1.0, CLIP_NORM / norm)
    count = jnp.full((1, 1), step_ref[0].astype(F32), F32)
    one_scale = 1.0 - jnp.exp(count * math.log(BETA_ONE))
    two_scale = 1.0 - jnp.exp(count * math.log(BETA_TWO))
    lines = FLAT_ROWS - 8

    def as_line(values):
        return jnp.broadcast_to(values, (lines, LANES)).reshape(lines * LANES)[0:FLAT]

    flat_grad = (cleaned[160 : 160 + lines] * factor).reshape(lines * LANES)[0:FLAT]
    flat_mom = BETA_ONE * flat_mom_ref[...] + (1.0 - BETA_ONE) * flat_grad
    flat_sec = BETA_TWO * flat_sec_ref[...] + (1.0 - BETA_TWO) * flat_grad * flat_grad
    flat_scaled = flat_mom / as_line(one_scale) / (jnp.sqrt(flat_sec / as_line(two_scale)) + ADAM_EPS)
    flat_new = flat_ref[...] - LEARN_RATE * (flat_scaled + WEIGHT_DECAY * flat_ref[...])
    flat_out[...] = flat_new
    flat_mom_out[...] = flat_mom
    flat_sec_out[...] = flat_sec
    flat_ema_out[...] = EMA_KEEP * flat_ema_ref[...] + (1.0 - EMA_KEEP) * flat_new
    folded = cleaned[128:160]
    stacked = [
        cleaned[0:64, 0:64],
        cleaned[0:64, 64:128],
        cleaned[64:128, 0:64],
        cleaned[64:128, 64:128],
        jnp.concatenate([folded[:, 0:64], folded[:, 64:128]], 0),
    ]
    grad = jnp.zeros((C1, C1), F32)
    owned = 0.0
    for position in range(NMATS):
        flag = jnp.where(owner_ref[position] == me, 1.0, 0.0)
        grad = grad + flag * stacked[position]
        owned = owned + flag
    raw = grad
    scale = (1.0 - BETA_TWO) * (factor * factor)
    grad = grad * factor
    basis_l = basis_l_ref[...]
    basis_r = basis_r_ref[...]
    left_new = BETA_TWO * left_ref[...] + scale * exact(raw, raw, ((1,), (1,)))
    right_new = BETA_TWO * right_ref[...] + scale * exact(raw, raw, ((0,), (0,)))
    both = orthonormal_pair(
        jnp.concatenate([exact(left_new, basis_l), exact(right_new, basis_r)], 1), both_ref
    )
    basis_l_new = both[:, 0:C1]
    basis_r_new = both[:, C1 : 2 * C1]
    rotated = exact(exact(basis_l, grad, ((0,), (0,))), basis_r)
    first_new = BETA_ONE * first_ref[...] + (1.0 - BETA_ONE) * rotated
    second_new = BETA_TWO * second_ref[...] + (1.0 - BETA_TWO) * rotated * rotated
    scaled = first_new / one_scale / (jnp.sqrt(second_new / two_scale) + ADAM_EPS)
    weight = weight_ref[...]
    weight_new = weight - LEARN_RATE * (
        exact(exact(basis_l, scaled), basis_r, ((1,), (1,))) + WEIGHT_DECAY * weight
    )
    plain = exact(exact(basis_l, first_new), basis_r, ((1,), (1,)))
    first_rotated = exact(exact(basis_l_new, plain, ((0,), (0,))), basis_r_new)
    average_new = EMA_KEEP * average_ref[...] + (1.0 - EMA_KEEP) * weight_new
    held = owned > 0.5
    weight_out[...] = jnp.where(held, weight_new, 0.0)
    first_out[...] = jnp.where(held, first_rotated, 0.0)
    second_out[...] = jnp.where(held, second_new, 0.0)
    left_out[...] = jnp.where(held, left_new, 0.0)
    right_out[...] = jnp.where(held, right_new, 0.0)
    basis_l_out[...] = jnp.where(held, basis_l_new, 0.0)
    basis_r_out[...] = jnp.where(held, basis_r_new, 0.0)
    average_out[...] = jnp.where(held, average_new, 0.0)


def local(
    points,
    route,
    labels,
    interp_src,
    pool_nbr,
    sample,
    coarse_nbr,
    owner,
    step,
    flat,
    flat_mom,
    flat_sec,
    flat_ema,
    mats,
    mats_mom,
    mats_sec,
    mats_left,
    mats_right,
    mats_basis_l,
    mats_basis_r,
    mats_ema,
):
    n_pts = lax.axis_size("pts")
    n_sub = lax.axis_size("sub")
    fine = points.shape[0]
    coarse = sample.shape[0]
    cap = n_sub * fine // n_pts
    slots = n_pts * cap
    sources = n_sub * n_pts
    half = coarse // n_sub
    edges = NEIGH * half
    parts = coarse // LOW_B
    my_parts = parts // n_sub
    vmem = pl.BlockSpec(memory_space=pltpu.VMEM)
    smem = pl.BlockSpec(memory_space=pltpu.SMEM)
    dma = pltpu.SemaphoreType.DMA
    scratch = [
        VMEM((6, fine), BF16),
        VMEM((1, fine), I32),
        VMEM((1, fine), I32),
        VMEM((3, fine), I32),
        VMEM((NEIGH, coarse), I32),
        VMEM((1, coarse), I32),
        VMEM((NEIGH, coarse), I32),
        pltpu.SMEM((NMATS,), I32),
        VMEM((C1, C1), F32),
        VMEM((FLAT,), F32),
        VMEM((FLAT_ROWS, LANES), F32),
        VMEM((LOW_B, LANES), BF16),
        VMEM((16, fine), F32),
        VMEM((n_pts * 16, cap), F32),
        VMEM((n_pts, 16, cap), BF16),
        VMEM((sources, 16, cap), BF16),
        VMEM((32, LANES), BF16),
        VMEM((n_pts, 32, LANES), BF16),
        VMEM((sources * 8, cap), BF16),
        VMEM((8, coarse), F32),
        VMEM((C1, edges), F32),
        VMEM((48, edges), BF16),
        VMEM((C1, half), F32),
        VMEM((C1, half), F32),
        VMEM((n_sub, my_parts * CH, LOW_B), BF16),
        VMEM((n_sub, my_parts * CH, LOW_B), BF16),
        VMEM((C1, edges), BF16),
        VMEM((144, edges), BF16),
        VMEM((144, edges), BF16),
        VMEM((LOW_B, edges), BF16),
        VMEM((C1, edges), F32),
        VMEM((GROUPS, edges), F32),
        VMEM((C1, half), F32),
        VMEM((C1, half), F32),
        VMEM((16, slots), F32),
        VMEM((80, slots), BF16),
        VMEM((80, slots), BF16),
        VMEM((C0, slots), F32),
        VMEM((3, LOW_B, slots), BF16),
        VMEM((3, C1, slots), BF16),
        VMEM((8, slots), F32),
        VMEM((parts, C0, LOW_B), F32),
        VMEM((my_parts, C0, LOW_B), F32),
        VMEM((parts, C1 + 8, LOW_B), F32),
        VMEM((my_parts, C1 + 8, LOW_B), F32),
        VMEM((LANES, LANES), F32),
        VMEM((LANES, LANES), F32),
        VMEM((LANES, LANES), F32),
        VMEM((LANES, LANES), F32),
        VMEM((LANES, LANES), F32),
        VMEM((LANES, LANES), F32),
        VMEM((LANES, LANES), F32),
        VMEM((LANES, LANES), F32),
        VMEM((LANES, LANES), F32),
        VMEM((80, LANES), F32),
        VMEM((48, LANES), F32),
        VMEM((144, LANES), F32),
        VMEM((144, LANES), F32),
        VMEM((144, LANES), F32),
        VMEM((256, LANES), F32),
        VMEM((128, LANES), F32),
        VMEM((128, LANES), F32),
        VMEM((n_pts, 8, LANES), F32),
        VMEM((256, LANES), F32),
        dma((n_pts,)),
        dma((n_pts,)),
        dma((n_pts,)),
        dma((n_pts,)),
        dma((n_pts,)),
        dma((n_pts,)),
        dma((n_pts,)),
        dma((n_pts,)),
        dma((8,)),
        dma((8,)),
        dma((10,)),
    ]
    reduced = pl.pallas_call(
        functools.partial(main_kernel, n_pts, n_sub),
        out_shape=jax.ShapeDtypeStruct((256, LANES), F32),
        in_specs=[pl.BlockSpec(memory_space=pltpu.HBM)] * 10,
        out_specs=vmem,
        scratch_shapes=scratch,
        compiler_params=pltpu.CompilerParams(
            collective_id=0, has_side_effects=True, vmem_limit_bytes=60 * 1024 * 1024
        ),
    )(
        points.T,
        route.reshape(1, fine),
        labels.reshape(1, fine),
        interp_src.T,
        pool_nbr.T,
        sample.reshape(1, coarse),
        coarse_nbr.T,
        owner,
        mats[0],
        flat,
    )
    square = jax.ShapeDtypeStruct((C1, C1), F32)
    line = jax.ShapeDtypeStruct((FLAT,), F32)
    single = jax.ShapeDtypeStruct((1, 1), F32)
    results = pl.pallas_call(
        soap_kernel,
        out_shape=[square] * 8 + [line] * 4 + [single] * 2,
        in_specs=[vmem] + [smem] * 2 + [vmem] * 12,
        out_specs=[vmem] * 14,
        scratch_shapes=[VMEM((C1, 2 * C1), F32)],
    )(
        reduced,
        owner,
        step,
        mats[0],
        mats_mom[0],
        mats_sec[0],
        mats_left[0],
        mats_right[0],
        mats_basis_l[0],
        mats_basis_r[0],
        mats_ema[0],
        flat,
        flat_mom,
        flat_sec,
        flat_ema,
    )
    scalars = (results[12].reshape(()), results[13].reshape(()))
    return scalars + tuple(results[8:12]) + tuple(result[None] for result in results[:8])


def solution(mesh):
    placed = (
        P(("pts", "sub"), None),
        P(("pts", "sub")),
        P(("pts", "sub")),
        P(("pts", "sub"), None),
        P("pts", None),
        P("pts"),
        P("pts", None),
        P(),
        P(),
        P(),
        P(),
        P(),
        P(),
    ) + (P("pts", None, None),) * 8
    mapped = jax.shard_map(
        local,
        mesh=mesh,
        in_specs=placed,
        out_specs=(P(),) * 6 + (P("pts", None, None),) * 8,
        check_vma=False,
    )

    def run(*arrays):
        with jax.sharding.use_abstract_mesh(mesh.abstract_mesh):
            return mapped(*arrays)

    return run
```
